32 devices in a mesh: magnet: 4 (over y, x), slab: 8 (over z, core).
Axes of the slice: x: 2, y: 2, z: 4, core: 2. Of those that a mesh axis runs over, the one named last changes fastest.
Arguments:
- foil_warmth: float32 [256, 512], P(('magnet', 'slab')), may hold values from 0.5 to 4
- terminal_voltage_input: float32 [256, 512], P(('magnet', 'slab')), may hold values from -6 to 6
- foil_segment_pattern: int32 [256, 512], P(('magnet', 'slab')), may hold values from 0 to 2
- underlying_block_map: int32 [256, 512], P('magnet'), may hold values from 768 to 1023
- prior_block_warmth: float32 [8, 256, 128], P('slab', 'magnet'), may hold values from 0 to 2
- substance_kind: int32 [8, 256, 128], P('slab', 'magnet'), may hold values from 0 to 3
Outputs:
- sheet_potential: float32 [256, 512], P(('magnet', 'slab'))
- brick_heated: float32 [8, 256, 128], P('slab', 'magnet')
The draws below stay inside these ranges and needn't reach their ends.
Inputs may be any that keep to these rules, and one draw needn't show every extreme that they name: `foil_segment_pattern`: 0 marks plain heater steel, 1 copper-plated stations, 2 current-lead contacts. `underlying_block_map`: the value is radial layer times 128 plus azimuthal cell. `substance_kind`: 0 insulation, 1 Nb3Sn coil, 2 copper wedge, 3 steel collar.
All inputs are finite; a program needn't handle non-finite values.
Results may differ from the reference program's by a relative error of at most 0.0001.
Values sent between devices are 32-bit elements; how exact they have to be, the bound alone decides.
A program may use at most 64 MiB of HBM per device.

```python
import math
import jax
import jax.numpy as jnp

SW = 512
BRD = 1
SPOKE_COUNT = 128
ITERS = 3
SUBSTEPS = 4
AXIAL_COUNT = 256
SHELL_COUNT = 8


def with_ends(array, key, smallest, high):
    dims = array.shape
    index_at = [jax.random.randint(jax.random.fold_in(key, axis), (), 0, dims[axis]) for axis in range(len(dims))]
    array = array.at[tuple(index_at)].set(smallest)
    longest = dims.index(max(dims))
    index_at[longest] = (index_at[longest] + 1) % dims[longest]
    return array.at[tuple(index_at)].set(high)


def shard_levels(rng, shape, split, least, high):
    loudness = 1.0
    for axis_at, shards_of in split:
        draws = jax.random.uniform(jax.random.fold_in(jax.random.fold_in(rng, 6), axis_at), (shards_of,), jnp.float32, least / len(split), high / len(split))
        loudness = loudness * jnp.repeat(jnp.exp(draws), shape[axis_at] // shards_of).reshape((-1,) + (1,) * (len(shape) - 1 - axis_at))
    return loudness


def noise(key, extent, width, most, pieces=(), held_as=jnp.bfloat16):
    values = jax.random.normal(key, extent, jnp.float32) * width
    if len(pieces) > 0:
        values = shard_levels(key, extent, pieces, -0.22, 0.18) * values
    return jnp.clip(values, min=-most, max=most).astype(held_as)


def setup_inputs(seed: int = 0) -> dict:
    streams_of = jax.random.split(jax.random.key(seed), 7)
    return {
        "foil_warmth": jnp.clip(jnp.exp(math.log(4.0) - 2.0794415 * jax.random.uniform(streams_of[0], (AXIAL_COUNT, SW), jnp.float32) ** shard_levels(streams_of[0], (AXIAL_COUNT, SW), ((0, 32),), -0.2, 0.2)), 0.5, 4.0),
        "terminal_voltage_input": noise(streams_of[1], (AXIAL_COUNT, SW), 1.0, 6.0, ((0, 32),), jnp.float32),
        "foil_segment_pattern": with_ends(jax.random.randint(streams_of[2], (AXIAL_COUNT, SW), 0, 3), jax.random.fold_in(streams_of[2], 1), 0, 2).astype(jnp.int32),
        "underlying_block_map": with_ends(jax.random.randint(streams_of[3], (AXIAL_COUNT, SW), (SHELL_COUNT - 2 * BRD) * SPOKE_COUNT, SHELL_COUNT * SPOKE_COUNT), jax.random.fold_in(streams_of[3], 1), (SHELL_COUNT - 2 * BRD) * SPOKE_COUNT, (SHELL_COUNT * SPOKE_COUNT) - 1).astype(jnp.int32),
        "prior_block_warmth": jnp.clip(2.0 * jax.random.uniform(streams_of[4], (SHELL_COUNT, AXIAL_COUNT, SPOKE_COUNT), jnp.float32) ** shard_levels(streams_of[4], (SHELL_COUNT, AXIAL_COUNT, SPOKE_COUNT), ((0, 8), (1, 4)), -0.2, 0.2), 0.0, 2.0),
        "substance_kind": with_ends(jax.random.randint(streams_of[5], (SHELL_COUNT, AXIAL_COUNT, SPOKE_COUNT), 0, 4), jax.random.fold_in(streams_of[5], 1), 0, 3).astype(jnp.int32),
    }


leak_diag = 0.25
contact_gain = 4.0
copper_factor = 3.0
sheet_slope = 0.5
heat_factor = 1.5
time_step = 0.03
conduct_table = (0.3, 1.0, 2.0, 0.6)
capacity_table = (1.0, 1.5, 2.0, 1.2)
diffusivity_derivative = 0.4


def lookup_table(substance_kind, table):
    running_total = jnp.zeros(substance_kind.shape, jnp.float32)
    for material_index in range(4):
        running_total = running_total + jnp.where(substance_kind == material_index, table[material_index], 0.0).astype(jnp.float32)
    return running_total


def face_coeffs(sigma_padded):
    centre = sigma_padded[1:-1, 1:-1]
    return (0.5 * (centre + sigma_padded[:-2, 1:-1]), 0.5 * (centre + sigma_padded[2:, 1:-1]),
            0.5 * (centre + sigma_padded[1:-1, :-2]), 0.5 * (centre + sigma_padded[1:-1, 2:]))


def neighbour_values(padded):
    return (padded[:-2, 1:-1], padded[2:, 1:-1], padded[1:-1, :-2], padded[1:-1, 2:])


def apply_sheet(values_grid, coeffs, diagonal):
    neighbours = neighbour_values(jnp.pad(values_grid, 1))
    result = diagonal * values_grid
    for coeff_face, neighbour in zip(coeffs, neighbours):
        result = result - coeff_face * neighbour
    return result


def diffusivity_update(temp_pad, cond_pad, resistive_power_density, specific_storage_grid):
    centre_t = temp_pad[1:-1, 1:-1]
    centre_k = cond_pad[1:-1, 1:-1]
    flux_total = jnp.zeros(centre_t.shape, jnp.float32)
    pairs = ((temp_pad[:-2, 1:-1], cond_pad[:-2, 1:-1]), (temp_pad[2:, 1:-1], cond_pad[2:, 1:-1]),
             (temp_pad[1:-1, :-2], cond_pad[1:-1, :-2]), (temp_pad[1:-1, 2:], cond_pad[1:-1, 2:]))
    for other_t, other_k in pairs:
        flux_total = flux_total + 0.5 * (centre_k + other_k) * (other_t - centre_t)
    for offset in (1, -1):
        other_t = jnp.roll(centre_t, offset, axis=2)
        other_k = jnp.roll(centre_k, offset, axis=2)
        flux_total = flux_total + 0.5 * (centre_k + other_k) * (other_t - centre_t)
    return centre_t + time_step * (flux_total + resistive_power_density) / specific_storage_grid


def reference(foil_warmth, terminal_voltage_input, foil_segment_pattern, underlying_block_map, prior_block_warmth, substance_kind):
    copper = jnp.where(foil_segment_pattern == 1, copper_factor, 1.0).astype(jnp.float32)
    sigma_cells = copper / (1.0 + sheet_slope * foil_warmth)
    coeffs = face_coeffs(jnp.pad(sigma_cells, 1))
    contact = jnp.where(foil_segment_pattern == 2, contact_gain, 0.0).astype(jnp.float32)
    diagonal = leak_diag + contact + coeffs[0] + coeffs[1] + coeffs[2] + coeffs[3]
    rhs_field = contact * terminal_voltage_input
    voltage_solution = jnp.zeros_like(rhs_field)
    residual = rhs_field
    direction = rhs_field
    norm_now = jnp.sum(residual * residual)
    for iteration in range(ITERS):
        image_field = apply_sheet(direction, coeffs, diagonal)
        step_length = norm_now / jnp.sum(direction * image_field)
        voltage_solution = voltage_solution + step_length * direction
        residual = residual - step_length * image_field
        if iteration + 1 < ITERS:
            norm_next = jnp.sum(residual * residual)
            direction = residual + (norm_next / norm_now) * direction
            norm_now = norm_next
    neighbours = neighbour_values(jnp.pad(voltage_solution, 1))
    joule = jnp.zeros_like(voltage_solution)
    for coeff_face, neighbour in zip(coeffs, neighbours):
        joule = joule + coeff_face * (voltage_solution - neighbour) ** 2
    joule = heat_factor * joule
    row_index = jnp.broadcast_to(jnp.arange(AXIAL_COUNT, dtype=jnp.int32)[:, None], underlying_block_map.shape)
    resistive_power_density = jnp.zeros((SHELL_COUNT, AXIAL_COUNT, SPOKE_COUNT), jnp.float32).at[underlying_block_map // SPOKE_COUNT, row_index, underlying_block_map % SPOKE_COUNT].add(joule)
    reference_diffusivity = lookup_table(substance_kind, conduct_table)
    specific_storage_grid = lookup_table(substance_kind, capacity_table)
    warmth_distribution = prior_block_warmth
    for substep in range(SUBSTEPS):
        diffusivity_coefficient = reference_diffusivity * (1.0 + diffusivity_derivative * warmth_distribution)
        margin_count = ((1, 1), (1, 1), (0, 0))
        warmth_distribution = diffusivity_update(jnp.pad(warmth_distribution, margin_count), jnp.pad(diffusivity_coefficient, margin_count), resistive_power_density, specific_storage_grid)
    return voltage_solution, warmth_distribution
```

```python
import functools

import jax
import jax.numpy as jnp
from jax import lax
from jax.experimental import pallas as pl
from jax.experimental.pallas import tpu as pltpu
from jax.sharding import PartitionSpec as P

MESH = pl.DeviceIdType.MESH
F32 = jnp.float32
leak_diag = 0.25
contact_gain = 4.0
copper_factor = 3.0
sheet_slope = 0.5
heat_factor = 1.5
time_step = 0.03
conduct_table = (0.3, 1.0, 2.0, 0.6)
capacity_table = (1.0, 1.5, 2.0, 1.2)
diffusivity_derivative = 0.4
REACH = 3
GRAM = ((0, 0), (0, 1), (0, 2), (0, 3), (1, 1), (1, 2), (1, 3), (2, 2), (2, 3))


def two_sum(a, b):
    s = a + b
    t = s - a
    return s, (a - (s - t)) + (b - t)


def halves(a):
    c = a * 4097.0
    high = c - (c - a)
    return high, a - high


def two_prod(a, b, sa, sb):
    p = a * b
    return p, ((sa[0] * sb[0] - p) + sa[0] * sb[1] + sa[1] * sb[0]) + sa[1] * sb[1]


def pair_add(x, y):
    s, e = two_sum(x[0], y[0])
    return s, e + (x[1] + y[1])


def tree(items, add):
    while len(items) > 1:
        items = [add(*items[i : i + 2]) if i + 1 < len(items) else items[i] for i in range(0, len(items), 2)]
    return items[0]


def pair_mul(x, y):
    p, e = two_prod(x[0], y[0], halves(x[0]), halves(y[0]))
    return p, e + (x[0] * y[1] + x[1] * y[0])


def quadratic(coefs, gram):
    terms = []
    for (i, j), g in gram.items():
        c = two_prod(coefs[i], coefs[j], halves(coefs[i]), halves(coefs[j]))
        terms.append(pair_mul(c, g))
    s = tree(terms, pair_add)
    return s[0] + s[1]


def lookup(kind, table):
    out = jnp.zeros(kind.shape, F32)
    for i, value in enumerate(table):
        out = jnp.where(kind == float(i), value, out)
    return out


def fluxes(temps, conds, first, last):
    rows = temps[0].shape[0]
    face = {}
    for i in range(first - 1, last):
        face[i] = (conds[i] + conds[i + 1]) * (temps[i + 1] - temps[i])
    out = []
    for i in range(first, last):
        t, k = temps[i], conds[i]
        total = face[i] - face[i - 1]
        for axis, size in ((0, rows), (1, t.shape[1])):
            f = (k + pltpu.roll(k, 1, axis)) * (pltpu.roll(t, 1, axis) - t)
            total = total + (f - pltpu.roll(f, size - 1, axis))
        out.append(0.5 * total)
    return out


def kernel(
    M, S, shells,
    warm_in, volt_in, pat_in, map_in, temp_in, kind_in,
    pot_out, brick_out,
    sheet_f, sheet_i, kind_v, first_b, later_b, onehot, red1, red2, heat_own, heat_ext, heat_b,
    local_sem, sheet_send, sheet_recv, len_send, len_recv, rad_send, rad_recv, late_send, late_recv,
    r1_send, r1_recv, r2_send, r2_recv, h_send, h_recv, e_send, e_recv,
):
    m = lax.axis_index("magnet")
    s = lax.axis_index("slab")
    rs, width = warm_in.shape
    rows, spokes = temp_in.shape[1], temp_in.shape[2]
    ext = 3 * rs
    brick = rows + 16
    g = m * S + s
    target0 = max(0, S - 2 - REACH)
    heated = s >= target0

    own_rows = pl.ds(pl.multiple_of(s * rs, 8), rs)
    mid = pl.ds(rs, rs)
    bmid = pl.ds(8, rows)
    zf = jnp.zeros((2, rs, width), F32)
    zi = jnp.zeros((2, rs, width), jnp.int32)
    for lo in (0, 2 * rs):
        sheet_f[:, lo : lo + rs, :] = zf
        sheet_i[:, lo : lo + rs, :] = zi
    ghost_t = jnp.zeros((brick, spokes), F32)
    ghost_k = jnp.full((brick, spokes), -1.0, F32)
    for buf in (first_b, later_b):
        for i in range(buf.shape[0]):
            buf[i, 0] = ghost_t
            buf[i, 1] = ghost_k
    local = [
        pltpu.make_async_copy(kind_in.at[0], kind_v, local_sem.at[0]),
        pltpu.make_async_copy(temp_in.at[0], first_b.at[1, 0, bmid, :], local_sem.at[1]),
        pltpu.make_async_copy(warm_in, sheet_f.at[0, mid, :], local_sem.at[2]),
        pltpu.make_async_copy(volt_in, sheet_f.at[1, mid, :], local_sem.at[3]),
        pltpu.make_async_copy(pat_in, sheet_i.at[0, mid, :], local_sem.at[4]),
        pltpu.make_async_copy(map_in.at[own_rows, :], sheet_i.at[1, mid, :], local_sem.at[5]),
    ]
    for c in local:
        c.start()

    barrier = pltpu.get_barrier_semaphore()

    def greet(who):
        pl.semaphore_signal(barrier, inc=1, device_id=who, device_id_type=MESH)

    for d in range(1, S):
        greet((m, lax.rem(s + d, S)))
    for d in range(1, M):
        greet((lax.rem(m + d, M), s))
    cross_up = (s == 0) & (m > 0)
    cross_down = (s == S - 1) & (m < M - 1)
    pl.when(cross_up)(lambda: greet((m - 1, S - 1)))
    pl.when(cross_down)(lambda: greet((m + 1, 0)))
    extra = jnp.where(cross_up | cross_down, 1, 0)
    for c in local:
        c.wait()
    first_b[1, 1, bmid, :] = kind_v[...].astype(F32)
    pl.semaphore_wait(barrier, S + M - 2 + extra)

    pending = []

    def sent(copies):
        for pred, c in copies:
            if pred is None:
                c.wait_send()
            else:
                pl.when(pred)(c.wait_send)

    def remote(pred, src, dst, send, recv, who):
        nonlocal pending
        c = pltpu.make_async_remote_copy(
            src_ref=src, dst_ref=dst, send_sem=send, recv_sem=recv, device_id=who, device_id_type=MESH
        )
        if pred is None:
            c.start()
        else:
            pl.when(pred)(c.start)
        pending.append((pred, c))

    def arrived(pred, src, dst, send, recv):
        c = pltpu.make_async_remote_copy(
            src_ref=src, dst_ref=dst, send_sem=send, recv_sem=recv, device_id=(m, s), device_id_type=MESH
        )
        if pred is None:
            c.wait_recv()
        else:
            pl.when(pred)(c.wait_recv)

    has_prev, has_next = g > 0, g < M * S - 1
    prev = (jnp.where(s == 0, m - 1, m), jnp.where(s == 0, S - 1, s - 1))
    nxt = (jnp.where(s == S - 1, m + 1, m), jnp.where(s == S - 1, 0, s + 1))
    before, after = pl.ds(0, rs), pl.ds(2 * rs, rs)
    for k, buf in enumerate((sheet_f, sheet_i)):
        remote(has_next, buf.at[:, mid, :], buf.at[:, before, :], sheet_send.at[2 * k], sheet_recv.at[2 * k], nxt)
        remote(has_prev, buf.at[:, mid, :], buf.at[:, after, :], sheet_send.at[2 * k + 1], sheet_recv.at[2 * k + 1], prev)
    layer = first_b.at[1]
    top_rows, end_rows = pl.ds(8, 8), pl.ds(rows, 8)
    top_halo, end_halo = pl.ds(0, 8), pl.ds(rows + 8, 8)
    remote(m < M - 1, layer.at[:, end_rows, :], layer.at[:, top_halo, :], len_send.at[0], len_recv.at[0], (m + 1, s))
    remote(m > 0, layer.at[:, top_rows, :], layer.at[:, end_halo, :], len_send.at[1], len_recv.at[1], (m - 1, s))

    lane_id = lax.broadcasted_iota(jnp.int32, (spokes, width), 0)
    base_cell = (shells - 2) * spokes
    cell_own = sheet_i[1, rs : 2 * rs, :] - base_cell
    upper_own = cell_own >= spokes
    col_own = jnp.where(upper_own, cell_own - spokes, cell_own)

    def put_onehot(at, row):
        onehot[at * spokes : (at + 1) * spokes, :] = jnp.where(lane_id == row, 1.0, 0.0).astype(jnp.bfloat16)

    for i in range(rs):
        put_onehot(i, col_own[i : i + 1, :])

    arrived(m > 0, layer.at[:, end_rows, :], layer.at[:, top_halo, :], len_send.at[0], len_recv.at[0])
    arrived(m < M - 1, layer.at[:, top_rows, :], layer.at[:, end_halo, :], len_send.at[1], len_recv.at[1])
    remote(s < S - 1, layer, first_b.at[0], rad_send.at[0], rad_recv.at[0], (m, s + 1))
    remote(s > 0, layer, first_b.at[2], rad_send.at[1], rad_recv.at[1], (m, s - 1))

    for k, buf in enumerate((sheet_f, sheet_i)):
        arrived(has_prev, buf.at[:, mid, :], buf.at[:, before, :], sheet_send.at[2 * k], sheet_recv.at[2 * k])
        arrived(has_next, buf.at[:, mid, :], buf.at[:, after, :], sheet_send.at[2 * k + 1], sheet_recv.at[2 * k + 1])

    pattern = sheet_i[0]
    row_id = lax.broadcasted_iota(jnp.int32, (ext, width), 0) + (g - 1) * rs
    col_id = lax.broadcasted_iota(jnp.int32, (ext, width), 1)
    valid = (row_id >= 0) & (row_id < M * S * rs)
    left_edge, right_edge = col_id == 0, col_id == width - 1

    def from_up(v):
        return pltpu.roll(v, 1, 0)

    def from_down(v):
        return pltpu.roll(v, ext - 1, 0)

    def from_left(v):
        return jnp.where(left_edge, 0.0, pltpu.roll(v, 1, 1))

    def from_right(v):
        return jnp.where(right_edge, 0.0, pltpu.roll(v, width - 1, 1))

    sides = (from_up, from_down, from_left, from_right)
    sigma = jnp.where(valid, jnp.where(pattern == 1, copper_factor, 1.0) / (1.0 + sheet_slope * sheet_f[0]), 0.0)
    coeffs = [0.5 * (sigma + side(sigma)) for side in sides]
    contact = jnp.where(pattern == 2, contact_gain, 0.0)
    diagonal = leak_diag + contact + coeffs[0] + coeffs[1] + coeffs[2] + coeffs[3]

    def apply(v):
        out = diagonal * v
        for c, side in zip(coeffs, sides):
            out = out - c * side(v)
        return jnp.where(valid, out, 0.0)

    basis = [jnp.where(valid, contact * sheet_f[1], 0.0)]
    for _ in range(3):
        basis.append(apply(basis[-1]))

    chunks = [[v[rs : 2 * rs, c : c + 128] for c in range(0, width, 128)] for v in basis]
    split = [[halves(v) for v in field] for field in chunks]
    highs, lows = [], []
    for i, j in GRAM:
        pairs = [two_prod(a, b, sa, sb) for a, b, sa, sb in zip(chunks[i], chunks[j], split[i], split[j])]
        p = tree(pairs, pair_add)
        for step in (4, 2, 1):
            p = pair_add(p, (pltpu.roll(p[0], step, 0), pltpu.roll(p[1], step, 0)))
        highs.append(p[0][0:1])
        lows.append(p[1][0:1])
    fill = [jnp.zeros((16 - len(GRAM), 128), F32)]
    red1[s] = jnp.concatenate(highs + fill + lows + fill, axis=0)
    for d in range(1, S):
        remote(None, red1.at[s], red1.at[s], r1_send.at[d], r1_recv.at[d], (m, lax.rem(s + d, S)))

    arrived(s > 0, layer, first_b.at[0], rad_send.at[0], rad_recv.at[0])
    arrived(s < S - 1, layer, first_b.at[2], rad_send.at[1], rad_recv.at[1])

    def conduct(temps, kinds):
        return [lookup(k, conduct_table) * (1.0 + diffusivity_derivative * t) for t, k in zip(temps, kinds)]

    def rate(kind):
        return lookup(kind, tuple(time_step / c for c in capacity_table))

    temps = [first_b[i, 0] for i in range(3)]
    kinds = [first_b[i, 1] for i in range(3)]
    (flux,) = fluxes(temps, conduct(temps, kinds), 1, 2)
    later_b[REACH, 0] = temps[1] + rate(kinds[1]) * flux
    later_b[REACH, 1] = kinds[1]
    early, pending = pending, []
    for d in range(1, REACH + 1):
        remote(s < S - d, later_b.at[REACH], later_b.at[REACH - d], late_send.at[2 * d - 2], late_recv.at[2 * d - 2], (m, s + d))
        remote(s >= d, later_b.at[REACH], later_b.at[REACH + d], late_send.at[2 * d - 1], late_recv.at[2 * d - 1], (m, s - d))

    late, pending = pending, []

    before_string = s == 0

    def outer(a):
        return jnp.where(before_string, pltpu.roll(a[0:rs], 3, 0), a[2 * rs :])

    cell_ext = outer(sheet_i[1]) - base_cell
    cell_ext = jnp.clip(cell_ext, 0, 2 * spokes - 1)
    upper_ext = cell_ext >= spokes
    col_ext = jnp.where(upper_ext, cell_ext - spokes, cell_ext)
    for i in range(3):
        put_onehot(rs + i, col_ext[i : i + 1, :])

    def pair_of(ref, i):
        return ref[i, 0:16], ref[i, 16:32]

    for d in range(1, S):
        src = lax.rem(s + S - d, S)
        arrived(None, red1.at[s], red1.at[src], r1_send.at[d], r1_recv.at[d])
    total = tree([pair_of(red1, i) for i in range(S)], pair_add)
    red2[m] = jnp.concatenate(total, axis=0)
    for d in range(1, M):
        remote(None, red2.at[m], red2.at[m], r2_send.at[d], r2_recv.at[d], (lax.rem(m + d, M), s))
    for d in range(1, M):
        src = lax.rem(m + M - d, M)
        arrived(None, red2.at[m], red2.at[src], r2_send.at[d], r2_recv.at[d])
    high, low = tree([pair_of(red2, i) for i in range(M)], pair_add)
    grid = 1024.0 * jnp.max(jnp.abs(high), axis=1, keepdims=True)
    coarse = (high + grid) - grid
    rest = jnp.sum((high - coarse) + low, axis=1, keepdims=True)
    sums = two_sum(jnp.sum(coarse, axis=1, keepdims=True), rest)
    gram = {ij: (sums[0][n : n + 1], sums[1][n : n + 1]) for n, ij in enumerate(GRAM)}

    def twice(x):
        return 2.0 * x[0], 2.0 * x[1]

    plain = {(i, j): gram[i, j] if i == j else twice(gram[i, j]) for i, j in GRAM if j < 3}
    with_a = {
        (0, 0): gram[0, 1],
        (0, 1): pair_add(gram[0, 2], gram[1, 1]),
        (1, 1): gram[1, 2],
        (0, 2): pair_add(gram[0, 3], gram[1, 2]),
        (1, 2): pair_add(gram[1, 3], gram[2, 2]),
        (2, 2): gram[2, 3],
    }

    def upto(table, n):
        return {ij: v for ij, v in table.items() if ij[1] < n}

    one = jnp.ones_like(gram[0, 0][0])
    norm0 = gram[0, 0][0]
    a0 = norm0 / gram[0, 1][0]
    norm1 = quadratic([one, -a0], upto(plain, 2))
    b1 = norm1 / norm0
    p1 = [1.0 + b1, -a0]
    a1 = norm1 / quadratic(p1, upto(with_a, 2))
    r2 = [one, -a0 - a1 * p1[0], -a1 * p1[1]]
    norm2 = quadratic(r2, plain)
    b2 = norm2 / norm1
    p2 = [r2[0] + b2 * p1[0], r2[1] + b2 * p1[1], r2[2]]
    a2 = norm2 / quadratic(p2, with_a)
    weights = [a0 + a1 * p1[0] + a2 * p2[0], a1 * p1[1] + a2 * p2[1], a2 * p2[2]]
    potential = weights[0] * basis[0] + weights[1] * basis[1] + weights[2] * basis[2]
    pot_out[...] = potential[rs : 2 * rs]

    joule = jnp.zeros_like(potential)
    for c, side in zip(coeffs, sides):
        drop = potential - side(potential)
        joule = joule + c * (drop * drop)
    joule = heat_factor * joule
    sub_id = lax.broadcasted_iota(jnp.int32, (rs, spokes), 0)

    def binned(power, upper, first, count):
        parts = []
        for value in (jnp.where(upper, 0.0, power), jnp.where(upper, power, 0.0)):
            for _ in range(3):
                part = value.astype(jnp.bfloat16).astype(F32)
                parts.append(part)
                value = value - part
        lhs = jnp.concatenate(parts, axis=0).astype(jnp.bfloat16)
        cols = onehot[first * spokes : (first + count) * spokes, :]
        out = lax.dot_general(lhs, cols, (((1,), (1,)), ((), ())), preferred_element_type=F32)
        heats = []
        for k in range(2):
            part = out[3 * k * rs : (3 * k + 1) * rs]
            part = part + out[(3 * k + 1) * rs : (3 * k + 2) * rs] + out[(3 * k + 2) * rs : (3 * k + 3) * rs]
            heat = jnp.zeros((rs, spokes), F32)
            for i in range(count):
                heat = jnp.where(sub_id == i, part[:, i * spokes : (i + 1) * spokes], heat)
            heats.append(heat)
        return heats

    lower, higher = binned(joule[rs : 2 * rs], upper_own, 0, rs)
    heat_own[0] = lower
    heat_own[1] = higher
    at = pl.ds(pl.multiple_of(8 + rs * s, 8), rs)
    for n, t in enumerate(range(target0, S)):
        remote(s != t, heat_own, heat_b.at[:, at, :], h_send.at[n], h_recv.at[s], (m, t))
    ext_lower, ext_higher = binned(outer(joule), upper_ext, rs, 3)
    heat_ext[0] = jnp.where(before_string, pltpu.roll(ext_lower, rs - 3, 0), ext_lower)
    heat_ext[1] = jnp.where(before_string, pltpu.roll(ext_higher, rs - 3, 0), ext_higher)
    for n, t in enumerate(range(target0, S)):
        remote((s == 0) & (s != t), heat_ext, heat_b.at[:, top_halo, :], e_send.at[n, 0], e_recv.at[0], (m, t))
        remote((s == S - 1) & (s != t), heat_ext, heat_b.at[:, end_halo, :], e_send.at[n, 1], e_recv.at[1], (m, t))

    @pl.when(heated)
    def _():
        heat_b[0, at, :] = lower
        heat_b[1, at, :] = higher

    @pl.when(s == S - 1)
    def _():
        heat_b[:, end_halo, :] = heat_ext[...]

    if target0 == 0:
        @pl.when(s == 0)
        def _():
            heat_b[:, top_halo, :] = heat_ext[...]

    for d in range(1, REACH + 1):
        arrived(s >= d, later_b.at[REACH], later_b.at[REACH - d], late_send.at[2 * d - 2], late_recv.at[2 * d - 2])
        arrived(s < S - d, later_b.at[REACH], later_b.at[REACH + d], late_send.at[2 * d - 1], late_recv.at[2 * d - 1])
    for j in range(S):
        part = heat_b.at[:, 8 + rs * j : 8 + rs * (j + 1), :]
        arrived(heated & (s != j), heat_own, part, h_send.at[0], h_recv.at[j])
    arrived(heated & (s != 0), heat_ext, heat_b.at[:, top_halo, :], e_send.at[0, 0], e_recv.at[0])
    arrived(heated & (s != S - 1), heat_ext, heat_b.at[:, end_halo, :], e_send.at[0, 1], e_recv.at[1])
    sent(late)
    for k in range(2):
        slot = REACH + (S - 2 + k) - s

        @pl.when((slot <= 2 * REACH) & (slot >= 0))
        def _():
            later_b[slot, 0] = later_b[slot, 0] + rate(later_b[slot, 1]) * heat_b[k]

    count = 2 * REACH + 1
    temps = [later_b[i, 0] for i in range(count)]
    kinds = [later_b[i, 1] for i in range(count)]
    heat_low, heat_high = heat_b[0], heat_b[1]
    for step in range(1, REACH + 1):
        conds = conduct(temps, kinds)
        flux = fluxes(temps, conds, step, count - step)
        for i, f in zip(range(step, count - step), flux):
            place = s + i - REACH
            heat = jnp.where(place == S - 2, heat_low, jnp.where(place == S - 1, heat_high, 0.0))
            temps[i] = temps[i] + rate(kinds[i]) * (f + heat)
    brick_out[0] = temps[REACH][8 : 8 + rows]
    sent(early + pending)


def solution(mesh):
    M, S = mesh.shape["magnet"], mesh.shape["slab"]

    def local(warm, volt, pattern, cells, temp, kind):
        rs, width = warm.shape
        depth, rows, spokes = temp.shape
        brick = rows + 16
        dma = pltpu.SemaphoreType.DMA
        targets = REACH + 2
        return pl.pallas_call(
            functools.partial(kernel, M, S, depth * S),
            out_shape=(
                jax.ShapeDtypeStruct((rs, width), F32),
                jax.ShapeDtypeStruct((depth, rows, spokes), F32),
            ),
            in_specs=[pl.BlockSpec(memory_space=pl.ANY)] * 6,
            out_specs=[pl.BlockSpec(memory_space=pltpu.VMEM)] * 2,
            scratch_shapes=[
                pltpu.VMEM((2, 3 * rs, width), F32),
                pltpu.VMEM((2, 3 * rs, width), jnp.int32),
                pltpu.VMEM((rows, spokes), jnp.int32),
                pltpu.VMEM((3, 2, brick, spokes), F32),
                pltpu.VMEM((2 * REACH + 1, 2, brick, spokes), F32),
                pltpu.VMEM(((rs + 3) * spokes, width), jnp.bfloat16),
                pltpu.VMEM((S, 32, 128), F32),
                pltpu.VMEM((M, 32, 128), F32),
                pltpu.VMEM((2, rs, spokes), F32),
                pltpu.VMEM((2, rs, spokes), F32),
                pltpu.VMEM((2, brick, spokes), F32),
                dma((6,)),
                dma((4,)), dma((4,)),
                dma((2,)), dma((2,)),
                dma((2,)), dma((2,)),
                dma((2 * REACH,)), dma((2 * REACH,)),
                dma((S,)), dma((S,)),
                dma((M,)), dma((M,)),
                dma((targets,)), dma((S,)),
                dma((targets, 2)), dma((2,)),
            ],
            compiler_params=pltpu.CompilerParams(
                collective_id=0, has_side_effects=True, vmem_limit_bytes=48 * 1024 * 1024
            ),
            name="window",
        )(warm, volt, pattern, cells, temp, kind)

    return jax.shard_map(
        local,
        mesh=mesh,
        in_specs=(
            P(("magnet", "slab"), None),
            P(("magnet", "slab"), None),
            P(("magnet", "slab"), None),
            P("magnet", None),
            P("slab", "magnet", None),
            P("slab", "magnet", None),
        ),
        out_specs=(P(("magnet", "slab"), None), P("slab", "magnet", None)),
        check_vma=False,
    )
```

```python
import functools

import jax
import jax.numpy as jnp
from jax import lax
from jax.experimental import pallas as pl
from jax.experimental.pallas import tpu as pltpu
from jax.sharding import PartitionSpec as P

MESH = pl.DeviceIdType.MESH
F32 = jnp.float32
leak_diag = 0.25
contact_gain = 4.0
copper_factor = 3.0
sheet_slope = 0.5
heat_factor = 1.5
time_step = 0.03
conduct_table = (0.3, 1.0, 2.0, 0.6)
capacity_table = (1.0, 1.5, 2.0, 1.2)
diffusivity_derivative = 0.4
REACH = 3
GRAM = ((0, 0), (0, 1), (0, 2), (0, 3), (1, 1), (1, 2), (1, 3), (2, 2), (2, 3))


def two_sum(a, b):
    s = a + b
    t = s - a
    return s, (a - (s - t)) + (b - t)


def halves(a):
    c = a * 4097.0
    high = c - (c - a)
    return high, a - high


def two_prod(a, b, sa, sb):
    p = a * b
    return p, ((sa[0] * sb[0] - p) + sa[0] * sb[1] + sa[1] * sb[0]) + sa[1] * sb[1]


def pair_add(x, y):
    s, e = two_sum(x[0], y[0])
    return s, e + (x[1] + y[1])


def tree(items, add):
    while len(items) > 1:
        items = [add(*items[i : i + 2]) if i + 1 < len(items) else items[i] for i in range(0, len(items), 2)]
    return items[0]


def pair_mul(x, y):
    p, e = two_prod(x[0], y[0], halves(x[0]), halves(y[0]))
    return p, e + (x[0] * y[1] + x[1] * y[0])


def quadratic(coefs, gram):
    terms = []
    for (i, j), g in gram.items():
        c = two_prod(coefs[i], coefs[j], halves(coefs[i]), halves(coefs[j]))
        terms.append(pair_mul(c, g))
    s = tree(terms, pair_add)
    return s[0] + s[1]


def lookup(kind, table):
    out = jnp.zeros(kind.shape, F32)
    for i, value in enumerate(table):
        out = jnp.where(kind == float(i), value, out)
    return out


def fluxes(temps, conds, first, last):
    rows = temps[0].shape[0]
    face = {}
    for i in range(first - 1, last):
        face[i] = (conds[i] + conds[i + 1]) * (temps[i + 1] - temps[i])
    out = []
    for i in range(first, last):
        t, k = temps[i], conds[i]
        total = face[i] - face[i - 1]
        for axis, size in ((0, rows), (1, t.shape[1])):
            f = (k + pltpu.roll(k, 1, axis)) * (pltpu.roll(t, 1, axis) - t)
            total = total + (f - pltpu.roll(f, size - 1, axis))
        out.append(0.5 * total)
    return out


def kernel(
    M, S, shells,
    warm_in, volt_in, pat_in, map_in, temp_in, kind_in,
    pot_out, brick_out,
    sheet_f, sheet_i, kind_v, first_b, later_b, onehot, red1, red2, heat_own, heat_ext, heat_b,
    local_sem, sheet_send, sheet_recv, len_send, len_recv, rad_send, rad_recv, late_send, late_recv,
    r1_send, r1_recv, r2_send, r2_recv, h_send, h_recv, e_send, e_recv,
):
    m = lax.axis_index("magnet")
    s = lax.axis_index("slab")
    rs, width = warm_in.shape
    rows, spokes = temp_in.shape[1], temp_in.shape[2]
    ext = 3 * rs
    brick = rows + 16
    g = m * S + s
    target0 = max(0, S - 2 - REACH)
    heated = s >= target0

    own_rows = pl.ds(pl.multiple_of(s * rs, 8), rs)
    mid = pl.ds(rs, rs)
    bmid = pl.ds(8, rows)
    zf = jnp.zeros((2, rs, width), F32)
    zi = jnp.zeros((2, rs, width), jnp.int32)
    for lo in (0, 2 * rs):
        sheet_f[:, lo : lo + rs, :] = zf
        sheet_i[:, lo : lo + rs, :] = zi
    ghost_t = jnp.zeros((brick, spokes), F32)
    ghost_k = jnp.full((brick, spokes), -1.0, F32)
    for buf in (first_b, later_b):
        for i in range(buf.shape[0]):
            buf[i, 0] = ghost_t
            buf[i, 1] = ghost_k
    local = [
        pltpu.make_async_copy(kind_in.at[0], kind_v, local_sem.at[0]),
        pltpu.make_async_copy(temp_in.at[0], first_b.at[1, 0, bmid, :], local_sem.at[1]),
        pltpu.make_async_copy(warm_in, sheet_f.at[0, mid, :], local_sem.at[2]),
        pltpu.make_async_copy(volt_in, sheet_f.at[1, mid, :], local_sem.at[3]),
        pltpu.make_async_copy(pat_in, sheet_i.at[0, mid, :], local_sem.at[4]),
        pltpu.make_async_copy(map_in.at[own_rows, :], sheet_i.at[1, mid, :], local_sem.at[5]),
    ]
    for c in local:
        c.start()

    barrier = pltpu.get_barrier_semaphore()

    def greet(who):
        pl.semaphore_signal(barrier, inc=1, device_id=who, device_id_type=MESH)

    for d in range(1, S):
        greet((m, lax.rem(s + d, S)))
    for d in range(1, M):
        greet((lax.rem(m + d, M), s))
    cross_up = (s == 0) & (m > 0)
    cross_down = (s == S - 1) & (m < M - 1)
    pl.when(cross_up)(lambda: greet((m - 1, S - 1)))
    pl.when(cross_down)(lambda: greet((m + 1, 0)))
    extra = jnp.where(cross_up | cross_down, 1, 0)
    for c in local:
        c.wait()
    first_b[1, 1, bmid, :] = kind_v[...].astype(F32)
    pl.semaphore_wait(barrier, S + M - 2 + extra)

    pending = []

    def sent(copies):
        for pred, c in copies:
            if pred is None:
                c.wait_send()
            else:
                pl.when(pred)(c.wait_send)

    def remote(pred, src, dst, send, recv, who):
        nonlocal pending
        c = pltpu.make_async_remote_copy(
            src_ref=src, dst_ref=dst, send_sem=send, recv_sem=recv, device_id=who, device_id_type=MESH
        )
        if pred is None:
            c.start()
        else:
            pl.when(pred)(c.start)
        pending.append((pred, c))

    def arrived(pred, src, dst, send, recv):
        c = pltpu.make_async_remote_copy(
            src_ref=src, dst_ref=dst, send_sem=send, recv_sem=recv, device_id=(m, s), device_id_type=MESH
        )
        if pred is None:
            c.wait_recv()
        else:
            pl.when(pred)(c.wait_recv)

    has_prev, has_next = g > 0, g < M * S - 1
    prev = (jnp.where(s == 0, m - 1, m), jnp.where(s == 0, S - 1, s - 1))
    nxt = (jnp.where(s == S - 1, m + 1, m), jnp.where(s == S - 1, 0, s + 1))
    before, after = pl.ds(0, rs), pl.ds(2 * rs, rs)
    for k, buf in enumerate((sheet_f, sheet_i)):
        remote(has_next, buf.at[:, mid, :], buf.at[:, before, :], sheet_send.at[2 * k], sheet_recv.at[2 * k], nxt)
        remote(has_prev, buf.at[:, mid, :], buf.at[:, after, :], sheet_send.at[2 * k + 1], sheet_recv.at[2 * k + 1], prev)
    layer = first_b.at[1]
    top_rows, end_rows = pl.ds(8, 8), pl.ds(rows, 8)
    top_halo, end_halo = pl.ds(0, 8), pl.ds(rows + 8, 8)
    remote(m < M - 1, layer.at[:, end_rows, :], layer.at[:, top_halo, :], len_send.at[0], len_recv.at[0], (m + 1, s))
    remote(m > 0, layer.at[:, top_rows, :], layer.at[:, end_halo, :], len_send.at[1], len_recv.at[1], (m - 1, s))

    lane_id = lax.broadcasted_iota(jnp.int32, (spokes, width), 0)
    base_cell = (shells - 2) * spokes
    cell_own = sheet_i[1, rs : 2 * rs, :] - base_cell
    upper_own = cell_own >= spokes
    col_own = jnp.where(upper_own, cell_own - spokes, cell_own)

    def put_onehot(at, row):
        onehot[at * spokes : (at + 1) * spokes, :] = jnp.where(lane_id == row, 1.0, 0.0).astype(jnp.bfloat16)

    for i in range(rs):
        put_onehot(i, col_own[i : i + 1, :])

    arrived(m > 0, layer.at[:, end_rows, :], layer.at[:, top_halo, :], len_send.at[0], len_recv.at[0])
    arrived(m < M - 1, layer.at[:, top_rows, :], layer.at[:, end_halo, :], len_send.at[1], len_recv.at[1])
    remote(s < S - 1, layer, first_b.at[0], rad_send.at[0], rad_recv.at[0], (m, s + 1))
    remote(s > 0, layer, first_b.at[2], rad_send.at[1], rad_recv.at[1], (m, s - 1))

    for k, buf in enumerate((sheet_f, sheet_i)):
        arrived(has_prev, buf.at[:, mid, :], buf.at[:, before, :], sheet_send.at[2 * k], sheet_recv.at[2 * k])
        arrived(has_next, buf.at[:, mid, :], buf.at[:, after, :], sheet_send.at[2 * k + 1], sheet_recv.at[2 * k + 1])

    pattern = sheet_i[0]
    row_id = lax.broadcasted_iota(jnp.int32, (ext, width), 0) + (g - 1) * rs
    col_id = lax.broadcasted_iota(jnp.int32, (ext, width), 1)
    valid = (row_id >= 0) & (row_id < M * S * rs)
    left_edge, right_edge = col_id == 0, col_id == width - 1

    def from_up(v):
        return pltpu.roll(v, 1, 0)

    def from_down(v):
        return pltpu.roll(v, ext - 1, 0)

    def from_left(v):
        return jnp.where(left_edge, 0.0, pltpu.roll(v, 1, 1))

    def from_right(v):
        return jnp.where(right_edge, 0.0, pltpu.roll(v, width - 1, 1))

    sides = (from_up, from_down, from_left, from_right)
    sigma = jnp.where(valid, jnp.where(pattern == 1, copper_factor, 1.0) / (1.0 + sheet_slope * sheet_f[0]), 0.0)
    coeffs = [0.5 * (sigma + side(sigma)) for side in sides]
    contact = jnp.where(pattern == 2, contact_gain, 0.0)
    diagonal = leak_diag + contact + coeffs[0] + coeffs[1] + coeffs[2] + coeffs[3]

    def apply(v):
        out = diagonal * v
        for c, side in zip(coeffs, sides):
            out = out - c * side(v)
        return jnp.where(valid, out, 0.0)

    basis = [jnp.where(valid, contact * sheet_f[1], 0.0)]
    for _ in range(3):
        basis.append(apply(basis[-1]))

    chunks = [[v[rs : 2 * rs, c : c + 128] for c in range(0, width, 128)] for v in basis]
    split = [[halves(v) for v in field] for field in chunks]
    highs, lows = [], []
    for i, j in GRAM:
        pairs = [two_prod(a, b, sa, sb) for a, b, sa, sb in zip(chunks[i], chunks[j], split[i], split[j])]
        p = tree(pairs, pair_add)
        for step in (4, 2, 1):
            p = pair_add(p, (pltpu.roll(p[0], step, 0), pltpu.roll(p[1], step, 0)))
        highs.append(p[0][0:1])
        lows.append(p[1][0:1])
    fill = [jnp.zeros((16 - len(GRAM), 128), F32)]
    red1[s] = jnp.concatenate(highs + fill + lows + fill, axis=0)
    for d in range(1, S):
        remote(None, red1.at[s], red1.at[s], r1_send.at[d], r1_recv.at[d], (m, lax.rem(s + d, S)))

    arrived(s > 0, layer, first_b.at[0], rad_send.at[0], rad_recv.at[0])
    arrived(s < S - 1, layer, first_b.at[2], rad_send.at[1], rad_recv.at[1])

    def conduct(temps, kinds):
        return [lookup(k, conduct_table) * (1.0 + diffusivity_derivative * t) for t, k in zip(temps, kinds)]

    def rate(kind):
        return lookup(kind, tuple(time_step / c for c in capacity_table))

    temps = [first_b[i, 0] for i in range(3)]
    kinds = [first_b[i, 1] for i in range(3)]
    (flux,) = fluxes(temps, conduct(temps, kinds), 1, 2)
    later_b[REACH, 0] = temps[1] + rate(kinds[1]) * flux
    later_b[REACH, 1] = kinds[1]
    early, pending = pending, []
    def part(slot, d):
        if d == 1:
            return later_b.at[slot, 0]
        return later_b.at[slot, :, bmid, :] if d == REACH else later_b.at[slot]

    later_b[REACH - 1, 1] = kinds[0]
    later_b[REACH + 1, 1] = kinds[2]
    for d in range(1, REACH + 1):
        remote(s < S - d, part(REACH, d), part(REACH - d, d), late_send.at[2 * d - 2], late_recv.at[2 * d - 2], (m, s + d))
        remote(s >= d, part(REACH, d), part(REACH + d, d), late_send.at[2 * d - 1], late_recv.at[2 * d - 1], (m, s - d))
    late, pending = pending, []

    before_string = s == 0

    def outer(a):
        return jnp.where(before_string, pltpu.roll(a[0:rs], 3, 0), a[2 * rs :])

    cell_ext = outer(sheet_i[1]) - base_cell
    cell_ext = jnp.clip(cell_ext, 0, 2 * spokes - 1)
    upper_ext = cell_ext >= spokes
    col_ext = jnp.where(upper_ext, cell_ext - spokes, cell_ext)
    for i in range(3):
        put_onehot(rs + i, col_ext[i : i + 1, :])

    def pair_of(ref, i):
        return ref[i, 0:16], ref[i, 16:32]

    for d in range(1, S):
        src = lax.rem(s + S - d, S)
        arrived(None, red1.at[s], red1.at[src], r1_send.at[d], r1_recv.at[d])
    total = tree([pair_of(red1, i) for i in range(S)], pair_add)
    red2[m] = jnp.concatenate(total, axis=0)
    for d in range(1, M):
        remote(None, red2.at[m], red2.at[m], r2_send.at[d], r2_recv.at[d], (lax.rem(m + d, M), s))
    for d in range(1, M):
        src = lax.rem(m + M - d, M)
        arrived(None, red2.at[m], red2.at[src], r2_send.at[d], r2_recv.at[d])
    high, low = tree([pair_of(red2, i) for i in range(M)], pair_add)
    grid = 1024.0 * jnp.max(jnp.abs(high), axis=1, keepdims=True)
    coarse = (high + grid) - grid
    rest = jnp.sum((high - coarse) + low, axis=1, keepdims=True)
    sums = two_sum(jnp.sum(coarse, axis=1, keepdims=True), rest)
    gram = {ij: (sums[0][n : n + 1], sums[1][n : n + 1]) for n, ij in enumerate(GRAM)}

    def twice(x):
        return 2.0 * x[0], 2.0 * x[1]

    plain = {(i, j): gram[i, j] if i == j else twice(gram[i, j]) for i, j in GRAM if j < 3}
    with_a = {
        (0, 0): gram[0, 1],
        (0, 1): pair_add(gram[0, 2], gram[1, 1]),
        (1, 1): gram[1, 2],
        (0, 2): pair_add(gram[0, 3], gram[1, 2]),
        (1, 2): pair_add(gram[1, 3], gram[2, 2]),
        (2, 2): gram[2, 3],
    }

    def upto(table, n):
        return {ij: v for ij, v in table.items() if ij[1] < n}

    one = jnp.ones_like(gram[0, 0][0])
    norm0 = gram[0, 0][0]
    a0 = norm0 / gram[0, 1][0]
    norm1 = quadratic([one, -a0], upto(plain, 2))
    b1 = norm1 / norm0
    p1 = [1.0 + b1, -a0]
    a1 = norm1 / quadratic(p1, upto(with_a, 2))
    r2 = [one, -a0 - a1 * p1[0], -a1 * p1[1]]
    norm2 = quadratic(r2, plain)
    b2 = norm2 / norm1
    p2 = [r2[0] + b2 * p1[0], r2[1] + b2 * p1[1], r2[2]]
    a2 = norm2 / quadratic(p2, with_a)
    weights = [a0 + a1 * p1[0] + a2 * p2[0], a1 * p1[1] + a2 * p2[1], a2 * p2[2]]
    potential = weights[0] * basis[0] + weights[1] * basis[1] + weights[2] * basis[2]
    pot_out[...] = potential[rs : 2 * rs]

    joule = jnp.zeros_like(potential)
    for c, side in zip(coeffs, sides):
        drop = potential - side(potential)
        joule = joule + c * (drop * drop)
    joule = heat_factor * joule
    sub_id = lax.broadcasted_iota(jnp.int32, (rs, spokes), 0)

    def binned(power, upper, first, count):
        parts = []
        for value in (jnp.where(upper, 0.0, power), jnp.where(upper, power, 0.0)):
            for _ in range(3):
                part = value.astype(jnp.bfloat16).astype(F32)
                parts.append(part)
                value = value - part
        lhs = jnp.concatenate(parts, axis=0).astype(jnp.bfloat16)
        cols = onehot[first * spokes : (first + count) * spokes, :]
        out = lax.dot_general(lhs, cols, (((1,), (1,)), ((), ())), preferred_element_type=F32)
        heats = []
        for k in range(2):
            part = out[3 * k * rs : (3 * k + 1) * rs]
            part = part + out[(3 * k + 1) * rs : (3 * k + 2) * rs] + out[(3 * k + 2) * rs : (3 * k + 3) * rs]
            heat = jnp.zeros((rs, spokes), F32)
            for i in range(count):
                heat = jnp.where(sub_id == i, part[:, i * spokes : (i + 1) * spokes], heat)
            heats.append(heat)
        return heats

    lower, higher = binned(joule[rs : 2 * rs], upper_own, 0, rs)
    heat_own[0] = lower
    heat_own[1] = higher
    at = pl.ds(pl.multiple_of(8 + rs * s, 8), rs)
    for n, t in enumerate(range(target0, S)):
        remote(s != t, heat_own, heat_b.at[:, at, :], h_send.at[n], h_recv.at[s], (m, t))
    ext_lower, ext_higher = binned(outer(joule), upper_ext, rs, 3)
    heat_ext[0] = jnp.where(before_string, pltpu.roll(ext_lower, rs - 3, 0), ext_lower)
    heat_ext[1] = jnp.where(before_string, pltpu.roll(ext_higher, rs - 3, 0), ext_higher)
    for n, t in enumerate(range(target0, S)):
        remote((s == 0) & (s != t), heat_ext, heat_b.at[:, top_halo, :], e_send.at[n, 0], e_recv.at[0], (m, t))
        remote((s == S - 1) & (s != t), heat_ext, heat_b.at[:, end_halo, :], e_send.at[n, 1], e_recv.at[1], (m, t))

    @pl.when(heated)
    def _():
        heat_b[0, at, :] = lower
        heat_b[1, at, :] = higher

    @pl.when(s == S - 1)
    def _():
        heat_b[:, end_halo, :] = heat_ext[...]

    if target0 == 0:
        @pl.when(s == 0)
        def _():
            heat_b[:, top_halo, :] = heat_ext[...]

    for d in range(1, REACH + 1):
        arrived(s >= d, part(REACH, d), part(REACH - d, d), late_send.at[2 * d - 2], late_recv.at[2 * d - 2])
        arrived(s < S - d, part(REACH, d), part(REACH + d, d), late_send.at[2 * d - 1], late_recv.at[2 * d - 1])
    for j in range(S):
        part = heat_b.at[:, 8 + rs * j : 8 + rs * (j + 1), :]
        arrived(heated & (s != j), heat_own, part, h_send.at[0], h_recv.at[j])
    arrived(heated & (s != 0), heat_ext, heat_b.at[:, top_halo, :], e_send.at[0, 0], e_recv.at[0])
    arrived(heated & (s != S - 1), heat_ext, heat_b.at[:, end_halo, :], e_send.at[0, 1], e_recv.at[1])
    sent(late)
    for k in range(2):
        slot = REACH + (S - 2 + k) - s

        @pl.when((slot <= 2 * REACH) & (slot >= 0))
        def _():
            later_b[slot, 0] = later_b[slot, 0] + rate(later_b[slot, 1]) * heat_b[k]

    count = 2 * REACH + 1
    temps = [later_b[i, 0] for i in range(count)]
    kinds = [later_b[i, 1] for i in range(count)]
    heat_low, heat_high = heat_b[0], heat_b[1]
    for step in range(1, REACH + 1):
        conds = conduct(temps, kinds)
        flux = fluxes(temps, conds, step, count - step)
        for i, f in zip(range(step, count - step), flux):
            place = s + i - REACH
            heat = jnp.where(place == S - 2, heat_low, jnp.where(place == S - 1, heat_high, 0.0))
            temps[i] = temps[i] + rate(kinds[i]) * (f + heat)
    brick_out[0] = temps[REACH][8 : 8 + rows]
    sent(early + pending)


def hand_over(pot, brick, pot_out, brick_out, sem):
    copies = [pltpu.make_async_copy(pot, pot_out, sem.at[0]), pltpu.make_async_copy(brick, brick_out, sem.at[1])]
    for c in copies:
        c.start()
    for c in copies:
        c.wait()


def solution(mesh):
    M, S = mesh.shape["magnet"], mesh.shape["slab"]

    def local(warm, volt, pattern, cells, temp, kind):
        rs, width = warm.shape
        depth, rows, spokes = temp.shape
        brick = rows + 16
        dma = pltpu.SemaphoreType.DMA
        targets = REACH + 2
        shapes = (
            jax.ShapeDtypeStruct((rs, width), F32),
            jax.ShapeDtypeStruct((depth, rows, spokes), F32),
        )
        outs = pl.pallas_call(
            functools.partial(kernel, M, S, depth * S),
            out_shape=shapes,
            in_specs=[pl.BlockSpec(memory_space=pltpu.HBM)] * 6,
            out_specs=[pl.BlockSpec(memory_space=pltpu.VMEM)] * 2,
            scratch_shapes=[
                pltpu.VMEM((2, 3 * rs, width), F32),
                pltpu.VMEM((2, 3 * rs, width), jnp.int32),
                pltpu.VMEM((rows, spokes), jnp.int32),
                pltpu.VMEM((3, 2, brick, spokes), F32),
                pltpu.VMEM((2 * REACH + 1, 2, brick, spokes), F32),
                pltpu.VMEM(((rs + 3) * spokes, width), jnp.bfloat16),
                pltpu.VMEM((S, 32, 128), F32),
                pltpu.VMEM((M, 32, 128), F32),
                pltpu.VMEM((2, rs, spokes), F32),
                pltpu.VMEM((2, rs, spokes), F32),
                pltpu.VMEM((2, brick, spokes), F32),
                dma((6,)),
                dma((4,)), dma((4,)),
                dma((2,)), dma((2,)),
                dma((2,)), dma((2,)),
                dma((2 * REACH,)), dma((2 * REACH,)),
                dma((S,)), dma((S,)),
                dma((M,)), dma((M,)),
                dma((targets,)), dma((S,)),
                dma((targets, 2)), dma((2,)),
            ],
            compiler_params=pltpu.CompilerParams(
                collective_id=0, has_side_effects=True, vmem_limit_bytes=63 * 1024 * 1024
            ),
            name="window",
        )(warm, volt, pattern, cells, temp, kind)
        return pl.pallas_call(
            hand_over,
            out_shape=shapes,
            in_specs=[pl.BlockSpec(memory_space=pltpu.HBM)] * 2,
            out_specs=[pl.BlockSpec(memory_space=pltpu.HBM)] * 2,
            scratch_shapes=[dma((2,))],
            compiler_params=pltpu.CompilerParams(vmem_limit_bytes=63 * 1024 * 1024),
            name="hand_over",
        )(*outs)

    return jax.shard_map(
        local,
        mesh=mesh,
        in_specs=(
            P(("magnet", "slab"), None),
            P(("magnet", "slab"), None),
            P(("magnet", "slab"), None),
            P("magnet", None),
            P("slab", "magnet", None),
            P("slab", "magnet", None),
        ),
        out_specs=(P(("magnet", "slab"), None), P("slab", "magnet", None)),
        check_vma=False,
    )
```

```python
import functools

import jax
import jax.numpy as jnp
from jax import lax
from jax.experimental import pallas as pl
from jax.experimental.pallas import tpu as pltpu
from jax.sharding import PartitionSpec as P

MESH = pl.DeviceIdType.MESH
F32 = jnp.float32
leak_diag = 0.25
contact_gain = 4.0
copper_factor = 3.0
sheet_slope = 0.5
heat_factor = 1.5
time_step = 0.03
conduct_table = (0.3, 1.0, 2.0, 0.6)
capacity_table = (1.0, 1.5, 2.0, 1.2)
diffusivity_derivative = 0.4
REACH = 3
GRAM = ((0, 0), (0, 1), (0, 2), (0, 3), (1, 1), (1, 2), (1, 3), (2, 2), (2, 3))


def two_sum(a, b):
    s = a + b
    t = s - a
    return s, (a - (s - t)) + (b - t)


def halves(a):
    c = a * 4097.0
    high = c - (c - a)
    return high, a - high


def two_prod(a, b, sa, sb):
    p = a * b
    return p, ((sa[0] * sb[0] - p) + sa[0] * sb[1] + sa[1] * sb[0]) + sa[1] * sb[1]


def pair_add(x, y):
    s, e = two_sum(x[0], y[0])
    return s, e + (x[1] + y[1])


def tree(items, add):
    while len(items) > 1:
        items = [add(*items[i : i + 2]) if i + 1 < len(items) else items[i] for i in range(0, len(items), 2)]
    return items[0]


def pair_mul(x, y):
    p, e = two_prod(x[0], y[0], halves(x[0]), halves(y[0]))
    return p, e + (x[0] * y[1] + x[1] * y[0])


def quadratic(coefs, gram):
    terms = []
    for (i, j), g in gram.items():
        c = two_prod(coefs[i], coefs[j], halves(coefs[i]), halves(coefs[j]))
        terms.append(pair_mul(c, g))
    s = tree(terms, pair_add)
    return s[0] + s[1]


def lookup(kind, table):
    out = jnp.zeros(kind.shape, F32)
    for i, value in enumerate(table):
        out = jnp.where(kind == float(i), value, out)
    return out


def fluxes(temps, conds, first, last):
    rows = temps[0].shape[0]
    face = {}
    for i in range(first - 1, last):
        face[i] = (conds[i] + conds[i + 1]) * (temps[i + 1] - temps[i])
    out = []
    for i in range(first, last):
        t, k = temps[i], conds[i]
        total = face[i] - face[i - 1]
        for axis, size in ((0, rows), (1, t.shape[1])):
            f = (k + pltpu.roll(k, 1, axis)) * (pltpu.roll(t, 1, axis) - t)
            total = total + (f - pltpu.roll(f, size - 1, axis))
        out.append(0.5 * total)
    return out


def kernel(
    M, S, shells,
    warm_in, volt_in, pat_in, map_in, temp_in, kind_in,
    pot_out, brick_out,
    sheet_f, sheet_i, kind_v, first_b, later_b, onehot, red1, red2, heat_own, heat_ext, heat_b, base_b, rate_b,
    local_sem, sheet_send, sheet_recv, len_send, len_recv, rad_send, rad_recv, late_send, late_recv,
    r1_send, r1_recv, r2_send, r2_recv, h_send, h_recv, e_send, e_recv,
):
    m = lax.axis_index("magnet")
    s = lax.axis_index("slab")
    rs, width = warm_in.shape
    rows, spokes = temp_in.shape[1], temp_in.shape[2]
    ext = 3 * rs
    brick = rows + 16
    g = m * S + s
    target0 = max(0, S - 2 - REACH)
    heated = s >= target0

    own_rows = pl.ds(pl.multiple_of(s * rs, 8), rs)
    mid = pl.ds(rs, rs)
    bmid = pl.ds(8, rows)
    zf = jnp.zeros((2, rs, width), F32)
    zi = jnp.zeros((2, rs, width), jnp.int32)
    for lo in (0, 2 * rs):
        sheet_f[:, lo : lo + rs, :] = zf
        sheet_i[:, lo : lo + rs, :] = zi
    ghost_t = jnp.zeros((brick, spokes), F32)
    ghost_k = jnp.full((brick, spokes), -1.0, F32)
    for buf in (first_b, later_b):
        for i in range(buf.shape[0]):
            buf[i, 0] = ghost_t
            buf[i, 1] = ghost_k
    for i in range(heat_b.shape[0]):
        heat_b[i] = ghost_t
    local = [
        pltpu.make_async_copy(kind_in.at[0], kind_v, local_sem.at[0]),
        pltpu.make_async_copy(temp_in.at[0], first_b.at[1, 0, bmid, :], local_sem.at[1]),
        pltpu.make_async_copy(warm_in, sheet_f.at[0, mid, :], local_sem.at[2]),
        pltpu.make_async_copy(volt_in, sheet_f.at[1, mid, :], local_sem.at[3]),
        pltpu.make_async_copy(pat_in, sheet_i.at[0, mid, :], local_sem.at[4]),
        pltpu.make_async_copy(map_in.at[own_rows, :], sheet_i.at[1, mid, :], local_sem.at[5]),
    ]
    for c in local:
        c.start()

    barrier = pltpu.get_barrier_semaphore()

    def greet(who):
        pl.semaphore_signal(barrier, inc=1, device_id=who, device_id_type=MESH)

    for d in range(1, S):
        greet((m, lax.rem(s + d, S)))
    for d in range(1, M):
        greet((lax.rem(m + d, M), s))
    cross_up = (s == 0) & (m > 0)
    cross_down = (s == S - 1) & (m < M - 1)
    pl.when(cross_up)(lambda: greet((m - 1, S - 1)))
    pl.when(cross_down)(lambda: greet((m + 1, 0)))
    extra = jnp.where(cross_up | cross_down, 1, 0)
    for c in local:
        c.wait()
    first_b[1, 1, bmid, :] = kind_v[...].astype(F32)
    pl.semaphore_wait(barrier, S + M - 2 + extra)

    pending = []

    def sent(copies):
        for pred, c in copies:
            if pred is None:
                c.wait_send()
            else:
                pl.when(pred)(c.wait_send)

    def remote(pred, src, dst, send, recv, who):
        nonlocal pending
        c = pltpu.make_async_remote_copy(
            src_ref=src, dst_ref=dst, send_sem=send, recv_sem=recv, device_id=who, device_id_type=MESH
        )
        if pred is None:
            c.start()
        else:
            pl.when(pred)(c.start)
        pending.append((pred, c))

    def arrived(pred, src, dst, send, recv):
        c = pltpu.make_async_remote_copy(
            src_ref=src, dst_ref=dst, send_sem=send, recv_sem=recv, device_id=(m, s), device_id_type=MESH
        )
        if pred is None:
            c.wait_recv()
        else:
            pl.when(pred)(c.wait_recv)

    has_prev, has_next = g > 0, g < M * S - 1
    prev = (jnp.where(s == 0, m - 1, m), jnp.where(s == 0, S - 1, s - 1))
    nxt = (jnp.where(s == S - 1, m + 1, m), jnp.where(s == S - 1, 0, s + 1))
    before, after = pl.ds(0, rs), pl.ds(2 * rs, rs)
    for k, buf in enumerate((sheet_f, sheet_i)):
        remote(has_next, buf.at[:, mid, :], buf.at[:, before, :], sheet_send.at[2 * k], sheet_recv.at[2 * k], nxt)
        remote(has_prev, buf.at[:, mid, :], buf.at[:, after, :], sheet_send.at[2 * k + 1], sheet_recv.at[2 * k + 1], prev)
    layer = first_b.at[1]
    top_rows, end_rows = pl.ds(8, 8), pl.ds(rows, 8)
    top_halo, end_halo = pl.ds(0, 8), pl.ds(rows + 8, 8)
    remote(m < M - 1, layer.at[:, end_rows, :], layer.at[:, top_halo, :], len_send.at[0], len_recv.at[0], (m + 1, s))
    remote(m > 0, layer.at[:, top_rows, :], layer.at[:, end_halo, :], len_send.at[1], len_recv.at[1], (m - 1, s))

    lane_id = lax.broadcasted_iota(jnp.int32, (spokes, width), 0)
    base_cell = (shells - 2) * spokes
    cell_own = sheet_i[1, rs : 2 * rs, :] - base_cell
    upper_own = cell_own >= spokes
    col_own = jnp.where(upper_own, cell_own - spokes, cell_own)

    def put_onehot(at, row):
        onehot[at * spokes : (at + 1) * spokes, :] = jnp.where(lane_id == row, 1.0, 0.0).astype(jnp.bfloat16)

    for i in range(rs):
        put_onehot(i, col_own[i : i + 1, :])

    arrived(m > 0, layer.at[:, end_rows, :], layer.at[:, top_halo, :], len_send.at[0], len_recv.at[0])
    arrived(m < M - 1, layer.at[:, top_rows, :], layer.at[:, end_halo, :], len_send.at[1], len_recv.at[1])
    remote(s < S - 1, layer, first_b.at[0], rad_send.at[0], rad_recv.at[0], (m, s + 1))
    remote(s > 0, layer, first_b.at[2], rad_send.at[1], rad_recv.at[1], (m, s - 1))

    for k, buf in enumerate((sheet_f, sheet_i)):
        arrived(has_prev, buf.at[:, mid, :], buf.at[:, before, :], sheet_send.at[2 * k], sheet_recv.at[2 * k])
        arrived(has_next, buf.at[:, mid, :], buf.at[:, after, :], sheet_send.at[2 * k + 1], sheet_recv.at[2 * k + 1])

    pattern = sheet_i[0]
    row_id = lax.broadcasted_iota(jnp.int32, (ext, width), 0) + (g - 1) * rs
    col_id = lax.broadcasted_iota(jnp.int32, (ext, width), 1)
    valid = (row_id >= 0) & (row_id < M * S * rs)
    left_edge, right_edge = col_id == 0, col_id == width - 1

    def from_up(v):
        return pltpu.roll(v, 1, 0)

    def from_down(v):
        return pltpu.roll(v, ext - 1, 0)

    def from_left(v):
        return jnp.where(left_edge, 0.0, pltpu.roll(v, 1, 1))

    def from_right(v):
        return jnp.where(right_edge, 0.0, pltpu.roll(v, width - 1, 1))

    sides = (from_up, from_down, from_left, from_right)
    sigma = jnp.where(valid, jnp.where(pattern == 1, copper_factor, 1.0) / (1.0 + sheet_slope * sheet_f[0]), 0.0)
    coeffs = [0.5 * (sigma + side(sigma)) for side in sides]
    contact = jnp.where(pattern == 2, contact_gain, 0.0)
    diagonal = leak_diag + contact + coeffs[0] + coeffs[1] + coeffs[2] + coeffs[3]

    def apply(v):
        out = diagonal * v
        for c, side in zip(coeffs, sides):
            out = out - c * side(v)
        return jnp.where(valid, out, 0.0)

    basis = [jnp.where(valid, contact * sheet_f[1], 0.0)]
    for _ in range(3):
        basis.append(apply(basis[-1]))

    chunks = [[v[rs : 2 * rs, c : c + 128] for c in range(0, width, 128)] for v in basis]
    split = [[halves(v) for v in field] for field in chunks]
    pairs = []
    for i, j in GRAM:
        terms = [two_prod(a, b, sa, sb) for a, b, sa, sb in zip(chunks[i], chunks[j], split[i], split[j])]
        pairs.append(tree(terms, pair_add))
    sub = lax.broadcasted_iota(jnp.int32, (8, 128), 0)
    lane = lax.broadcasted_iota(jnp.int32, (8, 128), 1)

    def folded(a, b, step):
        first = (sub & step) == 0
        near = jnp.where(first, a, b)
        far = jnp.where(first, pltpu.roll(a, 8 - step, 0), pltpu.roll(b, step, 0))
        return near, far

    eight, ninth = pairs[:8], pairs[8]
    for step in (4, 2, 1):
        merged = []
        for a, b in zip(eight[:step], eight[step:]):
            parts = [folded(x, y, step) for x, y in zip(a, b)]
            merged.append(pair_add((parts[0][0], parts[1][0]), (parts[0][1], parts[1][1])))
        eight = merged

    def fold_lanes(p):
        for step in (64, 32):
            p = pair_add(p, (pltpu.roll(p[0], step, 1), pltpu.roll(p[1], step, 1)))
        return p

    eight, ninth = fold_lanes(eight[0]), fold_lanes(ninth)
    is_low = (lane & 32) != 0
    both = [jnp.where(lane < 64, a, b) for a, b in zip(eight, ninth)]
    red1[s] = jnp.where(is_low, both[1], both[0])
    for d in range(1, S):
        remote(None, red1.at[s], red1.at[s], r1_send.at[d], r1_recv.at[d], (m, lax.rem(s + d, S)))

    arrived(s > 0, layer, first_b.at[0], rad_send.at[0], rad_recv.at[0])
    arrived(s < S - 1, layer, first_b.at[2], rad_send.at[1], rad_recv.at[1])

    def conduct(temps, kinds):
        return [lookup(k, conduct_table) * (1.0 + diffusivity_derivative * t) for t, k in zip(temps, kinds)]

    def rate(kind):
        return lookup(kind, tuple(time_step / c for c in capacity_table))

    temps = [first_b[i, 0] for i in range(3)]
    kinds = [first_b[i, 1] for i in range(3)]
    (flux,) = fluxes(temps, conduct(temps, kinds), 1, 2)
    later_b[REACH, 0] = temps[1] + rate(kinds[1]) * flux
    later_b[REACH, 1] = kinds[1]
    early, pending = pending, []
    def part(slot, d):
        if d == 1:
            return later_b.at[slot, 0]
        return later_b.at[slot, :, bmid, :] if d == REACH else later_b.at[slot]

    later_b[REACH - 1, 1] = kinds[0]
    later_b[REACH + 1, 1] = kinds[2]
    for d in range(1, REACH + 1):
        remote(s < S - d, part(REACH, d), part(REACH - d, d), late_send.at[2 * d - 2], late_recv.at[2 * d - 2], (m, s + d))
        remote(s >= d, part(REACH, d), part(REACH + d, d), late_send.at[2 * d - 1], late_recv.at[2 * d - 1], (m, s - d))
    late, pending = pending, []

    before_string = s == 0

    def outer(a):
        return jnp.where(before_string, pltpu.roll(a[0:rs], 3, 0), a[2 * rs :])

    cell_ext = outer(sheet_i[1]) - base_cell
    cell_ext = jnp.clip(cell_ext, 0, 2 * spokes - 1)
    upper_ext = cell_ext >= spokes
    col_ext = jnp.where(upper_ext, cell_ext - spokes, cell_ext)
    for i in range(3):
        put_onehot(rs + i, col_ext[i : i + 1, :])

    def pair_of(ref, i):
        tile = ref[i]
        return tile, pltpu.roll(tile, 96, 1)

    for d in range(1, S):
        src = lax.rem(s + S - d, S)
        arrived(None, red1.at[s], red1.at[src], r1_send.at[d], r1_recv.at[d])
    total = tree([pair_of(red1, i) for i in range(S)], pair_add)
    red2[m] = jnp.where(is_low, pltpu.roll(total[1], 32, 1), total[0])
    for d in range(1, M):
        remote(None, red2.at[m], red2.at[m], r2_send.at[d], r2_recv.at[d], (lax.rem(m + d, M), s))
    for d in range(1, M):
        src = lax.rem(m + M - d, M)
        arrived(None, red2.at[m], red2.at[src], r2_send.at[d], r2_recv.at[d])
    high, low = tree([pair_of(red2, i) for i in range(M)], pair_add)
    def added(high, low, axes):
        grid = 1024.0 * jnp.max(jnp.abs(high), axis=axes, keepdims=True)
        coarse = (high + grid) - grid
        rest = jnp.sum((high - coarse) + low, axis=axes, keepdims=True)
        return two_sum(jnp.sum(coarse, axis=axes, keepdims=True), rest)

    in_eight, in_ninth = lane < 32, (lane >= 64) & (lane < 96)
    sums = added(jnp.where(in_eight, high, 0.0), jnp.where(in_eight, low, 0.0), 1)
    gram = {ij: (sums[0][n : n + 1], sums[1][n : n + 1]) for n, ij in enumerate(GRAM[:8])}
    gram[GRAM[8]] = added(jnp.where(in_ninth, high, 0.0), jnp.where(in_ninth, low, 0.0), (0, 1))

    def twice(x):
        return 2.0 * x[0], 2.0 * x[1]

    plain = {(i, j): gram[i, j] if i == j else twice(gram[i, j]) for i, j in GRAM if j < 3}
    with_a = {
        (0, 0): gram[0, 1],
        (0, 1): pair_add(gram[0, 2], gram[1, 1]),
        (1, 1): gram[1, 2],
        (0, 2): pair_add(gram[0, 3], gram[1, 2]),
        (1, 2): pair_add(gram[1, 3], gram[2, 2]),
        (2, 2): gram[2, 3],
    }

    def upto(table, n):
        return {ij: v for ij, v in table.items() if ij[1] < n}

    one = jnp.ones_like(gram[0, 0][0])
    norm0 = gram[0, 0][0]
    a0 = norm0 / gram[0, 1][0]
    norm1 = quadratic([one, -a0], upto(plain, 2))
    b1 = norm1 / norm0
    p1 = [1.0 + b1, -a0]
    a1 = norm1 / quadratic(p1, upto(with_a, 2))
    r2 = [one, -a0 - a1 * p1[0], -a1 * p1[1]]
    norm2 = quadratic(r2, plain)
    b2 = norm2 / norm1
    p2 = [r2[0] + b2 * p1[0], r2[1] + b2 * p1[1], r2[2]]
    a2 = norm2 / quadratic(p2, with_a)
    weights = [a0 + a1 * p1[0] + a2 * p2[0], a1 * p1[1] + a2 * p2[1], a2 * p2[2]]
    potential = weights[0] * basis[0] + weights[1] * basis[1] + weights[2] * basis[2]
    pot_out[...] = potential[rs : 2 * rs]

    joule = jnp.zeros_like(potential)
    for c, side in zip(coeffs, sides):
        drop = potential - side(potential)
        joule = joule + c * (drop * drop)
    joule = heat_factor * joule
    sub_id = lax.broadcasted_iota(jnp.int32, (rs, spokes), 0)

    def binned(power, upper, first, count):
        parts = []
        for value in (jnp.where(upper, 0.0, power), jnp.where(upper, power, 0.0)):
            for _ in range(2):
                part = value.astype(jnp.bfloat16).astype(F32)
                parts.append(part)
                value = value - part
        lhs = jnp.concatenate(parts, axis=0).astype(jnp.bfloat16)
        cols = onehot[first * spokes : (first + count) * spokes, :]
        out = lax.dot_general(lhs, cols, (((1,), (1,)), ((), ())), preferred_element_type=F32)
        heats = []
        for k in range(2):
            part = out[2 * k * rs : (2 * k + 1) * rs] + out[(2 * k + 1) * rs : (2 * k + 2) * rs]
            heat = jnp.zeros((rs, spokes), F32)
            for i in range(count):
                heat = jnp.where(sub_id == i, part[:, i * spokes : (i + 1) * spokes], heat)
            heats.append(heat)
        return heats

    lower, higher = binned(joule[rs : 2 * rs], upper_own, 0, rs)
    heat_own[0] = lower
    heat_own[1] = higher
    at = pl.ds(pl.multiple_of(8 + rs * s, 8), rs)

    def slots(t):
        return pl.ds(REACH + S - 2 - t, 2)

    mine, pending = pending, []
    for n, t in enumerate(range(target0, S)):
        remote(s != t, heat_own, heat_b.at[slots(t), at, :], h_send.at[n], h_recv.at[s], (m, t))
    ext_lower, ext_higher = binned(outer(joule), upper_ext, rs, 3)
    heat_ext[0] = jnp.where(before_string, pltpu.roll(ext_lower, rs - 3, 0), ext_lower)
    heat_ext[1] = jnp.where(before_string, pltpu.roll(ext_higher, rs - 3, 0), ext_higher)
    at_end = (s == 0) | (s == S - 1)
    side_of = jnp.where(before_string, 0, 1)
    ext_at = pl.ds(pl.multiple_of(jnp.where(before_string, 0, rows + 8), 8), 8)
    for n, t in enumerate(range(target0, S)):
        remote(at_end & (s != t), heat_ext, heat_b.at[slots(t), ext_at, :], e_send.at[n], e_recv.at[side_of], (m, t))

    @pl.when(heated)
    def _():
        slot = REACH + S - 2 - s
        heat_b[slot, at, :] = lower
        heat_b[slot + 1, at, :] = higher

        @pl.when(at_end)
        def _():
            heat_b[slot, ext_at, :] = heat_ext[0]
            heat_b[slot + 1, ext_at, :] = heat_ext[1]

    for d in range(1, REACH + 1):
        arrived(s >= d, part(REACH, d), part(REACH - d, d), late_send.at[2 * d - 2], late_recv.at[2 * d - 2])
        arrived(s < S - d, part(REACH, d), part(REACH + d, d), late_send.at[2 * d - 1], late_recv.at[2 * d - 1])
    count = 2 * REACH + 1
    for i in range(count):
        kind = later_b[i, 1]
        base_b[i] = lookup(kind, conduct_table)
        rate_b[i] = rate(kind)
    sent(early + late + mine)
    pair = pl.ds(0, 2)
    for j in range(S):
        at_j = pl.ds(8 + rs * j, rs)
        arrived(heated & (s != j), heat_own, heat_b.at[pair, at_j, :], h_send.at[0], h_recv.at[j])
    arrived(heated & (s != 0), heat_ext, heat_b.at[pair, top_halo, :], e_send.at[0], e_recv.at[0])
    arrived(heated & (s != S - 1), heat_ext, heat_b.at[pair, end_halo, :], e_send.at[0], e_recv.at[1])

    count = 2 * REACH + 1
    temps = [later_b[i, 0] + rate_b[i] * heat_b[i] for i in range(count)]
    for step in range(1, REACH + 1):
        first, last = step, count - step
        near = range(first - 1, last + 1)
        conds = {i: base_b[i] * (1.0 + diffusivity_derivative * temps[i]) for i in near}
        for i, f in zip(range(first, last), fluxes(temps, conds, first, last)):
            temps[i] = temps[i] + rate_b[i] * (f + heat_b[i])
    brick_out[0] = temps[REACH][8 : 8 + rows]
    sent(pending)


def solution(mesh):
    M, S = mesh.shape["magnet"], mesh.shape["slab"]

    def local(warm, volt, pattern, cells, temp, kind):
        rs, width = warm.shape
        depth, rows, spokes = temp.shape
        brick = rows + 16
        dma = pltpu.SemaphoreType.DMA
        targets = REACH + 2
        shapes = (
            jax.ShapeDtypeStruct((rs, width), F32),
            jax.ShapeDtypeStruct((depth, rows, spokes), F32),
        )
        return pl.pallas_call(
            functools.partial(kernel, M, S, depth * S),
            out_shape=shapes,
            in_specs=[pl.BlockSpec(memory_space=pltpu.HBM)] * 6,
            out_specs=[pl.BlockSpec(memory_space=pltpu.VMEM)] * 2,
            scratch_shapes=[
                pltpu.VMEM((2, 3 * rs, width), F32),
                pltpu.VMEM((2, 3 * rs, width), jnp.int32),
                pltpu.VMEM((rows, spokes), jnp.int32),
                pltpu.VMEM((3, 2, brick, spokes), F32),
                pltpu.VMEM((2 * REACH + 1, 2, brick, spokes), F32),
                pltpu.VMEM(((rs + 3) * spokes, width), jnp.bfloat16),
                pltpu.VMEM((S, 8, 128), F32),
                pltpu.VMEM((M, 8, 128), F32),
                pltpu.VMEM((2, rs, spokes), F32),
                pltpu.VMEM((2, rs, spokes), F32),
                pltpu.VMEM((2 * REACH + 2, brick, spokes), F32),
                pltpu.VMEM((2 * REACH + 1, brick, spokes), F32),
                pltpu.VMEM((2 * REACH + 1, brick, spokes), F32),
                dma((6,)),
                dma((4,)), dma((4,)),
                dma((2,)), dma((2,)),
                dma((2,)), dma((2,)),
                dma((2 * REACH,)), dma((2 * REACH,)),
                dma((S,)), dma((S,)),
                dma((M,)), dma((M,)),
                dma((targets,)), dma((S,)),
                dma((targets,)), dma((2,)),
            ],
            compiler_params=pltpu.CompilerParams(
                collective_id=0, has_side_effects=True, vmem_limit_bytes=63 * 1024 * 1024
            ),
            name="window",
        )(warm, volt, pattern, cells, temp, kind)

    return jax.shard_map(
        local,
        mesh=mesh,
        in_specs=(
            P(("magnet", "slab"), None),
            P(("magnet", "slab"), None),
            P(("magnet", "slab"), None),
            P("magnet", None),
            P("slab", "magnet", None),
            P("slab", "magnet", None),
        ),
        out_specs=(P(("magnet", "slab"), None), P("slab", "magnet", None)),
        check_vma=False,
    )
```

```python
import functools

import jax
import jax.numpy as jnp
from jax import lax
from jax.experimental import pallas as pl
from jax.experimental.pallas import tpu as pltpu
from jax.sharding import PartitionSpec as P

MESH = pl.DeviceIdType.MESH
F32 = jnp.float32
leak_diag = 0.25
contact_gain = 4.0
copper_factor = 3.0
sheet_slope = 0.5
heat_factor = 1.5
time_step = 0.03
conduct_table = (0.3, 1.0, 2.0, 0.6)
capacity_table = (1.0, 1.5, 2.0, 1.2)
diffusivity_derivative = 0.4
REACH = 3
GRAM = ((0, 0), (0, 1), (0, 2), (0, 3), (1, 1), (1, 2), (1, 3), (2, 2), (2, 3))


def two_sum(a, b):
    s = a + b
    t = s - a
    return s, (a - (s - t)) + (b - t)


def halves(a):
    c = a * 4097.0
    high = c - (c - a)
    return high, a - high


def two_prod(a, b, sa, sb):
    p = a * b
    return p, ((sa[0] * sb[0] - p) + sa[0] * sb[1] + sa[1] * sb[0]) + sa[1] * sb[1]


def pair_add(x, y):
    s, e = two_sum(x[0], y[0])
    return s, e + (x[1] + y[1])


def tree(items, add):
    while len(items) > 1:
        items = [add(*items[i : i + 2]) if i + 1 < len(items) else items[i] for i in range(0, len(items), 2)]
    return items[0]


def pair_mul(x, y):
    p, e = two_prod(x[0], y[0], halves(x[0]), halves(y[0]))
    return p, e + (x[0] * y[1] + x[1] * y[0])


def quadratic(coefs, gram):
    terms = []
    for (i, j), g in gram.items():
        c = two_prod(coefs[i], coefs[j], halves(coefs[i]), halves(coefs[j]))
        terms.append(pair_mul(c, g))
    s = tree(terms, pair_add)
    return s[0] + s[1]


def lookup(kind, table):
    out = jnp.zeros(kind.shape, F32)
    for i, value in enumerate(table):
        out = jnp.where(kind == float(i), value, out)
    return out


def fluxes(temps, conds, first, last):
    rows = temps[0].shape[0]
    face = {}
    for i in range(first - 1, last):
        face[i] = (conds[i] + conds[i + 1]) * (temps[i + 1] - temps[i])
    out = []
    for i in range(first, last):
        t, k = temps[i], conds[i]
        total = face[i] - face[i - 1]
        for axis, size in ((0, rows), (1, t.shape[1])):
            f = (k + pltpu.roll(k, 1, axis)) * (pltpu.roll(t, 1, axis) - t)
            total = total + (f - pltpu.roll(f, size - 1, axis))
        out.append(0.5 * total)
    return out


def kernel(
    M, S, shells,
    warm_in, volt_in, pat_in, map_in, temp_in, kind_in,
    pot_out, brick_out,
    sheet_f, sheet_i, kind_v, first_b, later_b, onehot, red1, red2, heat_own, heat_ext, heat_b, base_b, rate_b,
    border_f, border_i, cross_f, cross_i,
    border_send, border_recv, pass_send, pass_recv,
    local_sem, sheet_send, sheet_recv, len_send, len_recv, rad_send, rad_recv, late_send, late_recv,
    r1_send, r1_recv, r2_send, r2_recv, h_send, h_recv, e_send, e_recv,
):
    m = lax.axis_index("magnet")
    s = lax.axis_index("slab")
    rs, width = warm_in.shape
    rows, spokes = temp_in.shape[1], temp_in.shape[2]
    brick = rows + 16
    g = m * S + s
    target0 = max(0, S - 2 - REACH)
    heated = s >= target0

    own_rows = pl.ds(pl.multiple_of(s * rs, 8), rs)
    mid = pl.ds(rs, rs)
    bmid = pl.ds(8, rows)
    zf = jnp.zeros((2, rs, width), F32)
    zi = jnp.zeros((2, rs, width), jnp.int32)
    for lo in (0, 2 * rs):
        sheet_f[:, lo : lo + rs, :] = zf
        sheet_i[:, lo : lo + rs, :] = zi
    ghost_t = jnp.zeros((brick, spokes), F32)
    ghost_k = jnp.full((brick, spokes), -1.0, F32)
    for buf in (first_b, later_b):
        for i in range(buf.shape[0]):
            buf[i, 0] = ghost_t
            buf[i, 1] = ghost_k
    for i in range(heat_b.shape[0]):
        heat_b[i] = ghost_t
    local = [
        pltpu.make_async_copy(kind_in.at[0], kind_v, local_sem.at[0]),
        pltpu.make_async_copy(temp_in.at[0], first_b.at[1, 0, bmid, :], local_sem.at[1]),
        pltpu.make_async_copy(warm_in, sheet_f.at[0, mid, :], local_sem.at[2]),
        pltpu.make_async_copy(volt_in, sheet_f.at[1, mid, :], local_sem.at[3]),
        pltpu.make_async_copy(pat_in, sheet_i.at[0, mid, :], local_sem.at[4]),
        pltpu.make_async_copy(map_in.at[own_rows, :], sheet_i.at[1, mid, :], local_sem.at[5]),
    ]
    for c in local:
        c.start()

    barrier = pltpu.get_barrier_semaphore()

    def greet(who):
        pl.semaphore_signal(barrier, inc=1, device_id=who, device_id_type=MESH)

    for d in range(1, S):
        greet((m, lax.rem(s + d, S)))
    for d in range(1, M):
        greet((lax.rem(m + d, M), s))
    middle = S // 2 - 1
    at_top, at_end = (s <= 1) & (m > 0), (s >= S - 2) & (m < M - 1)
    is_middle = (s == middle) & (m < M - 1)
    pl.when(at_top)(lambda: greet((m - 1, middle)))

    @pl.when(is_middle)
    def _():
        greet((m + 1, 0))
        greet((m + 1, 1))

    extra = jnp.where(at_top, 1, 0) + jnp.where(is_middle, 2, 0)
    for c in local:
        c.wait()
    first_b[1, 1, bmid, :] = kind_v[...].astype(F32)
    pl.semaphore_wait(barrier, S + M - 2 + extra)

    pending = []

    def sent(copies):
        for pred, c in copies:
            if pred is None:
                c.wait_send()
            else:
                pl.when(pred)(c.wait_send)

    def remote(pred, src, dst, send, recv, who):
        nonlocal pending
        c = pltpu.make_async_remote_copy(
            src_ref=src, dst_ref=dst, send_sem=send, recv_sem=recv, device_id=who, device_id_type=MESH
        )
        if pred is None:
            c.start()
        else:
            pl.when(pred)(c.start)
        pending.append((pred, c))

    def arrived(pred, src, dst, send, recv):
        c = pltpu.make_async_remote_copy(
            src_ref=src, dst_ref=dst, send_sem=send, recv_sem=recv, device_id=(m, s), device_id_type=MESH
        )
        if pred is None:
            c.wait_recv()
        else:
            pl.when(pred)(c.wait_recv)

    has_prev, has_next = s > 0, s < S - 1
    prev, nxt = (m, s - 1), (m, s + 1)
    before, after = pl.ds(0, rs), pl.ds(2 * rs, rs)
    for k, buf in enumerate((sheet_f, sheet_i)):
        remote(has_next, buf.at[:, mid, :], buf.at[:, before, :], sheet_send.at[2 * k], sheet_recv.at[2 * k], nxt)
        remote(has_prev, buf.at[:, mid, :], buf.at[:, after, :], sheet_send.at[2 * k + 1], sheet_recv.at[2 * k + 1], prev)
    border_at = pl.ds(pl.multiple_of(jnp.where(at_top, 2 + s, jnp.where(at_end, s - (S - 2), 0)) * rs, 8), rs)
    border_slot = jnp.where(at_top, 2 + s, jnp.where(at_end, s - (S - 2), 0))
    border_to = (jnp.where(at_top, m - 1, m), middle)
    for k, (buf, border) in enumerate(((sheet_f, border_f), (sheet_i, border_i))):
        remote(
            at_top | at_end, buf.at[:, mid, :], border.at[:, border_at, :],
            border_send.at[k], border_recv.at[k, border_slot], border_to,
        )
    layer = first_b.at[1]
    top_rows, end_rows = pl.ds(8, 8), pl.ds(rows, 8)
    top_halo, end_halo = pl.ds(0, 8), pl.ds(rows + 8, 8)
    remote(m < M - 1, layer.at[:, end_rows, :], layer.at[:, top_halo, :], len_send.at[0], len_recv.at[0], (m + 1, s))
    remote(m > 0, layer.at[:, top_rows, :], layer.at[:, end_halo, :], len_send.at[1], len_recv.at[1], (m - 1, s))

    lane_id = lax.broadcasted_iota(jnp.int32, (spokes, width), 0)
    base_cell = (shells - 2) * spokes
    cell_own = sheet_i[1, rs : 2 * rs, :] - base_cell
    upper_own = cell_own >= spokes
    col_own = jnp.where(upper_own, cell_own - spokes, cell_own)

    def put_onehot(at, row):
        onehot[at * spokes : (at + 1) * spokes, :] = jnp.where(lane_id == row, 1.0, 0.0).astype(jnp.bfloat16)

    for i in range(rs):
        put_onehot(i, col_own[i : i + 1, :])

    arrived(m > 0, layer.at[:, end_rows, :], layer.at[:, top_halo, :], len_send.at[0], len_recv.at[0])
    arrived(m < M - 1, layer.at[:, top_rows, :], layer.at[:, end_halo, :], len_send.at[1], len_recv.at[1])
    remote(s < S - 1, layer, first_b.at[0], rad_send.at[0], rad_recv.at[0], (m, s + 1))
    remote(s > 0, layer, first_b.at[2], rad_send.at[1], rad_recv.at[1], (m, s - 1))

    for k, buf in enumerate((sheet_f, sheet_i)):
        arrived(has_prev, buf.at[:, mid, :], buf.at[:, before, :], sheet_send.at[2 * k], sheet_recv.at[2 * k])
        arrived(has_next, buf.at[:, mid, :], buf.at[:, after, :], sheet_send.at[2 * k + 1], sheet_recv.at[2 * k + 1])

    def field_steps(n, first_row):
        row_id = lax.broadcasted_iota(jnp.int32, (n, width), 0) + first_row
        col_id = lax.broadcasted_iota(jnp.int32, (n, width), 1)
        valid = (row_id >= 0) & (row_id < M * S * rs)
        left_edge, right_edge = col_id == 0, col_id == width - 1

        def from_up(v):
            return pltpu.roll(v, 1, 0)

        def from_down(v):
            return pltpu.roll(v, n - 1, 0)

        def from_left(v):
            return jnp.where(left_edge, 0.0, pltpu.roll(v, 1, 1))

        def from_right(v):
            return jnp.where(right_edge, 0.0, pltpu.roll(v, width - 1, 1))

        return valid, (from_up, from_down, from_left, from_right)

    def krylov(warm, volt, pattern, first_row, count):
        valid, sides = field_steps(warm.shape[0], first_row)
        sigma = jnp.where(valid, jnp.where(pattern == 1, copper_factor, 1.0) / (1.0 + sheet_slope * warm), 0.0)
        coeffs = [0.5 * (sigma + side(sigma)) for side in sides]
        contact = jnp.where(pattern == 2, contact_gain, 0.0)
        diagonal = leak_diag + contact + coeffs[0] + coeffs[1] + coeffs[2] + coeffs[3]
        basis = [jnp.where(valid, contact * volt, 0.0)]
        for _ in range(count - 1):
            v = basis[-1]
            out = diagonal * v
            for c, side in zip(coeffs, sides):
                out = out - c * side(v)
            basis.append(jnp.where(valid, out, 0.0))
        return coeffs, sides, basis

    sub = lax.broadcasted_iota(jnp.int32, (8, 128), 0)
    lane = lax.broadcasted_iota(jnp.int32, (8, 128), 1)
    is_low = (lane & 32) != 0

    def folded(a, b, step):
        first = (sub & step) == 0
        near = jnp.where(first, a, b)
        far = jnp.where(first, pltpu.roll(a, 8 - step, 0), pltpu.roll(b, step, 0))
        return near, far

    def fold_lanes(p):
        for step in (64, 32):
            p = pair_add(p, (pltpu.roll(p[0], step, 1), pltpu.roll(p[1], step, 1)))
        return p

    def unpacked(tile):
        return tile, pltpu.roll(tile, 96, 1)

    def packed(p):
        return jnp.where(is_low, pltpu.roll(p[1], 32, 1), p[0])

    def gram_tile(basis, lo, hi):
        cells = [(r, c) for r in range(lo, hi, 8) for c in range(0, width, 128)]
        chunks = [[v[r : r + 8, c : c + 128] for r, c in cells] for v in basis]
        split = [[halves(v) for v in field] for field in chunks]
        pairs = []
        for i, j in GRAM:
            terms = [two_prod(a, b, sa, sb) for a, b, sa, sb in zip(chunks[i], chunks[j], split[i], split[j])]
            pairs.append(tree(terms, pair_add))
        eight, ninth = pairs[:8], pairs[8]
        for step in (4, 2, 1):
            merged = []
            for a, b in zip(eight[:step], eight[step:]):
                parts = [folded(x, y, step) for x, y in zip(a, b)]
                merged.append(pair_add((parts[0][0], parts[1][0]), (parts[0][1], parts[1][1])))
            eight = merged
        eight, ninth = fold_lanes(eight[0]), fold_lanes(ninth)
        both = [jnp.where(lane < 64, a, b) for a, b in zip(eight, ninth)]
        return jnp.where(is_low, both[1], both[0])

    _, _, basis = krylov(sheet_f[0], sheet_f[1], sheet_i[0], (g - 1) * rs, 4)
    cross_up, cross_down = (s == 0) & (m > 0), (s == S - 1) & (m < M - 1)
    is_cross = cross_up | cross_down
    red1[s] = jnp.where(is_cross, 0.0, gram_tile(basis, rs, 2 * rs))

    @pl.when(is_middle)
    def _():
        for k, (buf, border) in enumerate(((sheet_f, border_f), (sheet_i, border_i))):
            for slot in range(4):
                arrived(None, buf.at[:, mid, :], border.at[:, slot * rs : (slot + 1) * rs, :], border_send.at[k], border_recv.at[k, slot])

    for k, (border, cross) in enumerate(((border_f, cross_f), (border_i, cross_i))):
        remote(is_middle, border.at[:, 2 * rs : 3 * rs, :], cross, pass_send.at[k, 0], pass_recv.at[k], (m, S - 1))
        remote(is_middle, border.at[:, rs : 2 * rs, :], cross, pass_send.at[k, 1], pass_recv.at[k], (m + 1, 0))

    @pl.when(is_middle)
    def _():
        _, _, fields = krylov(border_f[0], border_f[1], border_i[0], (m * S + S - 2) * rs, 4)
        tile = gram_tile(fields, rs, 3 * rs)
        red1[s] = packed(pair_add(unpacked(red1[s]), unpacked(tile)))

    for d in range(1, S):
        remote(None, red1.at[s], red1.at[s], r1_send.at[d], r1_recv.at[d], (m, lax.rem(s + d, S)))

    arrived(s > 0, layer, first_b.at[0], rad_send.at[0], rad_recv.at[0])
    arrived(s < S - 1, layer, first_b.at[2], rad_send.at[1], rad_recv.at[1])

    def conduct(temps, kinds):
        return [lookup(k, conduct_table) * (1.0 + diffusivity_derivative * t) for t, k in zip(temps, kinds)]

    def rate(kind):
        return lookup(kind, tuple(time_step / c for c in capacity_table))

    temps = [first_b[i, 0] for i in range(3)]
    kinds = [first_b[i, 1] for i in range(3)]
    (flux,) = fluxes(temps, conduct(temps, kinds), 1, 2)
    later_b[REACH, 0] = temps[1] + rate(kinds[1]) * flux
    later_b[REACH, 1] = kinds[1]
    early, pending = pending, []
    def part(slot, d):
        if d == 1:
            return later_b.at[slot, 0]
        return later_b.at[slot, :, bmid, :] if d == REACH else later_b.at[slot]

    later_b[REACH - 1, 1] = kinds[0]
    later_b[REACH + 1, 1] = kinds[2]
    for d in range(1, REACH + 1):
        remote(s < S - d, part(REACH, d), part(REACH - d, d), late_send.at[2 * d - 2], late_recv.at[2 * d - 2], (m, s + d))
        remote(s >= d, part(REACH, d), part(REACH + d, d), late_send.at[2 * d - 1], late_recv.at[2 * d - 1], (m, s - d))
    late, pending = pending, []

    def pair_of(ref, i):
        return unpacked(ref[i])

    for d in range(1, S):
        src = lax.rem(s + S - d, S)
        arrived(None, red1.at[s], red1.at[src], r1_send.at[d], r1_recv.at[d])
    total = tree([pair_of(red1, i) for i in range(S)], pair_add)
    red2[m] = packed(total)
    for d in range(1, M):
        remote(None, red2.at[m], red2.at[m], r2_send.at[d], r2_recv.at[d], (lax.rem(m + d, M), s))
    for k, (border, cross) in enumerate(((border_f, cross_f), (border_i, cross_i))):
        arrived(is_cross, border.at[:, before, :], cross, pass_send.at[k, 0], pass_recv.at[k])

    @pl.when(cross_up)
    def _():
        sheet_f[:, before, :] = cross_f[...]
        sheet_i[:, before, :] = cross_i[...]

    @pl.when(cross_down)
    def _():
        sheet_f[:, after, :] = cross_f[...]
        sheet_i[:, after, :] = cross_i[...]

    coeffs, sides, basis = krylov(sheet_f[0], sheet_f[1], sheet_i[0], (g - 1) * rs, 3)

    before_string = s == 0

    def outer(a):
        return jnp.where(before_string, pltpu.roll(a[0:rs], 3, 0), a[2 * rs :])

    cell_ext = outer(sheet_i[1]) - base_cell
    cell_ext = jnp.clip(cell_ext, 0, 2 * spokes - 1)
    upper_ext = cell_ext >= spokes
    col_ext = jnp.where(upper_ext, cell_ext - spokes, cell_ext)
    for i in range(3):
        put_onehot(rs + i, col_ext[i : i + 1, :])

    for d in range(1, M):
        src = lax.rem(m + M - d, M)
        arrived(None, red2.at[m], red2.at[src], r2_send.at[d], r2_recv.at[d])
    high, low = tree([pair_of(red2, i) for i in range(M)], pair_add)
    def added(high, low, axes):
        grid = 1024.0 * jnp.max(jnp.abs(high), axis=axes, keepdims=True)
        coarse = (high + grid) - grid
        rest = jnp.sum((high - coarse) + low, axis=axes, keepdims=True)
        return two_sum(jnp.sum(coarse, axis=axes, keepdims=True), rest)

    in_eight, in_ninth = lane < 32, (lane >= 64) & (lane < 96)
    sums = added(jnp.where(in_eight, high, 0.0), jnp.where(in_eight, low, 0.0), 1)
    gram = {ij: (sums[0][n : n + 1], sums[1][n : n + 1]) for n, ij in enumerate(GRAM[:8])}
    gram[GRAM[8]] = added(jnp.where(in_ninth, high, 0.0), jnp.where(in_ninth, low, 0.0), (0, 1))

    def twice(x):
        return 2.0 * x[0], 2.0 * x[1]

    plain = {(i, j): gram[i, j] if i == j else twice(gram[i, j]) for i, j in GRAM if j < 3}
    with_a = {
        (0, 0): gram[0, 1],
        (0, 1): pair_add(gram[0, 2], gram[1, 1]),
        (1, 1): gram[1, 2],
        (0, 2): pair_add(gram[0, 3], gram[1, 2]),
        (1, 2): pair_add(gram[1, 3], gram[2, 2]),
        (2, 2): gram[2, 3],
    }

    def upto(table, n):
        return {ij: v for ij, v in table.items() if ij[1] < n}

    one = jnp.ones_like(gram[0, 0][0])
    norm0 = gram[0, 0][0]
    a0 = norm0 / gram[0, 1][0]
    norm1 = quadratic([one, -a0], upto(plain, 2))
    b1 = norm1 / norm0
    p1 = [1.0 + b1, -a0]
    a1 = norm1 / quadratic(p1, upto(with_a, 2))
    r2 = [one, -a0 - a1 * p1[0], -a1 * p1[1]]
    norm2 = quadratic(r2, plain)
    b2 = norm2 / norm1
    p2 = [r2[0] + b2 * p1[0], r2[1] + b2 * p1[1], r2[2]]
    a2 = norm2 / quadratic(p2, with_a)
    weights = [a0 + a1 * p1[0] + a2 * p2[0], a1 * p1[1] + a2 * p2[1], a2 * p2[2]]
    potential = weights[0] * basis[0] + weights[1] * basis[1] + weights[2] * basis[2]
    pot_out[...] = potential[rs : 2 * rs]

    joule = jnp.zeros_like(potential)
    for c, side in zip(coeffs, sides):
        drop = potential - side(potential)
        joule = joule + c * (drop * drop)
    joule = heat_factor * joule
    sub_id = lax.broadcasted_iota(jnp.int32, (rs, spokes), 0)

    def binned(power, upper, first, count):
        parts = []
        for value in (jnp.where(upper, 0.0, power), jnp.where(upper, power, 0.0)):
            for _ in range(2):
                part = value.astype(jnp.bfloat16).astype(F32)
                parts.append(part)
                value = value - part
        lhs = jnp.concatenate(parts, axis=0).astype(jnp.bfloat16)
        cols = onehot[first * spokes : (first + count) * spokes, :]
        out = lax.dot_general(lhs, cols, (((1,), (1,)), ((), ())), preferred_element_type=F32)
        heats = []
        for k in range(2):
            part = out[2 * k * rs : (2 * k + 1) * rs] + out[(2 * k + 1) * rs : (2 * k + 2) * rs]
            heat = jnp.zeros((rs, spokes), F32)
            for i in range(count):
                heat = jnp.where(sub_id == i, part[:, i * spokes : (i + 1) * spokes], heat)
            heats.append(heat)
        return heats

    lower, higher = binned(joule[rs : 2 * rs], upper_own, 0, rs)
    heat_own[0] = lower
    heat_own[1] = higher
    at = pl.ds(pl.multiple_of(8 + rs * s, 8), rs)

    def slots(t):
        return pl.ds(REACH + S - 2 - t, 2)

    mine, pending = pending, []
    for n, t in enumerate(range(target0, S)):
        remote(s != t, heat_own, heat_b.at[slots(t), at, :], h_send.at[n], h_recv.at[s], (m, t))
    ext_lower, ext_higher = binned(outer(joule), upper_ext, rs, 3)
    heat_ext[0] = jnp.where(before_string, pltpu.roll(ext_lower, rs - 3, 0), ext_lower)
    heat_ext[1] = jnp.where(before_string, pltpu.roll(ext_higher, rs - 3, 0), ext_higher)
    at_rim = (s == 0) | (s == S - 1)
    side_of = jnp.where(before_string, 0, 1)
    ext_at = pl.ds(pl.multiple_of(jnp.where(before_string, 0, rows + 8), 8), 8)
    for n, t in enumerate(range(target0, S)):
        remote(at_rim & (s != t), heat_ext, heat_b.at[slots(t), ext_at, :], e_send.at[n], e_recv.at[side_of], (m, t))

    @pl.when(heated)
    def _():
        slot = REACH + S - 2 - s
        heat_b[slot, at, :] = lower
        heat_b[slot + 1, at, :] = higher

        @pl.when(at_rim)
        def _():
            heat_b[slot, ext_at, :] = heat_ext[0]
            heat_b[slot + 1, ext_at, :] = heat_ext[1]

    for d in range(1, REACH + 1):
        arrived(s >= d, part(REACH, d), part(REACH - d, d), late_send.at[2 * d - 2], late_recv.at[2 * d - 2])
        arrived(s < S - d, part(REACH, d), part(REACH + d, d), late_send.at[2 * d - 1], late_recv.at[2 * d - 1])
    count = 2 * REACH + 1
    for i in range(count):
        kind = later_b[i, 1]
        base_b[i] = lookup(kind, conduct_table)
        rate_b[i] = rate(kind)
    sent(early + late + mine)
    pair = pl.ds(0, 2)
    for j in range(S):
        at_j = pl.ds(8 + rs * j, rs)
        arrived(heated & (s != j), heat_own, heat_b.at[pair, at_j, :], h_send.at[0], h_recv.at[j])
    arrived(heated & (s != 0), heat_ext, heat_b.at[pair, top_halo, :], e_send.at[0], e_recv.at[0])
    arrived(heated & (s != S - 1), heat_ext, heat_b.at[pair, end_halo, :], e_send.at[0], e_recv.at[1])

    count = 2 * REACH + 1
    temps = [later_b[i, 0] + rate_b[i] * heat_b[i] for i in range(count)]
    for step in range(1, REACH + 1):
        first, last = step, count - step
        near = range(first - 1, last + 1)
        conds = {i: base_b[i] * (1.0 + diffusivity_derivative * temps[i]) for i in near}
        for i, f in zip(range(first, last), fluxes(temps, conds, first, last)):
            temps[i] = temps[i] + rate_b[i] * (f + heat_b[i])
    brick_out[0] = temps[REACH][8 : 8 + rows]
    sent(pending)


def solution(mesh):
    M, S = mesh.shape["magnet"], mesh.shape["slab"]

    def local(warm, volt, pattern, cells, temp, kind):
        rs, width = warm.shape
        depth, rows, spokes = temp.shape
        brick = rows + 16
        dma = pltpu.SemaphoreType.DMA
        targets = REACH + 2
        shapes = (
            jax.ShapeDtypeStruct((rs, width), F32),
            jax.ShapeDtypeStruct((depth, rows, spokes), F32),
        )
        return pl.pallas_call(
            functools.partial(kernel, M, S, depth * S),
            out_shape=shapes,
            in_specs=[pl.BlockSpec(memory_space=pltpu.HBM)] * 6,
            out_specs=[pl.BlockSpec(memory_space=pltpu.VMEM)] * 2,
            scratch_shapes=[
                pltpu.VMEM((2, 3 * rs, width), F32),
                pltpu.VMEM((2, 3 * rs, width), jnp.int32),
                pltpu.VMEM((rows, spokes), jnp.int32),
                pltpu.VMEM((3, 2, brick, spokes), F32),
                pltpu.VMEM((2 * REACH + 1, 2, brick, spokes), F32),
                pltpu.VMEM(((rs + 3) * spokes, width), jnp.bfloat16),
                pltpu.VMEM((S, 8, 128), F32),
                pltpu.VMEM((M, 8, 128), F32),
                pltpu.VMEM((2, rs, spokes), F32),
                pltpu.VMEM((2, rs, spokes), F32),
                pltpu.VMEM((2 * REACH + 2, brick, spokes), F32),
                pltpu.VMEM((2 * REACH + 1, brick, spokes), F32),
                pltpu.VMEM((2 * REACH + 1, brick, spokes), F32),
                pltpu.VMEM((2, 4 * rs, width), F32),
                pltpu.VMEM((2, 4 * rs, width), jnp.int32),
                pltpu.VMEM((2, rs, width), F32),
                pltpu.VMEM((2, rs, width), jnp.int32),
                dma((2,)), dma((2, 4)),
                dma((2, 2)), dma((2,)),
                dma((6,)),
                dma((4,)), dma((4,)),
                dma((2,)), dma((2,)),
                dma((2,)), dma((2,)),
                dma((2 * REACH,)), dma((2 * REACH,)),
                dma((S,)), dma((S,)),
                dma((M,)), dma((M,)),
                dma((targets,)), dma((S,)),
                dma((targets,)), dma((2,)),
            ],
            compiler_params=pltpu.CompilerParams(
                collective_id=0, has_side_effects=True, vmem_limit_bytes=63 * 1024 * 1024
            ),
            name="window",
        )(warm, volt, pattern, cells, temp, kind)

    return jax.shard_map(
        local,
        mesh=mesh,
        in_specs=(
            P(("magnet", "slab"), None),
            P(("magnet", "slab"), None),
            P(("magnet", "slab"), None),
            P("magnet", None),
            P("slab", "magnet", None),
            P("slab", "magnet", None),
        ),
        out_specs=(P(("magnet", "slab"), None), P("slab", "magnet", None)),
        check_vma=False,
    )
```

```python
import functools

import jax
import jax.numpy as jnp
from jax import lax
from jax.experimental import pallas as pl
from jax.experimental.pallas import tpu as pltpu
from jax.sharding import PartitionSpec as P

MESH = pl.DeviceIdType.MESH
F32 = jnp.float32
leak_diag = 0.25
contact_gain = 4.0
copper_factor = 3.0
sheet_slope = 0.5
heat_factor = 1.5
time_step = 0.03
conduct_table = (0.3, 1.0, 2.0, 0.6)
capacity_table = (1.0, 1.5, 2.0, 1.2)
diffusivity_derivative = 0.4
REACH = 3
GRAM = ((0, 0), (0, 1), (0, 2), (0, 3), (1, 1), (1, 2), (1, 3), (2, 2), (2, 3))


def two_sum(a, b):
    s = a + b
    t = s - a
    return s, (a - (s - t)) + (b - t)


def halves(a):
    c = a * 4097.0
    high = c - (c - a)
    return high, a - high


def two_prod(a, b, sa, sb):
    p = a * b
    return p, ((sa[0] * sb[0] - p) + sa[0] * sb[1] + sa[1] * sb[0]) + sa[1] * sb[1]


def pair_add(x, y):
    s, e = two_sum(x[0], y[0])
    return s, e + (x[1] + y[1])


def tree(items, add):
    while len(items) > 1:
        items = [add(*items[i : i + 2]) if i + 1 < len(items) else items[i] for i in range(0, len(items), 2)]
    return items[0]


def pair_mul(x, y):
    p, e = two_prod(x[0], y[0], halves(x[0]), halves(y[0]))
    return p, e + (x[0] * y[1] + x[1] * y[0])


def quadratic(coefs, gram):
    terms = []
    for (i, j), g in gram.items():
        c = two_prod(coefs[i], coefs[j], halves(coefs[i]), halves(coefs[j]))
        terms.append(pair_mul(c, g))
    s = tree(terms, pair_add)
    return s[0] + s[1]


def lookup(kind, table):
    out = jnp.zeros(kind.shape, F32)
    for i, value in enumerate(table):
        out = jnp.where(kind == float(i), value, out)
    return out


def fluxes(temps, conds, first, last):
    rows = temps[0].shape[0]
    face = {}
    for i in range(first - 1, last):
        face[i] = (conds[i] + conds[i + 1]) * (temps[i + 1] - temps[i])
    out = []
    for i in range(first, last):
        t, k = temps[i], conds[i]
        total = face[i] - face[i - 1]
        for axis, size in ((0, rows), (1, t.shape[1])):
            f = (k + pltpu.roll(k, 1, axis)) * (pltpu.roll(t, 1, axis) - t)
            total = total + (f - pltpu.roll(f, size - 1, axis))
        out.append(0.5 * total)
    return out


def kernel(
    M, S, shells,
    warm_in, volt_in, pat_in, map_in, temp_in, kind_in,
    pot_out, brick_out,
    sheet, ints, kind_v, first_b, later_b, onehot, red1, red2, heat_own, heat_ext, heat_b, base_b, rate_b,
    border, cross,
    border_send, border_recv, pass_send, pass_recv,
    local_sem, sheet_send, sheet_recv, len_send, len_recv, rad_send, rad_recv, late_send, late_recv,
    r1_send, r1_recv, r2_send, r2_recv, h_send, h_recv, e_send, e_recv,
):
    m = lax.axis_index("magnet")
    s = lax.axis_index("slab")
    rs, width = warm_in.shape
    rows, spokes = temp_in.shape[1], temp_in.shape[2]
    brick = rows + 16
    g = m * S + s
    target0 = max(0, S - 2 - REACH)
    heated = s >= target0

    own_rows = pl.ds(pl.multiple_of(s * rs, 8), rs)
    mid = pl.ds(rs, rs)
    bmid = pl.ds(8, rows)
    for lo in (0, 2 * rs):
        sheet[:, lo : lo + rs, :] = jnp.zeros((4, rs, width), F32)
    ghost_t = jnp.zeros((brick, spokes), F32)
    ghost_k = jnp.full((brick, spokes), -1.0, F32)
    for buf in (first_b, later_b):
        for i in range(buf.shape[0]):
            buf[i, 0] = ghost_t
            buf[i, 1] = ghost_k
    for i in range(heat_b.shape[0]):
        heat_b[i] = ghost_t
    local = [
        pltpu.make_async_copy(kind_in.at[0], kind_v, local_sem.at[0]),
        pltpu.make_async_copy(temp_in.at[0], first_b.at[1, 0, bmid, :], local_sem.at[1]),
        pltpu.make_async_copy(warm_in, sheet.at[0, mid, :], local_sem.at[2]),
        pltpu.make_async_copy(volt_in, sheet.at[1, mid, :], local_sem.at[3]),
        pltpu.make_async_copy(pat_in, ints.at[0], local_sem.at[4]),
        pltpu.make_async_copy(map_in.at[own_rows, :], ints.at[1], local_sem.at[5]),
    ]
    for c in local:
        c.start()

    barrier = pltpu.get_barrier_semaphore()

    def greet(who):
        pl.semaphore_signal(barrier, inc=1, device_id=who, device_id_type=MESH)

    for d in range(1, S):
        greet((m, lax.rem(s + d, S)))
    for d in range(1, M):
        greet((lax.rem(m + d, M), s))
    middle = S // 2 - 1
    at_top, at_end = (s <= 1) & (m > 0), (s >= S - 2) & (m < M - 1)
    is_middle = (s == middle) & (m < M - 1)
    pl.when(at_top)(lambda: greet((m - 1, middle)))

    @pl.when(is_middle)
    def _():
        greet((m + 1, 0))
        greet((m + 1, 1))

    extra = jnp.where(at_top, 1, 0) + jnp.where(is_middle, 2, 0)
    for c in local:
        c.wait()
    sheet[2:4, rs : 2 * rs, :] = ints[...].astype(F32)
    first_b[1, 1, bmid, :] = kind_v[...].astype(F32)
    pl.semaphore_wait(barrier, S + M - 2 + extra)

    pending = []

    def sent(copies):
        for pred, c in copies:
            if pred is None:
                c.wait_send()
            else:
                pl.when(pred)(c.wait_send)

    def remote(pred, src, dst, send, recv, who):
        nonlocal pending
        c = pltpu.make_async_remote_copy(
            src_ref=src, dst_ref=dst, send_sem=send, recv_sem=recv, device_id=who, device_id_type=MESH
        )
        if pred is None:
            c.start()
        else:
            pl.when(pred)(c.start)
        pending.append((pred, c))

    def arrived(pred, src, dst, send, recv):
        c = pltpu.make_async_remote_copy(
            src_ref=src, dst_ref=dst, send_sem=send, recv_sem=recv, device_id=(m, s), device_id_type=MESH
        )
        if pred is None:
            c.wait_recv()
        else:
            pl.when(pred)(c.wait_recv)

    has_prev, has_next = s > 0, s < S - 1
    prev, nxt = (m, s - 1), (m, s + 1)
    before, after = pl.ds(0, rs), pl.ds(2 * rs, rs)
    remote(has_next, sheet.at[:, mid, :], sheet.at[:, before, :], sheet_send.at[0], sheet_recv.at[0], nxt)
    remote(has_prev, sheet.at[:, mid, :], sheet.at[:, after, :], sheet_send.at[1], sheet_recv.at[1], prev)
    border_at = pl.ds(pl.multiple_of(jnp.where(at_top, 2 + s, jnp.where(at_end, s - (S - 2), 0)) * rs, 8), rs)
    border_slot = jnp.where(at_top, 2 + s, jnp.where(at_end, s - (S - 2), 0))
    border_to = (jnp.where(at_top, m - 1, m), middle)
    remote(
        at_top | at_end, sheet.at[:, mid, :], border.at[:, border_at, :],
        border_send.at[0], border_recv.at[border_slot], border_to,
    )
    layer = first_b.at[1]
    top_rows, end_rows = pl.ds(8, 8), pl.ds(rows, 8)
    top_halo, end_halo = pl.ds(0, 8), pl.ds(rows + 8, 8)
    remote(m < M - 1, layer.at[:, end_rows, :], layer.at[:, top_halo, :], len_send.at[0], len_recv.at[0], (m + 1, s))
    remote(m > 0, layer.at[:, top_rows, :], layer.at[:, end_halo, :], len_send.at[1], len_recv.at[1], (m - 1, s))

    lane_id = lax.broadcasted_iota(jnp.int32, (spokes, width), 0)
    base_cell = (shells - 2) * spokes
    cell_own = ints[1] - base_cell
    upper_own = cell_own >= spokes
    col_own = jnp.where(upper_own, cell_own - spokes, cell_own)

    def put_onehot(at, row):
        onehot[at * spokes : (at + 1) * spokes, :] = jnp.where(lane_id == row, 1.0, 0.0).astype(jnp.bfloat16)

    for i in range(rs):
        put_onehot(i, col_own[i : i + 1, :])

    arrived(has_prev, sheet.at[:, mid, :], sheet.at[:, before, :], sheet_send.at[0], sheet_recv.at[0])
    arrived(has_next, sheet.at[:, mid, :], sheet.at[:, after, :], sheet_send.at[1], sheet_recv.at[1])

    def field_steps(n, first_row):
        row_id = lax.broadcasted_iota(jnp.int32, (n, width), 0) + first_row
        col_id = lax.broadcasted_iota(jnp.int32, (n, width), 1)
        valid = (row_id >= 0) & (row_id < M * S * rs)
        left_edge, right_edge = col_id == 0, col_id == width - 1

        def from_up(v):
            return pltpu.roll(v, 1, 0)

        def from_down(v):
            return pltpu.roll(v, n - 1, 0)

        def from_left(v):
            return jnp.where(left_edge, 0.0, pltpu.roll(v, 1, 1))

        def from_right(v):
            return jnp.where(right_edge, 0.0, pltpu.roll(v, width - 1, 1))

        return valid, (from_up, from_down, from_left, from_right)

    def krylov(warm, volt, pattern, first_row, count):
        valid, sides = field_steps(warm.shape[0], first_row)
        sigma = jnp.where(valid, jnp.where(pattern == 1.0, copper_factor, 1.0) / (1.0 + sheet_slope * warm), 0.0)
        coeffs = [0.5 * (sigma + side(sigma)) for side in sides]
        contact = jnp.where(pattern == 2.0, contact_gain, 0.0)
        diagonal = leak_diag + contact + coeffs[0] + coeffs[1] + coeffs[2] + coeffs[3]
        basis = [jnp.where(valid, contact * volt, 0.0)]
        for _ in range(count - 1):
            v = basis[-1]
            out = diagonal * v
            for c, side in zip(coeffs, sides):
                out = out - c * side(v)
            basis.append(jnp.where(valid, out, 0.0))
        return coeffs, sides, basis

    sub = lax.broadcasted_iota(jnp.int32, (8, 128), 0)
    lane = lax.broadcasted_iota(jnp.int32, (8, 128), 1)
    is_low = (lane & 32) != 0

    def folded(a, b, step):
        first = (sub & step) == 0
        near = jnp.where(first, a, b)
        far = jnp.where(first, pltpu.roll(a, 8 - step, 0), pltpu.roll(b, step, 0))
        return near, far

    def fold_lanes(p):
        for step in (64, 32):
            p = pair_add(p, (pltpu.roll(p[0], step, 1), pltpu.roll(p[1], step, 1)))
        return p

    def unpacked(tile):
        return tile, pltpu.roll(tile, 96, 1)

    def packed(p):
        return jnp.where(is_low, pltpu.roll(p[1], 32, 1), p[0])

    def gram_tile(basis, lo, hi):
        cells = [(r, c) for r in range(lo, hi, 8) for c in range(0, width, 128)]
        chunks = [[v[r : r + 8, c : c + 128] for r, c in cells] for v in basis]
        split = [[halves(v) for v in field] for field in chunks]
        pairs = []
        for i, j in GRAM:
            terms = [two_prod(a, b, sa, sb) for a, b, sa, sb in zip(chunks[i], chunks[j], split[i], split[j])]
            pairs.append(tree(terms, pair_add))
        eight, ninth = pairs[:8], pairs[8]
        for step in (4, 2, 1):
            merged = []
            for a, b in zip(eight[:step], eight[step:]):
                parts = [folded(x, y, step) for x, y in zip(a, b)]
                merged.append(pair_add((parts[0][0], parts[1][0]), (parts[0][1], parts[1][1])))
            eight = merged
        eight, ninth = fold_lanes(eight[0]), fold_lanes(ninth)
        both = [jnp.where(lane < 64, a, b) for a, b in zip(eight, ninth)]
        return jnp.where(is_low, both[1], both[0])

    _, _, basis = krylov(sheet[0], sheet[1], sheet[2], (g - 1) * rs, 4)
    cross_up, cross_down = (s == 0) & (m > 0), (s == S - 1) & (m < M - 1)
    is_cross = cross_up | cross_down
    red1[s] = jnp.where(is_cross, 0.0, gram_tile(basis, rs, 2 * rs))

    @pl.when(is_middle)
    def _():
        for slot in range(4):
            arrived(None, sheet.at[:, mid, :], border.at[:, slot * rs : (slot + 1) * rs, :], border_send.at[0], border_recv.at[slot])

    remote(is_middle, border.at[:, 2 * rs : 3 * rs, :], cross, pass_send.at[0], pass_recv.at[0], (m, S - 1))
    remote(is_middle, border.at[:, rs : 2 * rs, :], cross, pass_send.at[1], pass_recv.at[0], (m + 1, 0))

    @pl.when(is_middle)
    def _():
        _, _, fields = krylov(border[0], border[1], border[2], (m * S + S - 2) * rs, 4)
        tile = gram_tile(fields, rs, 3 * rs)
        red1[s] = packed(pair_add(unpacked(red1[s]), unpacked(tile)))

    for d in range(1, S):
        remote(None, red1.at[s], red1.at[s], r1_send.at[d], r1_recv.at[d], (m, lax.rem(s + d, S)))

    arrived(m > 0, layer.at[:, end_rows, :], layer.at[:, top_halo, :], len_send.at[0], len_recv.at[0])
    arrived(m < M - 1, layer.at[:, top_rows, :], layer.at[:, end_halo, :], len_send.at[1], len_recv.at[1])
    remote(s < S - 1, layer, first_b.at[0], rad_send.at[0], rad_recv.at[0], (m, s + 1))
    remote(s > 0, layer, first_b.at[2], rad_send.at[1], rad_recv.at[1], (m, s - 1))

    def pair_of(ref, i):
        return unpacked(ref[i])

    for d in range(1, S):
        src = lax.rem(s + S - d, S)
        arrived(None, red1.at[s], red1.at[src], r1_send.at[d], r1_recv.at[d])
    total = tree([pair_of(red1, i) for i in range(S)], pair_add)
    red2[m] = packed(total)
    for d in range(1, M):
        remote(None, red2.at[m], red2.at[m], r2_send.at[d], r2_recv.at[d], (lax.rem(m + d, M), s))
    arrived(s > 0, layer, first_b.at[0], rad_send.at[0], rad_recv.at[0])
    arrived(s < S - 1, layer, first_b.at[2], rad_send.at[1], rad_recv.at[1])

    def conduct(temps, kinds):
        return [lookup(k, conduct_table) * (1.0 + diffusivity_derivative * t) for t, k in zip(temps, kinds)]

    def rate(kind):
        return lookup(kind, tuple(time_step / c for c in capacity_table))

    temps = [first_b[i, 0] for i in range(3)]
    kinds = [first_b[i, 1] for i in range(3)]
    (flux,) = fluxes(temps, conduct(temps, kinds), 1, 2)
    later_b[REACH, 0] = temps[1] + rate(kinds[1]) * flux
    later_b[REACH, 1] = kinds[1]
    early, pending = pending, []
    def part(slot, d):
        if d == 1:
            return later_b.at[slot, 0]
        return later_b.at[slot, :, bmid, :] if d == REACH else later_b.at[slot]

    later_b[REACH - 1, 1] = kinds[0]
    later_b[REACH + 1, 1] = kinds[2]
    for d in range(1, REACH + 1):
        remote(s < S - d, part(REACH, d), part(REACH - d, d), late_send.at[2 * d - 2], late_recv.at[2 * d - 2], (m, s + d))
        remote(s >= d, part(REACH, d), part(REACH + d, d), late_send.at[2 * d - 1], late_recv.at[2 * d - 1], (m, s - d))
    late, pending = pending, []

    arrived(is_cross, border.at[:, before, :], cross, pass_send.at[0], pass_recv.at[0])

    @pl.when(cross_up)
    def _():
        sheet[:, before, :] = cross[...]

    @pl.when(cross_down)
    def _():
        sheet[:, after, :] = cross[...]

    coeffs, sides, basis = krylov(sheet[0], sheet[1], sheet[2], (g - 1) * rs, 3)

    before_string = s == 0

    def outer(a):
        return jnp.where(before_string, pltpu.roll(a[0:rs], 3, 0), a[2 * rs :])

    cell_ext = outer(sheet[3]).astype(jnp.int32) - base_cell
    cell_ext = jnp.clip(cell_ext, 0, 2 * spokes - 1)
    upper_ext = cell_ext >= spokes
    col_ext = jnp.where(upper_ext, cell_ext - spokes, cell_ext)
    for i in range(3):
        put_onehot(rs + i, col_ext[i : i + 1, :])

    for d in range(1, M):
        src = lax.rem(m + M - d, M)
        arrived(None, red2.at[m], red2.at[src], r2_send.at[d], r2_recv.at[d])
    high, low = tree([pair_of(red2, i) for i in range(M)], pair_add)
    def added(high, low, axes):
        grid = 1024.0 * jnp.max(jnp.abs(high), axis=axes, keepdims=True)
        coarse = (high + grid) - grid
        rest = jnp.sum((high - coarse) + low, axis=axes, keepdims=True)
        return two_sum(jnp.sum(coarse, axis=axes, keepdims=True), rest)

    in_eight, in_ninth = lane < 32, (lane >= 64) & (lane < 96)
    sums = added(jnp.where(in_eight, high, 0.0), jnp.where(in_eight, low, 0.0), 1)
    gram = {ij: (sums[0][n : n + 1], sums[1][n : n + 1]) for n, ij in enumerate(GRAM[:8])}
    gram[GRAM[8]] = added(jnp.where(in_ninth, high, 0.0), jnp.where(in_ninth, low, 0.0), (0, 1))

    def twice(x):
        return 2.0 * x[0], 2.0 * x[1]

    plain = {(i, j): gram[i, j] if i == j else twice(gram[i, j]) for i, j in GRAM if j < 3}
    with_a = {
        (0, 0): gram[0, 1],
        (0, 1): pair_add(gram[0, 2], gram[1, 1]),
        (1, 1): gram[1, 2],
        (0, 2): pair_add(gram[0, 3], gram[1, 2]),
        (1, 2): pair_add(gram[1, 3], gram[2, 2]),
        (2, 2): gram[2, 3],
    }

    def upto(table, n):
        return {ij: v for ij, v in table.items() if ij[1] < n}

    one = jnp.ones_like(gram[0, 0][0])
    norm0 = gram[0, 0][0]
    a0 = norm0 / gram[0, 1][0]
    norm1 = quadratic([one, -a0], upto(plain, 2))
    b1 = norm1 / norm0
    p1 = [1.0 + b1, -a0]
    a1 = norm1 / quadratic(p1, upto(with_a, 2))
    r2 = [one, -a0 - a1 * p1[0], -a1 * p1[1]]
    norm2 = quadratic(r2, plain)
    b2 = norm2 / norm1
    p2 = [r2[0] + b2 * p1[0], r2[1] + b2 * p1[1], r2[2]]
    a2 = norm2 / quadratic(p2, with_a)
    weights = [a0 + a1 * p1[0] + a2 * p2[0], a1 * p1[1] + a2 * p2[1], a2 * p2[2]]
    potential = weights[0] * basis[0] + weights[1] * basis[1] + weights[2] * basis[2]
    pot_out[...] = potential[rs : 2 * rs]

    joule = jnp.zeros_like(potential)
    for c, side in zip(coeffs, sides):
        drop = potential - side(potential)
        joule = joule + c * (drop * drop)
    joule = heat_factor * joule
    sub_id = lax.broadcasted_iota(jnp.int32, (rs, spokes), 0)

    def binned(power, upper, first, count):
        parts = []
        for value in (jnp.where(upper, 0.0, power), jnp.where(upper, power, 0.0)):
            for _ in range(2):
                part = value.astype(jnp.bfloat16).astype(F32)
                parts.append(part)
                value = value - part
        lhs = jnp.concatenate(parts, axis=0).astype(jnp.bfloat16)
        cols = onehot[first * spokes : (first + count) * spokes, :]
        out = lax.dot_general(lhs, cols, (((1,), (1,)), ((), ())), preferred_element_type=F32)
        heats = []
        for k in range(2):
            part = out[2 * k * rs : (2 * k + 1) * rs] + out[(2 * k + 1) * rs : (2 * k + 2) * rs]
            heat = jnp.zeros((rs, spokes), F32)
            for i in range(count):
                heat = jnp.where(sub_id == i, part[:, i * spokes : (i + 1) * spokes], heat)
            heats.append(heat)
        return heats

    lower, higher = binned(joule[rs : 2 * rs], upper_own, 0, rs)
    heat_own[0] = lower
    heat_own[1] = higher
    at = pl.ds(pl.multiple_of(8 + rs * s, 8), rs)

    def slots(t):
        return pl.ds(REACH + S - 2 - t, 2)

    mine, pending = pending, []
    for n, t in enumerate(range(target0, S)):
        remote(s != t, heat_own, heat_b.at[slots(t), at, :], h_send.at[n], h_recv.at[s], (m, t))
    ext_lower, ext_higher = binned(outer(joule), upper_ext, rs, 3)
    heat_ext[0] = jnp.where(before_string, pltpu.roll(ext_lower, rs - 3, 0), ext_lower)
    heat_ext[1] = jnp.where(before_string, pltpu.roll(ext_higher, rs - 3, 0), ext_higher)
    at_rim = (s == 0) | (s == S - 1)
    side_of = jnp.where(before_string, 0, 1)
    ext_at = pl.ds(pl.multiple_of(jnp.where(before_string, 0, rows + 8), 8), 8)
    for n, t in enumerate(range(target0, S)):
        remote(at_rim & (s != t), heat_ext, heat_b.at[slots(t), ext_at, :], e_send.at[n], e_recv.at[side_of], (m, t))

    @pl.when(heated)
    def _():
        slot = REACH + S - 2 - s
        heat_b[slot, at, :] = lower
        heat_b[slot + 1, at, :] = higher

        @pl.when(at_rim)
        def _():
            heat_b[slot, ext_at, :] = heat_ext[0]
            heat_b[slot + 1, ext_at, :] = heat_ext[1]

    for d in range(1, REACH + 1):
        arrived(s >= d, part(REACH, d), part(REACH - d, d), late_send.at[2 * d - 2], late_recv.at[2 * d - 2])
        arrived(s < S - d, part(REACH, d), part(REACH + d, d), late_send.at[2 * d - 1], late_recv.at[2 * d - 1])
    count = 2 * REACH + 1
    for i in range(count):
        kind = later_b[i, 1]
        base_b[i] = lookup(kind, conduct_table)
        rate_b[i] = rate(kind)
    sent(early + late + mine)
    pair = pl.ds(0, 2)
    for j in range(S):
        at_j = pl.ds(8 + rs * j, rs)
        arrived(heated & (s != j), heat_own, heat_b.at[pair, at_j, :], h_send.at[0], h_recv.at[j])
    arrived(heated & (s != 0), heat_ext, heat_b.at[pair, top_halo, :], e_send.at[0], e_recv.at[0])
    arrived(heated & (s != S - 1), heat_ext, heat_b.at[pair, end_halo, :], e_send.at[0], e_recv.at[1])

    count = 2 * REACH + 1
    temps = [later_b[i, 0] + rate_b[i] * heat_b[i] for i in range(count)]
    for step in range(1, REACH + 1):
        first, last = step, count - step
        near = range(first - 1, last + 1)
        conds = {i: base_b[i] * (1.0 + diffusivity_derivative * temps[i]) for i in near}
        for i, f in zip(range(first, last), fluxes(temps, conds, first, last)):
            temps[i] = temps[i] + rate_b[i] * (f + heat_b[i])
    brick_out[0] = temps[REACH][8 : 8 + rows]
    sent(pending)


def solution(mesh):
    M, S = mesh.shape["magnet"], mesh.shape["slab"]

    def local(warm, volt, pattern, cells, temp, kind):
        rs, width = warm.shape
        depth, rows, spokes = temp.shape
        brick = rows + 16
        dma = pltpu.SemaphoreType.DMA
        targets = REACH + 2
        shapes = (
            jax.ShapeDtypeStruct((rs, width), F32),
            jax.ShapeDtypeStruct((depth, rows, spokes), F32),
        )
        return pl.pallas_call(
            functools.partial(kernel, M, S, depth * S),
            out_shape=shapes,
            in_specs=[pl.BlockSpec(memory_space=pltpu.HBM)] * 6,
            out_specs=[pl.BlockSpec(memory_space=pltpu.VMEM)] * 2,
            scratch_shapes=[
                pltpu.VMEM((4, 3 * rs, width), F32),
                pltpu.VMEM((2, rs, width), jnp.int32),
                pltpu.VMEM((rows, spokes), jnp.int32),
                pltpu.VMEM((3, 2, brick, spokes), F32),
                pltpu.VMEM((2 * REACH + 1, 2, brick, spokes), F32),
                pltpu.VMEM(((rs + 3) * spokes, width), jnp.bfloat16),
                pltpu.VMEM((S, 8, 128), F32),
                pltpu.VMEM((M, 8, 128), F32),
                pltpu.VMEM((2, rs, spokes), F32),
                pltpu.VMEM((2, rs, spokes), F32),
                pltpu.VMEM((2 * REACH + 2, brick, spokes), F32),
                pltpu.VMEM((2 * REACH + 1, brick, spokes), F32),
                pltpu.VMEM((2 * REACH + 1, brick, spokes), F32),
                pltpu.VMEM((4, 4 * rs, width), F32),
                pltpu.VMEM((4, rs, width), F32),
                dma((1,)), dma((4,)),
                dma((2,)), dma((1,)),
                dma((6,)),
                dma((2,)), dma((2,)),
                dma((2,)), dma((2,)),
                dma((2,)), dma((2,)),
                dma((2 * REACH,)), dma((2 * REACH,)),
                dma((S,)), dma((S,)),
                dma((M,)), dma((M,)),
                dma((targets,)), dma((S,)),
                dma((targets,)), dma((2,)),
            ],
            compiler_params=pltpu.CompilerParams(
                collective_id=0, has_side_effects=True, vmem_limit_bytes=63 * 1024 * 1024
            ),
            name="window",
        )(warm, volt, pattern, cells, temp, kind)

    return jax.shard_map(
        local,
        mesh=mesh,
        in_specs=(
            P(("magnet", "slab"), None),
            P(("magnet", "slab"), None),
            P(("magnet", "slab"), None),
            P("magnet", None),
            P("slab", "magnet", None),
            P("slab", "magnet", None),
        ),
        out_specs=(P(("magnet", "slab"), None), P("slab", "magnet", None)),
        check_vma=False,
    )
```

```python
import functools

import jax
import jax.numpy as jnp
from jax import lax
from jax.experimental import pallas as pl
from jax.experimental.pallas import tpu as pltpu
from jax.sharding import PartitionSpec as P

MESH = pl.DeviceIdType.MESH
F32 = jnp.float32
leak_diag = 0.25
contact_gain = 4.0
copper_factor = 3.0
sheet_slope = 0.5
heat_factor = 1.5
time_step = 0.03
conduct_table = (0.3, 1.0, 2.0, 0.6)
capacity_table = (1.0, 1.5, 2.0, 1.2)
diffusivity_derivative = 0.4
NEAR = 4
REACH = 3
GRAM = ((0, 0), (0, 1), (0, 2), (0, 3), (1, 1), (1, 2), (1, 3), (2, 2), (2, 3))


def two_sum(a, b):
    s = a + b
    t = s - a
    return s, (a - (s - t)) + (b - t)


def halves(a):
    c = a * 4097.0
    high = c - (c - a)
    return high, a - high


def two_prod(a, b, sa, sb):
    p = a * b
    return p, ((sa[0] * sb[0] - p) + sa[0] * sb[1] + sa[1] * sb[0]) + sa[1] * sb[1]


def pair_add(x, y):
    s, e = two_sum(x[0], y[0])
    return s, e + (x[1] + y[1])


def tree(items, add):
    while len(items) > 1:
        items = [add(*items[i : i + 2]) if i + 1 < len(items) else items[i] for i in range(0, len(items), 2)]
    return items[0]


def pair_mul(x, y):
    p, e = two_prod(x[0], y[0], halves(x[0]), halves(y[0]))
    return p, e + (x[0] * y[1] + x[1] * y[0])


def quadratic(coefs, gram):
    terms = []
    for (i, j), g in gram.items():
        c = two_prod(coefs[i], coefs[j], halves(coefs[i]), halves(coefs[j]))
        terms.append(pair_mul(c, g))
    s = tree(terms, pair_add)
    return s[0] + s[1]


def lookup(kind, table):
    out = jnp.zeros(kind.shape, F32)
    for i, value in enumerate(table):
        out = jnp.where(kind == float(i), value, out)
    return out


def fluxes(temps, conds, first, last):
    rows = temps[0].shape[0]
    face = {}
    for i in range(first - 1, last):
        face[i] = (conds[i] + conds[i + 1]) * (temps[i + 1] - temps[i])
    out = []
    for i in range(first, last):
        t, k = temps[i], conds[i]
        total = face[i] - face[i - 1]
        for axis, size in ((0, rows), (1, t.shape[1])):
            f = (k + pltpu.roll(k, 1, axis)) * (pltpu.roll(t, 1, axis) - t)
            total = total + (f - pltpu.roll(f, size - 1, axis))
        out.append(0.5 * total)
    return out


def kernel(
    M, S, shells,
    warm_in, volt_in, pat_in, map_in, temp_in, kind_in,
    pot_out, brick_out,
    sheet, ints, kind_v, first_b, later_b, onehot, red1, red2, heat_own, heat_ext, heat_b, base_b, rate_b,
    border, cross,
    border_send, border_recv, pass_send, pass_recv,
    known_sem, local_sem, sheet_send, sheet_recv, len_send, len_recv, rad_send, rad_recv, late_send, late_recv,
    r1_send, r1_recv, r2_send, r2_recv, h_send, h_recv, e_send, e_recv,
):
    m = lax.axis_index("magnet")
    s = lax.axis_index("slab")
    rs, width = warm_in.shape
    rows, spokes = temp_in.shape[1], temp_in.shape[2]
    brick = rows + 16
    g = m * S + s
    target0 = max(0, S - 2 - REACH)
    heated = s >= target0

    own_rows = pl.ds(pl.multiple_of(s * rs, 8), rs)
    mid = pl.ds(rs, rs)
    bmid = pl.ds(8, rows)
    for lo in (0, 2 * rs):
        sheet[:, lo : lo + rs, :] = jnp.zeros((4, rs, width), F32)
    ghost_t = jnp.zeros((brick, spokes), F32)
    ghost_k = jnp.full((brick, spokes), -1.0, F32)
    for buf in (first_b, later_b):
        for i in range(buf.shape[0]):
            buf[i, 0] = ghost_t
            buf[i, 1] = ghost_k
    for i in range(heat_b.shape[0]):
        heat_b[i] = ghost_t
    local = [
        pltpu.make_async_copy(kind_in.at[0], kind_v, local_sem.at[0]),
        pltpu.make_async_copy(temp_in.at[0], first_b.at[1, 0, bmid, :], local_sem.at[1]),
        pltpu.make_async_copy(warm_in, sheet.at[0, mid, :], local_sem.at[2]),
        pltpu.make_async_copy(volt_in, sheet.at[1, mid, :], local_sem.at[3]),
        pltpu.make_async_copy(pat_in, ints.at[0], local_sem.at[4]),
        pltpu.make_async_copy(map_in.at[own_rows, :], ints.at[1], local_sem.at[5]),
    ]
    for c in local:
        c.start()

    barrier = pltpu.get_barrier_semaphore()

    def greet(who):
        pl.semaphore_signal(barrier, inc=1, device_id=who, device_id_type=MESH)

    count = M - 1
    for d in range(1, NEAR + 1):
        pl.when(s >= d)(lambda: greet((m, s - d)))
        pl.when(s < S - d)(lambda: greet((m, s + d)))
        count = count + jnp.where(s >= d, 1, 0) + jnp.where(s < S - d, 1, 0)
    for d in range(1, M):
        greet((lax.rem(m + d, M), s))
    middle = S // 2 - 1
    at_top, at_end = (s <= 1) & (m > 0), (s >= S - 2) & (m < M - 1)
    is_middle = (s == middle) & (m < M - 1)
    pl.when(at_top)(lambda: greet((m - 1, middle)))

    @pl.when(is_middle)
    def _():
        greet((m + 1, 0))
        greet((m + 1, 1))

    count = count + jnp.where(at_top, 1, 0) + jnp.where(is_middle, 2, 0)
    if S - 1 - middle > NEAR:
        pl.when(at_end)(lambda: greet((m, middle)))

        @pl.when(is_middle)
        def _():
            greet((m, S - 2))
            greet((m, S - 1))

        count = count + jnp.where(at_end, 1, 0) + jnp.where(is_middle, 2, 0)
    for c in local:
        c.wait()
    sheet[2:4, rs : 2 * rs, :] = ints[...].astype(F32)
    first_b[1, 1, bmid, :] = kind_v[...].astype(F32)
    pl.semaphore_wait(barrier, count)

    pending = []

    def sent(copies):
        for pred, c in copies:
            if pred is None:
                c.wait_send()
            else:
                pl.when(pred)(c.wait_send)

    def remote(pred, src, dst, send, recv, who):
        nonlocal pending
        c = pltpu.make_async_remote_copy(
            src_ref=src, dst_ref=dst, send_sem=send, recv_sem=recv, device_id=who, device_id_type=MESH
        )
        if pred is None:
            c.start()
        else:
            pl.when(pred)(c.start)
        pending.append((pred, c))

    def arrived(pred, src, dst, send, recv):
        c = pltpu.make_async_remote_copy(
            src_ref=src, dst_ref=dst, send_sem=send, recv_sem=recv, device_id=(m, s), device_id_type=MESH
        )
        if pred is None:
            c.wait_recv()
        else:
            pl.when(pred)(c.wait_recv)

    has_prev, has_next = s > 0, s < S - 1
    prev, nxt = (m, s - 1), (m, s + 1)
    before, after = pl.ds(0, rs), pl.ds(2 * rs, rs)
    remote(has_next, sheet.at[:, mid, :], sheet.at[:, before, :], sheet_send.at[0], sheet_recv.at[0], nxt)
    remote(has_prev, sheet.at[:, mid, :], sheet.at[:, after, :], sheet_send.at[1], sheet_recv.at[1], prev)
    border_at = pl.ds(pl.multiple_of(jnp.where(at_top, 2 + s, jnp.where(at_end, s - (S - 2), 0)) * rs, 8), rs)
    border_slot = jnp.where(at_top, 2 + s, jnp.where(at_end, s - (S - 2), 0))
    border_to = (jnp.where(at_top, m - 1, m), middle)
    remote(
        at_top | at_end, sheet.at[:, mid, :], border.at[:, border_at, :],
        border_send.at[0], border_recv.at[border_slot], border_to,
    )
    layer = first_b.at[1]
    top_rows, end_rows = pl.ds(8, 8), pl.ds(rows, 8)
    top_halo, end_halo = pl.ds(0, 8), pl.ds(rows + 8, 8)
    remote(m < M - 1, layer.at[:, end_rows, :], layer.at[:, top_halo, :], len_send.at[0], len_recv.at[0], (m + 1, s))
    remote(m > 0, layer.at[:, top_rows, :], layer.at[:, end_halo, :], len_send.at[1], len_recv.at[1], (m - 1, s))

    lane_id = lax.broadcasted_iota(jnp.int32, (spokes, width), 0)
    base_cell = (shells - 2) * spokes
    cell_own = ints[1] - base_cell
    upper_own = cell_own >= spokes
    col_own = jnp.where(upper_own, cell_own - spokes, cell_own)

    def put_onehot(at, row):
        onehot[at * spokes : (at + 1) * spokes, :] = jnp.where(lane_id == row, 1.0, 0.0).astype(jnp.bfloat16)

    for i in range(rs):
        put_onehot(i, col_own[i : i + 1, :])

    arrived(has_prev, sheet.at[:, mid, :], sheet.at[:, before, :], sheet_send.at[0], sheet_recv.at[0])
    arrived(has_next, sheet.at[:, mid, :], sheet.at[:, after, :], sheet_send.at[1], sheet_recv.at[1])

    hops, known = [], NEAR + 1
    while known < S - 1:
        hops.append(min(known, S - 1 - known))
        known += hops[-1]

    def tell(n, d):
        def signal(who):
            pl.semaphore_signal(known_sem.at[n], inc=1, device_id=who, device_id_type=MESH)

        pl.when(s >= d)(lambda: signal((m, s - d)))
        pl.when(s < S - d)(lambda: signal((m, s + d)))

    def hear(n, d):
        pl.semaphore_wait(known_sem.at[n], jnp.where(s >= d, 1, 0) + jnp.where(s < S - d, 1, 0))

    if hops:
        tell(0, hops[0])

    def field_steps(n, first_row):
        row_id = lax.broadcasted_iota(jnp.int32, (n, width), 0) + first_row
        col_id = lax.broadcasted_iota(jnp.int32, (n, width), 1)
        valid = (row_id >= 0) & (row_id < M * S * rs)
        left_edge, right_edge = col_id == 0, col_id == width - 1

        def from_up(v):
            return pltpu.roll(v, 1, 0)

        def from_down(v):
            return pltpu.roll(v, n - 1, 0)

        def from_left(v):
            return jnp.where(left_edge, 0.0, pltpu.roll(v, 1, 1))

        def from_right(v):
            return jnp.where(right_edge, 0.0, pltpu.roll(v, width - 1, 1))

        return valid, (from_up, from_down, from_left, from_right)

    def krylov(warm, volt, pattern, first_row, count):
        valid, sides = field_steps(warm.shape[0], first_row)
        sigma = jnp.where(valid, jnp.where(pattern == 1.0, copper_factor, 1.0) / (1.0 + sheet_slope * warm), 0.0)
        coeffs = [0.5 * (sigma + side(sigma)) for side in sides]
        contact = jnp.where(pattern == 2.0, contact_gain, 0.0)
        diagonal = leak_diag + contact + coeffs[0] + coeffs[1] + coeffs[2] + coeffs[3]
        basis = [jnp.where(valid, contact * volt, 0.0)]
        for _ in range(count - 1):
            v = basis[-1]
            out = diagonal * v
            for c, side in zip(coeffs, sides):
                out = out - c * side(v)
            basis.append(jnp.where(valid, out, 0.0))
        return coeffs, sides, basis

    sub = lax.broadcasted_iota(jnp.int32, (8, 128), 0)
    lane = lax.broadcasted_iota(jnp.int32, (8, 128), 1)
    is_low = (lane & 32) != 0

    def folded(a, b, step):
        first = (sub & step) == 0
        near = jnp.where(first, a, b)
        far = jnp.where(first, pltpu.roll(a, 8 - step, 0), pltpu.roll(b, step, 0))
        return near, far

    def fold_lanes(p):
        for step in (64, 32):
            p = pair_add(p, (pltpu.roll(p[0], step, 1), pltpu.roll(p[1], step, 1)))
        return p

    def unpacked(tile):
        return tile, pltpu.roll(tile, 96, 1)

    def packed(p):
        return jnp.where(is_low, pltpu.roll(p[1], 32, 1), p[0])

    def gram_tile(basis, lo, hi):
        cells = [(r, c) for r in range(lo, hi, 8) for c in range(0, width, 128)]
        chunks = [[v[r : r + 8, c : c + 128] for r, c in cells] for v in basis]
        split = [[halves(v) for v in field] for field in chunks]
        pairs = []
        for i, j in GRAM:
            terms = [two_prod(a, b, sa, sb) for a, b, sa, sb in zip(chunks[i], chunks[j], split[i], split[j])]
            pairs.append(tree(terms, pair_add))
        eight, ninth = pairs[:8], pairs[8]
        for step in (4, 2, 1):
            merged = []
            for a, b in zip(eight[:step], eight[step:]):
                parts = [folded(x, y, step) for x, y in zip(a, b)]
                merged.append(pair_add((parts[0][0], parts[1][0]), (parts[0][1], parts[1][1])))
            eight = merged
        eight, ninth = fold_lanes(eight[0]), fold_lanes(ninth)
        both = [jnp.where(lane < 64, a, b) for a, b in zip(eight, ninth)]
        return jnp.where(is_low, both[1], both[0])

    _, _, basis = krylov(sheet[0], sheet[1], sheet[2], (g - 1) * rs, 4)
    cross_up, cross_down = (s == 0) & (m > 0), (s == S - 1) & (m < M - 1)
    is_cross = cross_up | cross_down
    red1[s] = jnp.where(is_cross, 0.0, gram_tile(basis, rs, 2 * rs))

    arrived(m > 0, layer.at[:, end_rows, :], layer.at[:, top_halo, :], len_send.at[0], len_recv.at[0])
    arrived(m < M - 1, layer.at[:, top_rows, :], layer.at[:, end_halo, :], len_send.at[1], len_recv.at[1])
    remote(s < S - 1, layer, first_b.at[0], rad_send.at[0], rad_recv.at[0], (m, s + 1))
    remote(s > 0, layer, first_b.at[2], rad_send.at[1], rad_recv.at[1], (m, s - 1))

    @pl.when(is_middle)
    def _():
        for slot in range(4):
            arrived(None, sheet.at[:, mid, :], border.at[:, slot * rs : (slot + 1) * rs, :], border_send.at[0], border_recv.at[slot])

    remote(is_middle, border.at[:, 2 * rs : 3 * rs, :], cross, pass_send.at[0], pass_recv.at[0], (m, S - 1))
    remote(is_middle, border.at[:, rs : 2 * rs, :], cross, pass_send.at[1], pass_recv.at[0], (m + 1, 0))

    @pl.when(is_middle)
    def _():
        _, _, fields = krylov(border[0], border[1], border[2], (m * S + S - 2) * rs, 4)
        tile = gram_tile(fields, rs, 3 * rs)
        red1[s] = packed(pair_add(unpacked(red1[s]), unpacked(tile)))

    for n, d in enumerate(hops):
        if n:
            tell(n, d)
        hear(n, d)
    for d in range(1, S):
        remote(None, red1.at[s], red1.at[s], r1_send.at[d], r1_recv.at[d], (m, lax.rem(s + d, S)))

    arrived(s > 0, layer, first_b.at[0], rad_send.at[0], rad_recv.at[0])
    arrived(s < S - 1, layer, first_b.at[2], rad_send.at[1], rad_recv.at[1])

    def conduct(temps, kinds):
        return [lookup(k, conduct_table) * (1.0 + diffusivity_derivative * t) for t, k in zip(temps, kinds)]

    def rate(kind):
        return lookup(kind, tuple(time_step / c for c in capacity_table))

    temps = [first_b[i, 0] for i in range(3)]
    kinds = [first_b[i, 1] for i in range(3)]
    (flux,) = fluxes(temps, conduct(temps, kinds), 1, 2)
    later_b[REACH, 0] = temps[1] + rate(kinds[1]) * flux
    later_b[REACH, 1] = kinds[1]
    early, pending = pending, []
    def part(slot, d):
        if d == 1:
            return later_b.at[slot, 0]
        return later_b.at[slot, :, bmid, :] if d == REACH else later_b.at[slot]

    later_b[REACH - 1, 1] = kinds[0]
    later_b[REACH + 1, 1] = kinds[2]
    for d in range(1, REACH + 1):
        remote(s < S - d, part(REACH, d), part(REACH - d, d), late_send.at[2 * d - 2], late_recv.at[2 * d - 2], (m, s + d))
        remote(s >= d, part(REACH, d), part(REACH + d, d), late_send.at[2 * d - 1], late_recv.at[2 * d - 1], (m, s - d))
    late, pending = pending, []

    def pair_of(ref, i):
        return unpacked(ref[i])

    for d in range(1, S):
        src = lax.rem(s + S - d, S)
        arrived(None, red1.at[s], red1.at[src], r1_send.at[d], r1_recv.at[d])
    total = tree([pair_of(red1, i) for i in range(S)], pair_add)
    red2[m] = packed(total)
    for d in range(1, M):
        remote(None, red2.at[m], red2.at[m], r2_send.at[d], r2_recv.at[d], (lax.rem(m + d, M), s))
    arrived(is_cross, border.at[:, before, :], cross, pass_send.at[0], pass_recv.at[0])

    @pl.when(cross_up)
    def _():
        sheet[:, before, :] = cross[...]

    @pl.when(cross_down)
    def _():
        sheet[:, after, :] = cross[...]

    coeffs, sides, basis = krylov(sheet[0], sheet[1], sheet[2], (g - 1) * rs, 3)

    before_string = s == 0

    def outer(a):
        return jnp.where(before_string, pltpu.roll(a[0:rs], 3, 0), a[2 * rs :])

    cell_ext = outer(sheet[3]).astype(jnp.int32) - base_cell
    cell_ext = jnp.clip(cell_ext, 0, 2 * spokes - 1)
    upper_ext = cell_ext >= spokes
    col_ext = jnp.where(upper_ext, cell_ext - spokes, cell_ext)
    for i in range(3):
        put_onehot(rs + i, col_ext[i : i + 1, :])

    for d in range(1, M):
        src = lax.rem(m + M - d, M)
        arrived(None, red2.at[m], red2.at[src], r2_send.at[d], r2_recv.at[d])
    high, low = tree([pair_of(red2, i) for i in range(M)], pair_add)
    def added(high, low, axes):
        grid = 1024.0 * jnp.max(jnp.abs(high), axis=axes, keepdims=True)
        coarse = (high + grid) - grid
        rest = jnp.sum((high - coarse) + low, axis=axes, keepdims=True)
        return two_sum(jnp.sum(coarse, axis=axes, keepdims=True), rest)

    in_eight, in_ninth = lane < 32, (lane >= 64) & (lane < 96)
    sums = added(jnp.where(in_eight, high, 0.0), jnp.where(in_eight, low, 0.0), 1)
    gram = {ij: (sums[0][n : n + 1], sums[1][n : n + 1]) for n, ij in enumerate(GRAM[:8])}
    gram[GRAM[8]] = added(jnp.where(in_ninth, high, 0.0), jnp.where(in_ninth, low, 0.0), (0, 1))

    def twice(x):
        return 2.0 * x[0], 2.0 * x[1]

    plain = {(i, j): gram[i, j] if i == j else twice(gram[i, j]) for i, j in GRAM if j < 3}
    with_a = {
        (0, 0): gram[0, 1],
        (0, 1): pair_add(gram[0, 2], gram[1, 1]),
        (1, 1): gram[1, 2],
        (0, 2): pair_add(gram[0, 3], gram[1, 2]),
        (1, 2): pair_add(gram[1, 3], gram[2, 2]),
        (2, 2): gram[2, 3],
    }

    def upto(table, n):
        return {ij: v for ij, v in table.items() if ij[1] < n}

    one = jnp.ones_like(gram[0, 0][0])
    norm0 = gram[0, 0][0]
    a0 = norm0 / gram[0, 1][0]
    norm1 = quadratic([one, -a0], upto(plain, 2))
    b1 = norm1 / norm0
    p1 = [1.0 + b1, -a0]
    a1 = norm1 / quadratic(p1, upto(with_a, 2))
    r2 = [one, -a0 - a1 * p1[0], -a1 * p1[1]]
    norm2 = quadratic(r2, plain)
    b2 = norm2 / norm1
    p2 = [r2[0] + b2 * p1[0], r2[1] + b2 * p1[1], r2[2]]
    a2 = norm2 / quadratic(p2, with_a)
    weights = [a0 + a1 * p1[0] + a2 * p2[0], a1 * p1[1] + a2 * p2[1], a2 * p2[2]]
    potential = weights[0] * basis[0] + weights[1] * basis[1] + weights[2] * basis[2]
    pot_out[...] = potential[rs : 2 * rs]

    joule = jnp.zeros_like(potential)
    for c, side in zip(coeffs, sides):
        drop = potential - side(potential)
        joule = joule + c * (drop * drop)
    joule = heat_factor * joule
    sub_id = lax.broadcasted_iota(jnp.int32, (rs, spokes), 0)

    def binned(power, upper, first, count):
        parts = []
        for value in (jnp.where(upper, 0.0, power), jnp.where(upper, power, 0.0)):
            for _ in range(2):
                part = value.astype(jnp.bfloat16).astype(F32)
                parts.append(part)
                value = value - part
        lhs = jnp.concatenate(parts, axis=0).astype(jnp.bfloat16)
        cols = onehot[first * spokes : (first + count) * spokes, :]
        out = lax.dot_general(lhs, cols, (((1,), (1,)), ((), ())), preferred_element_type=F32)
        heats = []
        for k in range(2):
            part = out[2 * k * rs : (2 * k + 1) * rs] + out[(2 * k + 1) * rs : (2 * k + 2) * rs]
            heat = jnp.zeros((rs, spokes), F32)
            for i in range(count):
                heat = jnp.where(sub_id == i, part[:, i * spokes : (i + 1) * spokes], heat)
            heats.append(heat)
        return heats

    lower, higher = binned(joule[rs : 2 * rs], upper_own, 0, rs)
    heat_own[0] = lower
    heat_own[1] = higher
    at = pl.ds(pl.multiple_of(8 + rs * s, 8), rs)

    def slots(t):
        return pl.ds(REACH + S - 2 - t, 2)

    mine, pending = pending, []
    for n, t in enumerate(range(target0, S)):
        remote(s != t, heat_own, heat_b.at[slots(t), at, :], h_send.at[n], h_recv.at[s], (m, t))
    ext_lower, ext_higher = binned(outer(joule), upper_ext, rs, 3)
    heat_ext[0] = jnp.where(before_string, pltpu.roll(ext_lower, rs - 3, 0), ext_lower)
    heat_ext[1] = jnp.where(before_string, pltpu.roll(ext_higher, rs - 3, 0), ext_higher)
    at_rim = (s == 0) | (s == S - 1)
    side_of = jnp.where(before_string, 0, 1)
    ext_at = pl.ds(pl.multiple_of(jnp.where(before_string, 0, rows + 8), 8), 8)
    for n, t in enumerate(range(target0, S)):
        remote(at_rim & (s != t), heat_ext, heat_b.at[slots(t), ext_at, :], e_send.at[n], e_recv.at[side_of], (m, t))

    @pl.when(heated)
    def _():
        slot = REACH + S - 2 - s
        heat_b[slot, at, :] = lower
        heat_b[slot + 1, at, :] = higher

        @pl.when(at_rim)
        def _():
            heat_b[slot, ext_at, :] = heat_ext[0]
            heat_b[slot + 1, ext_at, :] = heat_ext[1]

    for d in range(1, REACH + 1):
        arrived(s >= d, part(REACH, d), part(REACH - d, d), late_send.at[2 * d - 2], late_recv.at[2 * d - 2])
        arrived(s < S - d, part(REACH, d), part(REACH + d, d), late_send.at[2 * d - 1], late_recv.at[2 * d - 1])
    count = 2 * REACH + 1
    for i in range(count):
        kind = later_b[i, 1]
        base_b[i] = lookup(kind, conduct_table)
        rate_b[i] = rate(kind)
    sent(early + late + mine)
    pair = pl.ds(0, 2)
    for j in range(S):
        at_j = pl.ds(8 + rs * j, rs)
        arrived(heated & (s != j), heat_own, heat_b.at[pair, at_j, :], h_send.at[0], h_recv.at[j])
    arrived(heated & (s != 0), heat_ext, heat_b.at[pair, top_halo, :], e_send.at[0], e_recv.at[0])
    arrived(heated & (s != S - 1), heat_ext, heat_b.at[pair, end_halo, :], e_send.at[0], e_recv.at[1])

    count = 2 * REACH + 1
    temps = [later_b[i, 0] + rate_b[i] * heat_b[i] for i in range(count)]
    for step in range(1, REACH + 1):
        first, last = step, count - step
        near = range(first - 1, last + 1)
        conds = {i: base_b[i] * (1.0 + diffusivity_derivative * temps[i]) for i in near}
        for i, f in zip(range(first, last), fluxes(temps, conds, first, last)):
            temps[i] = temps[i] + rate_b[i] * (f + heat_b[i])
    brick_out[0] = temps[REACH][8 : 8 + rows]
    sent(pending)


def solution(mesh):
    M, S = mesh.shape["magnet"], mesh.shape["slab"]

    def local(warm, volt, pattern, cells, temp, kind):
        rs, width = warm.shape
        depth, rows, spokes = temp.shape
        brick = rows + 16
        dma = pltpu.SemaphoreType.DMA
        targets = REACH + 2
        shapes = (
            jax.ShapeDtypeStruct((rs, width), F32),
            jax.ShapeDtypeStruct((depth, rows, spokes), F32),
        )
        return pl.pallas_call(
            functools.partial(kernel, M, S, depth * S),
            out_shape=shapes,
            in_specs=[pl.BlockSpec(memory_space=pltpu.HBM)] * 6,
            out_specs=[pl.BlockSpec(memory_space=pltpu.VMEM)] * 2,
            scratch_shapes=[
                pltpu.VMEM((4, 3 * rs, width), F32),
                pltpu.VMEM((2, rs, width), jnp.int32),
                pltpu.VMEM((rows, spokes), jnp.int32),
                pltpu.VMEM((3, 2, brick, spokes), F32),
                pltpu.VMEM((2 * REACH + 1, 2, brick, spokes), F32),
                pltpu.VMEM(((rs + 3) * spokes, width), jnp.bfloat16),
                pltpu.VMEM((S, 8, 128), F32),
                pltpu.VMEM((M, 8, 128), F32),
                pltpu.VMEM((2, rs, spokes), F32),
                pltpu.VMEM((2, rs, spokes), F32),
                pltpu.VMEM((2 * REACH + 2, brick, spokes), F32),
                pltpu.VMEM((2 * REACH + 1, brick, spokes), F32),
                pltpu.VMEM((2 * REACH + 1, brick, spokes), F32),
                pltpu.VMEM((4, 4 * rs, width), F32),
                pltpu.VMEM((4, rs, width), F32),
                dma((1,)), dma((4,)),
                dma((2,)), dma((1,)),
                pltpu.SemaphoreType.REGULAR((8,)),
                dma((6,)),
                dma((2,)), dma((2,)),
                dma((2,)), dma((2,)),
                dma((2,)), dma((2,)),
                dma((2 * REACH,)), dma((2 * REACH,)),
                dma((S,)), dma((S,)),
                dma((M,)), dma((M,)),
                dma((targets,)), dma((S,)),
                dma((targets,)), dma((2,)),
            ],
            compiler_params=pltpu.CompilerParams(
                collective_id=0, has_side_effects=True, vmem_limit_bytes=63 * 1024 * 1024
            ),
            name="window",
        )(warm, volt, pattern, cells, temp, kind)

    return jax.shard_map(
        local,
        mesh=mesh,
        in_specs=(
            P(("magnet", "slab"), None),
            P(("magnet", "slab"), None),
            P(("magnet", "slab"), None),
            P("magnet", None),
            P("slab", "magnet", None),
            P("slab", "magnet", None),
        ),
        out_specs=(P(("magnet", "slab"), None), P("slab", "magnet", None)),
        check_vma=False,
    )
```

```python
import functools

import jax
import jax.numpy as jnp
from jax import lax
from jax.experimental import pallas as pl
from jax.experimental.pallas import tpu as pltpu
from jax.sharding import PartitionSpec as P

MESH = pl.DeviceIdType.MESH
F32 = jnp.float32
leak_diag = 0.25
contact_gain = 4.0
copper_factor = 3.0
sheet_slope = 0.5
heat_factor = 1.5
time_step = 0.03
conduct_table = (0.3, 1.0, 2.0, 0.6)
capacity_table = (1.0, 1.5, 2.0, 1.2)
diffusivity_derivative = 0.4
REACH = 3
GRAM = ((0, 0), (0, 1), (0, 2), (0, 3), (1, 1), (1, 2), (1, 3), (2, 2), (2, 3))


def two_sum(a, b):
    s = a + b
    t = s - a
    return s, (a - (s - t)) + (b - t)


def halves(a):
    c = a * 4097.0
    high = c - (c - a)
    return high, a - high


def two_prod(a, b, sa, sb):
    p = a * b
    return p, ((sa[0] * sb[0] - p) + sa[0] * sb[1] + sa[1] * sb[0]) + sa[1] * sb[1]


def pair_add(x, y):
    s, e = two_sum(x[0], y[0])
    return s, e + (x[1] + y[1])


def tree(items, add):
    while len(items) > 1:
        items = [add(*items[i : i + 2]) if i + 1 < len(items) else items[i] for i in range(0, len(items), 2)]
    return items[0]


def pair_mul(x, y):
    p, e = two_prod(x[0], y[0], halves(x[0]), halves(y[0]))
    return p, e + (x[0] * y[1] + x[1] * y[0])


def quadratic(coefs, gram):
    terms = []
    for (i, j), g in gram.items():
        c = two_prod(coefs[i], coefs[j], halves(coefs[i]), halves(coefs[j]))
        terms.append(pair_mul(c, g))
    s = tree(terms, pair_add)
    return s[0] + s[1]


def lookup(kind, table):
    out = jnp.zeros(kind.shape, F32)
    for i, value in enumerate(table):
        out = jnp.where(kind == float(i), value, out)
    return out


def fluxes(temps, conds, first, last):
    rows = temps[0].shape[0]
    face = {}
    for i in range(first - 1, last):
        face[i] = (conds[i] + conds[i + 1]) * (temps[i + 1] - temps[i])
    out = []
    for i in range(first, last):
        t, k = temps[i], conds[i]
        total = face[i] - face[i - 1]
        for axis, size in ((0, rows), (1, t.shape[1])):
            f = (k + pltpu.roll(k, 1, axis)) * (pltpu.roll(t, 1, axis) - t)
            total = total + (f - pltpu.roll(f, size - 1, axis))
        out.append(0.5 * total)
    return out


def kernel(
    M, S, shells,
    warm_in, volt_in, pat_in, map_in, temp_in, kind_in,
    pot_out, brick_out,
    sheet_f, sheet_i, kind_v, first_b, later_b, onehot, red1, red2, heat_own, heat_ext, heat_b, base_b, rate_b,
    border_f, border_i, cross_f, cross_i,
    border_send, border_recv, pass_send, pass_recv,
    local_sem, sheet_send, sheet_recv, len_send, len_recv, rad_send, rad_recv, late_send, late_recv,
    r1_send, r1_recv, r2_send, r2_recv, h_send, h_recv, e_send, e_recv,
):
    m = lax.axis_index("magnet")
    s = lax.axis_index("slab")
    rs, width = warm_in.shape
    rows, spokes = temp_in.shape[1], temp_in.shape[2]
    brick = rows + 16
    g = m * S + s
    target0 = max(0, S - 2 - REACH)
    heated = s >= target0

    own_rows = pl.ds(pl.multiple_of(s * rs, 8), rs)
    mid = pl.ds(rs, rs)
    bmid = pl.ds(8, rows)
    zf = jnp.zeros((2, rs, width), F32)
    zi = jnp.zeros((2, rs, width), jnp.int32)
    for lo in (0, 2 * rs):
        sheet_f[:, lo : lo + rs, :] = zf
        sheet_i[:, lo : lo + rs, :] = zi
    ghost_t = jnp.zeros((brick, spokes), F32)
    ghost_k = jnp.full((brick, spokes), -1.0, F32)
    for buf in (first_b, later_b):
        for i in range(buf.shape[0]):
            buf[i, 0] = ghost_t
            buf[i, 1] = ghost_k
    for i in range(heat_b.shape[0]):
        heat_b[i] = ghost_t
    local = [
        pltpu.make_async_copy(kind_in.at[0], kind_v, local_sem.at[0]),
        pltpu.make_async_copy(temp_in.at[0], first_b.at[1, 0, bmid, :], local_sem.at[1]),
        pltpu.make_async_copy(warm_in, sheet_f.at[0, mid, :], local_sem.at[2]),
        pltpu.make_async_copy(volt_in, sheet_f.at[1, mid, :], local_sem.at[3]),
        pltpu.make_async_copy(pat_in, sheet_i.at[0, mid, :], local_sem.at[4]),
        pltpu.make_async_copy(map_in.at[own_rows, :], sheet_i.at[1, mid, :], local_sem.at[5]),
    ]
    for c in local:
        c.start()

    barrier = pltpu.get_barrier_semaphore()

    def greet(who):
        pl.semaphore_signal(barrier, inc=1, device_id=who, device_id_type=MESH)

    for d in range(1, S):
        greet((m, lax.rem(s + d, S)))
    for d in range(1, M):
        greet((lax.rem(m + d, M), s))
    middle = S // 2 - 1
    at_top, at_end = (s <= 1) & (m > 0), (s >= S - 2) & (m < M - 1)
    is_middle = (s == middle) & (m < M - 1)
    pl.when(at_top)(lambda: greet((m - 1, middle)))

    @pl.when(is_middle)
    def _():
        greet((m + 1, 0))
        greet((m + 1, 1))

    extra = jnp.where(at_top, 1, 0) + jnp.where(is_middle, 2, 0)
    for c in local:
        c.wait()
    first_b[1, 1, bmid, :] = kind_v[...].astype(F32)
    pl.semaphore_wait(barrier, S + M - 2 + extra)

    pending = []

    def sent(copies):
        for pred, c in copies:
            if pred is None:
                c.wait_send()
            else:
                pl.when(pred)(c.wait_send)

    def remote(pred, src, dst, send, recv, who):
        nonlocal pending
        c = pltpu.make_async_remote_copy(
            src_ref=src, dst_ref=dst, send_sem=send, recv_sem=recv, device_id=who, device_id_type=MESH
        )
        if pred is None:
            c.start()
        else:
            pl.when(pred)(c.start)
        pending.append((pred, c))

    def arrived(pred, src, dst, send, recv):
        c = pltpu.make_async_remote_copy(
            src_ref=src, dst_ref=dst, send_sem=send, recv_sem=recv, device_id=(m, s), device_id_type=MESH
        )
        if pred is None:
            c.wait_recv()
        else:
            pl.when(pred)(c.wait_recv)

    has_prev, has_next = s > 0, s < S - 1
    prev, nxt = (m, s - 1), (m, s + 1)
    before, after = pl.ds(0, rs), pl.ds(2 * rs, rs)
    for k, buf in enumerate((sheet_f, sheet_i)):
        remote(has_next, buf.at[:, mid, :], buf.at[:, before, :], sheet_send.at[2 * k], sheet_recv.at[2 * k], nxt)
        remote(has_prev, buf.at[:, mid, :], buf.at[:, after, :], sheet_send.at[2 * k + 1], sheet_recv.at[2 * k + 1], prev)
    border_at = pl.ds(pl.multiple_of(jnp.where(at_top, 2 + s, jnp.where(at_end, s - (S - 2), 0)) * rs, 8), rs)
    border_slot = jnp.where(at_top, 2 + s, jnp.where(at_end, s - (S - 2), 0))
    border_to = (jnp.where(at_top, m - 1, m), middle)
    for k, (buf, border) in enumerate(((sheet_f, border_f), (sheet_i, border_i))):
        remote(
            at_top | at_end, buf.at[:, mid, :], border.at[:, border_at, :],
            border_send.at[k], border_recv.at[k, border_slot], border_to,
        )
    layer = first_b.at[1]
    top_rows, end_rows = pl.ds(8, 8), pl.ds(rows, 8)
    top_halo, end_halo = pl.ds(0, 8), pl.ds(rows + 8, 8)
    remote(m < M - 1, layer.at[:, end_rows, :], layer.at[:, top_halo, :], len_send.at[0], len_recv.at[0], (m + 1, s))
    remote(m > 0, layer.at[:, top_rows, :], layer.at[:, end_halo, :], len_send.at[1], len_recv.at[1], (m - 1, s))

    lane_id = lax.broadcasted_iota(jnp.int32, (spokes, width), 0)
    base_cell = (shells - 2) * spokes
    cell_own = sheet_i[1, rs : 2 * rs, :] - base_cell
    upper_own = cell_own >= spokes
    col_own = jnp.where(upper_own, cell_own - spokes, cell_own)

    def put_onehot(at, row):
        onehot[at * spokes : (at + 1) * spokes, :] = jnp.where(lane_id == row, 1.0, 0.0).astype(jnp.bfloat16)

    for i in range(rs):
        put_onehot(i, col_own[i : i + 1, :])

    arrived(m > 0, layer.at[:, end_rows, :], layer.at[:, top_halo, :], len_send.at[0], len_recv.at[0])
    arrived(m < M - 1, layer.at[:, top_rows, :], layer.at[:, end_halo, :], len_send.at[1], len_recv.at[1])
    remote(s < S - 1, layer, first_b.at[0], rad_send.at[0], rad_recv.at[0], (m, s + 1))
    remote(s > 0, layer, first_b.at[2], rad_send.at[1], rad_recv.at[1], (m, s - 1))

    for k, buf in enumerate((sheet_f, sheet_i)):
        arrived(has_prev, buf.at[:, mid, :], buf.at[:, before, :], sheet_send.at[2 * k], sheet_recv.at[2 * k])
        arrived(has_next, buf.at[:, mid, :], buf.at[:, after, :], sheet_send.at[2 * k + 1], sheet_recv.at[2 * k + 1])

    def field_steps(n, first_row):
        row_id = lax.broadcasted_iota(jnp.int32, (n, width), 0) + first_row
        col_id = lax.broadcasted_iota(jnp.int32, (n, width), 1)
        valid = (row_id >= 0) & (row_id < M * S * rs)
        left_edge, right_edge = col_id == 0, col_id == width - 1

        def from_up(v):
            return pltpu.roll(v, 1, 0)

        def from_down(v):
            return pltpu.roll(v, n - 1, 0)

        def from_left(v):
            return jnp.where(left_edge, 0.0, pltpu.roll(v, 1, 1))

        def from_right(v):
            return jnp.where(right_edge, 0.0, pltpu.roll(v, width - 1, 1))

        return valid, (from_up, from_down, from_left, from_right)

    def krylov(warm, volt, pattern, first_row, count):
        valid, sides = field_steps(warm.shape[0], first_row)
        sigma = jnp.where(valid, jnp.where(pattern == 1, copper_factor, 1.0) / (1.0 + sheet_slope * warm), 0.0)
        coeffs = [0.5 * (sigma + side(sigma)) for side in sides]
        contact = jnp.where(pattern == 2, contact_gain, 0.0)
        diagonal = leak_diag + contact + coeffs[0] + coeffs[1] + coeffs[2] + coeffs[3]
        basis = [jnp.where(valid, contact * volt, 0.0)]
        for _ in range(count - 1):
            v = basis[-1]
            out = diagonal * v
            for c, side in zip(coeffs, sides):
                out = out - c * side(v)
            basis.append(jnp.where(valid, out, 0.0))
        return coeffs, sides, basis

    sub = lax.broadcasted_iota(jnp.int32, (8, 128), 0)
    lane = lax.broadcasted_iota(jnp.int32, (8, 128), 1)
    is_low = (lane & 32) != 0

    def folded(a, b, step):
        first = (sub & step) == 0
        near = jnp.where(first, a, b)
        far = jnp.where(first, pltpu.roll(a, 8 - step, 0), pltpu.roll(b, step, 0))
        return near, far

    def fold_lanes(p):
        for step in (64, 32):
            p = pair_add(p, (pltpu.roll(p[0], step, 1), pltpu.roll(p[1], step, 1)))
        return p

    def unpacked(tile):
        return tile, pltpu.roll(tile, 96, 1)

    def packed(p):
        return jnp.where(is_low, pltpu.roll(p[1], 32, 1), p[0])

    def gram_tile(basis, lo, hi):
        cells = [(r, c) for r in range(lo, hi, 8) for c in range(0, width, 128)]
        chunks = [[v[r : r + 8, c : c + 128] for r, c in cells] for v in basis]
        split = [[halves(v) for v in field] for field in chunks]
        pairs = []
        for i, j in GRAM:
            terms = [two_prod(a, b, sa, sb) for a, b, sa, sb in zip(chunks[i], chunks[j], split[i], split[j])]
            pairs.append(tree(terms, pair_add))
        eight, ninth = pairs[:8], pairs[8]
        for step in (4, 2, 1):
            merged = []
            for a, b in zip(eight[:step], eight[step:]):
                parts = [folded(x, y, step) for x, y in zip(a, b)]
                merged.append(pair_add((parts[0][0], parts[1][0]), (parts[0][1], parts[1][1])))
            eight = merged
        eight, ninth = fold_lanes(eight[0]), fold_lanes(ninth)
        both = [jnp.where(lane < 64, a, b) for a, b in zip(eight, ninth)]
        return jnp.where(is_low, both[1], both[0])

    _, _, basis = krylov(sheet_f[0], sheet_f[1], sheet_i[0], (g - 1) * rs, 4)
    cross_up, cross_down = (s == 0) & (m > 0), (s == S - 1) & (m < M - 1)
    is_cross = cross_up | cross_down
    red1[s] = jnp.where(is_cross, 0.0, gram_tile(basis, rs, 2 * rs))

    @pl.when(is_middle)
    def _():
        for k, (buf, border) in enumerate(((sheet_f, border_f), (sheet_i, border_i))):
            for slot in range(4):
                arrived(None, buf.at[:, mid, :], border.at[:, slot * rs : (slot + 1) * rs, :], border_send.at[k], border_recv.at[k, slot])

    for k, (border, cross) in enumerate(((border_f, cross_f), (border_i, cross_i))):
        remote(is_middle, border.at[:, 2 * rs : 3 * rs, :], cross, pass_send.at[k, 0], pass_recv.at[k], (m, S - 1))
        remote(is_middle, border.at[:, rs : 2 * rs, :], cross, pass_send.at[k, 1], pass_recv.at[k], (m + 1, 0))

    @pl.when(is_middle)
    def _():
        _, _, fields = krylov(border_f[0], border_f[1], border_i[0], (m * S + S - 2) * rs, 4)
        tile = gram_tile(fields, rs, 3 * rs)
        red1[s] = packed(pair_add(unpacked(red1[s]), unpacked(tile)))

    for d in range(1, S):
        remote(None, red1.at[s], red1.at[s], r1_send.at[d], r1_recv.at[d], (m, lax.rem(s + d, S)))

    arrived(s > 0, layer, first_b.at[0], rad_send.at[0], rad_recv.at[0])
    arrived(s < S - 1, layer, first_b.at[2], rad_send.at[1], rad_recv.at[1])

    def conduct(temps, kinds):
        return [lookup(k, conduct_table) * (1.0 + diffusivity_derivative * t) for t, k in zip(temps, kinds)]

    def rate(kind):
        return lookup(kind, tuple(time_step / c for c in capacity_table))

    temps = [first_b[i, 0] for i in range(3)]
    kinds = [first_b[i, 1] for i in range(3)]
    (flux,) = fluxes(temps, conduct(temps, kinds), 1, 2)
    later_b[REACH, 0] = temps[1] + rate(kinds[1]) * flux
    later_b[REACH, 1] = kinds[1]
    early, pending = pending, []
    def part(slot, d):
        if d == 1:
            return later_b.at[slot, 0]
        return later_b.at[slot, :, bmid, :] if d == REACH else later_b.at[slot]

    later_b[REACH - 1, 1] = kinds[0]
    later_b[REACH + 1, 1] = kinds[2]
    for d in range(1, REACH + 1):
        remote(s < S - d, part(REACH, d), part(REACH - d, d), late_send.at[2 * d - 2], late_recv.at[2 * d - 2], (m, s + d))
        remote(s >= d, part(REACH, d), part(REACH + d, d), late_send.at[2 * d - 1], late_recv.at[2 * d - 1], (m, s - d))
    late, pending = pending, []

    def pair_of(ref, i):
        return unpacked(ref[i])

    for d in range(1, S):
        src = lax.rem(s + S - d, S)
        arrived(None, red1.at[s], red1.at[src], r1_send.at[d], r1_recv.at[d])
    total = tree([pair_of(red1, i) for i in range(S)], pair_add)
    red2[m] = packed(total)
    for d in range(1, M):
        remote(None, red2.at[m], red2.at[m], r2_send.at[d], r2_recv.at[d], (lax.rem(m + d, M), s))
    for k, (border, cross) in enumerate(((border_f, cross_f), (border_i, cross_i))):
        arrived(is_cross, border.at[:, before, :], cross, pass_send.at[k, 0], pass_recv.at[k])

    @pl.when(cross_up)
    def _():
        sheet_f[:, before, :] = cross_f[...]
        sheet_i[:, before, :] = cross_i[...]

    @pl.when(cross_down)
    def _():
        sheet_f[:, after, :] = cross_f[...]
        sheet_i[:, after, :] = cross_i[...]

    coeffs, sides, basis = krylov(sheet_f[0], sheet_f[1], sheet_i[0], (g - 1) * rs, 3)

    before_string = s == 0

    def outer(a):
        return jnp.where(before_string, pltpu.roll(a[0:rs], 3, 0), a[2 * rs :])

    cell_ext = outer(sheet_i[1]) - base_cell
    cell_ext = jnp.clip(cell_ext, 0, 2 * spokes - 1)
    upper_ext = cell_ext >= spokes
    col_ext = jnp.where(upper_ext, cell_ext - spokes, cell_ext)
    for i in range(3):
        put_onehot(rs + i, col_ext[i : i + 1, :])

    for d in range(1, M):
        src = lax.rem(m + M - d, M)
        arrived(None, red2.at[m], red2.at[src], r2_send.at[d], r2_recv.at[d])
    high, low = tree([pair_of(red2, i) for i in range(M)], pair_add)
    def added(high, low, axes):
        grid = 1024.0 * jnp.max(jnp.abs(high), axis=axes, keepdims=True)
        coarse = (high + grid) - grid
        rest = jnp.sum((high - coarse) + low, axis=axes, keepdims=True)
        return two_sum(jnp.sum(coarse, axis=axes, keepdims=True), rest)

    in_eight, in_ninth = lane < 32, (lane >= 64) & (lane < 96)
    sums = added(jnp.where(in_eight, high, 0.0), jnp.where(in_eight, low, 0.0), 1)
    gram = {ij: (sums[0][n : n + 1], sums[1][n : n + 1]) for n, ij in enumerate(GRAM[:8])}
    gram[GRAM[8]] = added(jnp.where(in_ninth, high, 0.0), jnp.where(in_ninth, low, 0.0), (0, 1))

    def twice(x):
        return 2.0 * x[0], 2.0 * x[1]

    plain = {(i, j): gram[i, j] if i == j else twice(gram[i, j]) for i, j in GRAM if j < 3}
    with_a = {
        (0, 0): gram[0, 1],
        (0, 1): pair_add(gram[0, 2], gram[1, 1]),
        (1, 1): gram[1, 2],
        (0, 2): pair_add(gram[0, 3], gram[1, 2]),
        (1, 2): pair_add(gram[1, 3], gram[2, 2]),
        (2, 2): gram[2, 3],
    }

    def upto(table, n):
        return {ij: v for ij, v in table.items() if ij[1] < n}

    one = jnp.ones_like(gram[0, 0][0])
    norm0 = gram[0, 0][0]
    a0 = norm0 / gram[0, 1][0]
    norm1 = quadratic([one, -a0], upto(plain, 2))
    b1 = norm1 / norm0
    p1 = [1.0 + b1, -a0]
    a1 = norm1 / quadratic(p1, upto(with_a, 2))
    r2 = [one, -a0 - a1 * p1[0], -a1 * p1[1]]
    norm2 = quadratic(r2, plain)
    b2 = norm2 / norm1
    p2 = [r2[0] + b2 * p1[0], r2[1] + b2 * p1[1], r2[2]]
    a2 = norm2 / quadratic(p2, with_a)
    weights = [a0 + a1 * p1[0] + a2 * p2[0], a1 * p1[1] + a2 * p2[1], a2 * p2[2]]
    potential = weights[0] * basis[0] + weights[1] * basis[1] + weights[2] * basis[2]
    pot_out[...] = potential[rs : 2 * rs]

    joule = jnp.zeros_like(potential)
    for c, side in zip(coeffs, sides):
        drop = potential - side(potential)
        joule = joule + c * (drop * drop)
    joule = heat_factor * joule
    sub_id = lax.broadcasted_iota(jnp.int32, (rs, spokes), 0)

    def binned(power, upper, first, count):
        parts = []
        for value in (jnp.where(upper, 0.0, power), jnp.where(upper, power, 0.0)):
            for _ in range(2):
                part = value.astype(jnp.bfloat16).astype(F32)
                parts.append(part)
                value = value - part
        lhs = jnp.concatenate(parts, axis=0).astype(jnp.bfloat16)
        cols = onehot[first * spokes : (first + count) * spokes, :]
        out = lax.dot_general(lhs, cols, (((1,), (1,)), ((), ())), preferred_element_type=F32)
        heats = []
        for k in range(2):
            part = out[2 * k * rs : (2 * k + 1) * rs] + out[(2 * k + 1) * rs : (2 * k + 2) * rs]
            heat = jnp.zeros((rs, spokes), F32)
            for i in range(count):
                heat = jnp.where(sub_id == i, part[:, i * spokes : (i + 1) * spokes], heat)
            heats.append(heat)
        return heats

    lower, higher = binned(joule[rs : 2 * rs], upper_own, 0, rs)
    heat_own[0] = lower
    heat_own[1] = higher
    at = pl.ds(pl.multiple_of(8 + rs * s, 8), rs)

    def slots(t):
        return pl.ds(REACH + S - 2 - t, 2)

    mine, pending = pending, []
    for n, t in enumerate(range(target0, S)):
        remote(s != t, heat_own, heat_b.at[slots(t), at, :], h_send.at[n], h_recv.at[s], (m, t))
    ext_lower, ext_higher = binned(outer(joule), upper_ext, rs, 3)
    heat_ext[0] = jnp.where(before_string, pltpu.roll(ext_lower, rs - 3, 0), ext_lower)
    heat_ext[1] = jnp.where(before_string, pltpu.roll(ext_higher, rs - 3, 0), ext_higher)
    at_rim = (s == 0) | (s == S - 1)
    side_of = jnp.where(before_string, 0, 1)
    ext_at = pl.ds(pl.multiple_of(jnp.where(before_string, 0, rows + 8), 8), 8)
    for n, t in enumerate(range(target0, S)):
        remote(at_rim & (s != t), heat_ext, heat_b.at[slots(t), ext_at, :], e_send.at[n], e_recv.at[side_of], (m, t))

    @pl.when(heated)
    def _():
        slot = REACH + S - 2 - s
        heat_b[slot, at, :] = lower
        heat_b[slot + 1, at, :] = higher

        @pl.when(at_rim)
        def _():
            heat_b[slot, ext_at, :] = heat_ext[0]
            heat_b[slot + 1, ext_at, :] = heat_ext[1]

    for d in range(1, REACH + 1):
        arrived(s >= d, part(REACH, d), part(REACH - d, d), late_send.at[2 * d - 2], late_recv.at[2 * d - 2])
        arrived(s < S - d, part(REACH, d), part(REACH + d, d), late_send.at[2 * d - 1], late_recv.at[2 * d - 1])
    count = 2 * REACH + 1
    for i in range(count):
        kind = later_b[i, 1]
        base_b[i] = lookup(kind, conduct_table)
        rate_b[i] = rate(kind)
    sent(early + late + mine)
    pair = pl.ds(0, 2)
    for j in range(S):
        at_j = pl.ds(8 + rs * j, rs)
        arrived(heated & (s != j), heat_own, heat_b.at[pair, at_j, :], h_send.at[0], h_recv.at[j])
    arrived(heated & (s != 0), heat_ext, heat_b.at[pair, top_halo, :], e_send.at[0], e_recv.at[0])
    arrived(heated & (s != S - 1), heat_ext, heat_b.at[pair, end_halo, :], e_send.at[0], e_recv.at[1])

    count = 2 * REACH + 1
    temps = [later_b[i, 0] + rate_b[i] * heat_b[i] for i in range(count)]
    for step in range(1, REACH + 1):
        first, last = step, count - step
        near = range(first - 1, last + 1)
        conds = {i: base_b[i] * (1.0 + diffusivity_derivative * temps[i]) for i in near}
        for i, f in zip(range(first, last), fluxes(temps, conds, first, last)):
            temps[i] = temps[i] + rate_b[i] * (f + heat_b[i])
    brick_out[0] = temps[REACH][8 : 8 + rows]
    sent(pending)


def hand_over(pot, brick, pot_out, brick_out):
    pot_out[...] = pot[...]
    brick_out[...] = brick[...]


def solution(mesh):
    M, S = mesh.shape["magnet"], mesh.shape["slab"]

    def local(warm, volt, pattern, cells, temp, kind):
        rs, width = warm.shape
        depth, rows, spokes = temp.shape
        brick = rows + 16
        dma = pltpu.SemaphoreType.DMA
        targets = REACH + 2
        shapes = (
            jax.ShapeDtypeStruct((rs, width), F32),
            jax.ShapeDtypeStruct((depth, rows, spokes), F32),
        )
        outs = pl.pallas_call(
            functools.partial(kernel, M, S, depth * S),
            out_shape=shapes,
            in_specs=[pl.BlockSpec(memory_space=pltpu.HBM)] * 6,
            out_specs=[pl.BlockSpec(memory_space=pltpu.VMEM)] * 2,
            scratch_shapes=[
                pltpu.VMEM((2, 3 * rs, width), F32),
                pltpu.VMEM((2, 3 * rs, width), jnp.int32),
                pltpu.VMEM((rows, spokes), jnp.int32),
                pltpu.VMEM((3, 2, brick, spokes), F32),
                pltpu.VMEM((2 * REACH + 1, 2, brick, spokes), F32),
                pltpu.VMEM(((rs + 3) * spokes, width), jnp.bfloat16),
                pltpu.VMEM((S, 8, 128), F32),
                pltpu.VMEM((M, 8, 128), F32),
                pltpu.VMEM((2, rs, spokes), F32),
                pltpu.VMEM((2, rs, spokes), F32),
                pltpu.VMEM((2 * REACH + 2, brick, spokes), F32),
                pltpu.VMEM((2 * REACH + 1, brick, spokes), F32),
                pltpu.VMEM((2 * REACH + 1, brick, spokes), F32),
                pltpu.VMEM((2, 4 * rs, width), F32),
                pltpu.VMEM((2, 4 * rs, width), jnp.int32),
                pltpu.VMEM((2, rs, width), F32),
                pltpu.VMEM((2, rs, width), jnp.int32),
                dma((2,)), dma((2, 4)),
                dma((2, 2)), dma((2,)),
                dma((6,)),
                dma((4,)), dma((4,)),
                dma((2,)), dma((2,)),
                dma((2,)), dma((2,)),
                dma((2 * REACH,)), dma((2 * REACH,)),
                dma((S,)), dma((S,)),
                dma((M,)), dma((M,)),
                dma((targets,)), dma((S,)),
                dma((targets,)), dma((2,)),
            ],
            compiler_params=pltpu.CompilerParams(
                collective_id=0, has_side_effects=True, vmem_limit_bytes=63 * 1024 * 1024
            ),
            name="window",
        )(warm, volt, pattern, cells, temp, kind)
        return pl.pallas_call(
            hand_over,
            out_shape=shapes,
            in_specs=[pl.BlockSpec(memory_space=pltpu.VMEM)] * 2,
            out_specs=[pl.BlockSpec(memory_space=pltpu.VMEM)] * 2,
            compiler_params=pltpu.CompilerParams(vmem_limit_bytes=63 * 1024 * 1024),
            name="hand_over",
        )(*outs)

    return jax.shard_map(
        local,
        mesh=mesh,
        in_specs=(
            P(("magnet", "slab"), None),
            P(("magnet", "slab"), None),
            P(("magnet", "slab"), None),
            P("magnet", None),
            P("slab", "magnet", None),
            P("slab", "magnet", None),
        ),
        out_specs=(P(("magnet", "slab"), None), P("slab", "magnet", None)),
        check_vma=False,
    )
```

```python
import functools

import jax
import jax.numpy as jnp
from jax import lax
from jax.experimental import pallas as pl
from jax.experimental.pallas import tpu as pltpu
from jax.sharding import PartitionSpec as P

MESH = pl.DeviceIdType.MESH
F32 = jnp.float32
leak_diag = 0.25
contact_gain = 4.0
copper_factor = 3.0
sheet_slope = 0.5
heat_factor = 1.5
time_step = 0.03
conduct_table = (0.3, 1.0, 2.0, 0.6)
capacity_table = (1.0, 1.5, 2.0, 1.2)
diffusivity_derivative = 0.4
REACH = 3
GRAM = ((0, 0), (0, 1), (0, 2), (0, 3), (1, 1), (1, 2), (1, 3), (2, 2), (2, 3))


def two_sum(a, b):
    s = a + b
    t = s - a
    return s, (a - (s - t)) + (b - t)


def halves(a):
    c = a * 4097.0
    high = c - (c - a)
    return high, a - high


def two_prod(a, b, sa, sb):
    p = a * b
    return p, ((sa[0] * sb[0] - p) + sa[0] * sb[1] + sa[1] * sb[0]) + sa[1] * sb[1]


def pair_add(x, y):
    s, e = two_sum(x[0], y[0])
    return s, e + (x[1] + y[1])


def tree(items, add):
    while len(items) > 1:
        items = [add(*items[i : i + 2]) if i + 1 < len(items) else items[i] for i in range(0, len(items), 2)]
    return items[0]


def pair_mul(x, y):
    p, e = two_prod(x[0], y[0], halves(x[0]), halves(y[0]))
    return p, e + (x[0] * y[1] + x[1] * y[0])


def quadratic(coefs, gram):
    terms = []
    for (i, j), g in gram.items():
        c = two_prod(coefs[i], coefs[j], halves(coefs[i]), halves(coefs[j]))
        terms.append(pair_mul(c, g))
    s = tree(terms, pair_add)
    return s[0] + s[1]


def lookup(kind, table):
    out = jnp.zeros(kind.shape, F32)
    for i, value in enumerate(table):
        out = jnp.where(kind == float(i), value, out)
    return out


def fluxes(temps, conds, first, last):
    rows = temps[0].shape[0]
    face = {}
    for i in range(first - 1, last):
        face[i] = (conds[i] + conds[i + 1]) * (temps[i + 1] - temps[i])
    out = []
    for i in range(first, last):
        t, k = temps[i], conds[i]
        total = face[i] - face[i - 1]
        for axis, size in ((0, rows), (1, t.shape[1])):
            f = (k + pltpu.roll(k, 1, axis)) * (pltpu.roll(t, 1, axis) - t)
            total = total + (f - pltpu.roll(f, size - 1, axis))
        out.append(0.5 * total)
    return out


def kernel(
    M, S, shells,
    warm_in, volt_in, pat_in, map_in, temp_in, kind_in,
    pot_out, brick_out,
    sheet_f, sheet_i, kind_v, first_b, later_b, onehot, red1, red2, heat_own, heat_ext, heat_b, base_b, rate_b,
    border_f, border_i, cross_f, cross_i,
    border_send, border_recv, pass_send, pass_recv,
    local_sem, sheet_send, sheet_recv, len_send, len_recv, rad_send, rad_recv, late_send, late_recv,
    r1_send, r1_recv, r2_send, r2_recv, h_send, h_recv, e_send, e_recv,
):
    m = lax.axis_index("magnet")
    s = lax.axis_index("slab")
    rs, width = warm_in.shape
    rows, spokes = temp_in.shape[1], temp_in.shape[2]
    brick = rows + 16
    g = m * S + s
    target0 = max(0, S - 2 - REACH)
    heated = s >= target0

    own_rows = pl.ds(pl.multiple_of(s * rs, 8), rs)
    mid = pl.ds(rs, rs)
    bmid = pl.ds(8, rows)
    zf = jnp.zeros((2, rs, width), F32)
    zi = jnp.zeros((2, rs, width), jnp.int32)
    for lo in (0, 2 * rs):
        sheet_f[:, lo : lo + rs, :] = zf
        sheet_i[:, lo : lo + rs, :] = zi
    ghost_t = jnp.zeros((brick, spokes), F32)
    ghost_k = jnp.full((brick, spokes), -1.0, F32)
    for buf in (first_b, later_b):
        for i in range(buf.shape[0]):
            buf[i, 0] = ghost_t
            buf[i, 1] = ghost_k
    for i in range(heat_b.shape[0]):
        heat_b[i] = ghost_t
    local = [
        pltpu.make_async_copy(kind_in.at[0], kind_v, local_sem.at[0]),
        pltpu.make_async_copy(temp_in.at[0], first_b.at[1, 0, bmid, :], local_sem.at[1]),
        pltpu.make_async_copy(warm_in, sheet_f.at[0, mid, :], local_sem.at[2]),
        pltpu.make_async_copy(volt_in, sheet_f.at[1, mid, :], local_sem.at[3]),
        pltpu.make_async_copy(pat_in, sheet_i.at[0, mid, :], local_sem.at[4]),
        pltpu.make_async_copy(map_in.at[own_rows, :], sheet_i.at[1, mid, :], local_sem.at[5]),
    ]
    for c in local:
        c.start()

    barrier = pltpu.get_barrier_semaphore()

    def greet(who):
        pl.semaphore_signal(barrier, inc=1, device_id=who, device_id_type=MESH)

    for d in range(1, S):
        greet((m, lax.rem(s + d, S)))
    for d in range(1, M):
        greet((lax.rem(m + d, M), s))
    middle = S // 2 - 1
    at_top, at_end = (s <= 1) & (m > 0), (s >= S - 2) & (m < M - 1)
    is_middle = (s == middle) & (m < M - 1)
    pl.when(at_top)(lambda: greet((m - 1, middle)))

    @pl.when(is_middle)
    def _():
        greet((m + 1, 0))
        greet((m + 1, 1))

    extra = jnp.where(at_top, 1, 0) + jnp.where(is_middle, 2, 0)
    for c in local:
        c.wait()
    first_b[1, 1, bmid, :] = kind_v[...].astype(F32)
    pl.semaphore_wait(barrier, S + M - 2 + extra)

    pending = []

    def sent(copies):
        for pred, c in copies:
            if pred is None:
                c.wait_send()
            else:
                pl.when(pred)(c.wait_send)

    def remote(pred, src, dst, send, recv, who):
        nonlocal pending
        c = pltpu.make_async_remote_copy(
            src_ref=src, dst_ref=dst, send_sem=send, recv_sem=recv, device_id=who, device_id_type=MESH
        )
        if pred is None:
            c.start()
        else:
            pl.when(pred)(c.start)
        pending.append((pred, c))

    def arrived(pred, src, dst, send, recv):
        c = pltpu.make_async_remote_copy(
            src_ref=src, dst_ref=dst, send_sem=send, recv_sem=recv, device_id=(m, s), device_id_type=MESH
        )
        if pred is None:
            c.wait_recv()
        else:
            pl.when(pred)(c.wait_recv)

    has_prev, has_next = s > 0, s < S - 1
    prev, nxt = (m, s - 1), (m, s + 1)
    before, after = pl.ds(0, rs), pl.ds(2 * rs, rs)
    for k, buf in enumerate((sheet_f, sheet_i)):
        remote(has_next, buf.at[:, mid, :], buf.at[:, before, :], sheet_send.at[2 * k], sheet_recv.at[2 * k], nxt)
        remote(has_prev, buf.at[:, mid, :], buf.at[:, after, :], sheet_send.at[2 * k + 1], sheet_recv.at[2 * k + 1], prev)
    border_at = pl.ds(pl.multiple_of(jnp.where(at_top, 2 + s, jnp.where(at_end, s - (S - 2), 0)) * rs, 8), rs)
    border_slot = jnp.where(at_top, 2 + s, jnp.where(at_end, s - (S - 2), 0))
    border_to = (jnp.where(at_top, m - 1, m), middle)
    for k, (buf, border) in enumerate(((sheet_f, border_f), (sheet_i, border_i))):
        remote(
            at_top | at_end, buf.at[:, mid, :], border.at[:, border_at, :],
            border_send.at[k], border_recv.at[k, border_slot], border_to,
        )
    layer = first_b.at[1]
    top_rows, end_rows = pl.ds(8, 8), pl.ds(rows, 8)
    top_halo, end_halo = pl.ds(0, 8), pl.ds(rows + 8, 8)
    remote(m < M - 1, layer.at[:, end_rows, :], layer.at[:, top_halo, :], len_send.at[0], len_recv.at[0], (m + 1, s))
    remote(m > 0, layer.at[:, top_rows, :], layer.at[:, end_halo, :], len_send.at[1], len_recv.at[1], (m - 1, s))

    lane_id = lax.broadcasted_iota(jnp.int32, (spokes, width), 0)
    base_cell = (shells - 2) * spokes
    cell_own = sheet_i[1, rs : 2 * rs, :] - base_cell
    upper_own = cell_own >= spokes
    col_own = jnp.where(upper_own, cell_own - spokes, cell_own)

    def put_onehot(at, row):
        onehot[at * spokes : (at + 1) * spokes, :] = jnp.where(lane_id == row, 1.0, 0.0).astype(jnp.bfloat16)

    for i in range(rs):
        put_onehot(i, col_own[i : i + 1, :])

    arrived(m > 0, layer.at[:, end_rows, :], layer.at[:, top_halo, :], len_send.at[0], len_recv.at[0])
    arrived(m < M - 1, layer.at[:, top_rows, :], layer.at[:, end_halo, :], len_send.at[1], len_recv.at[1])
    remote(s < S - 1, layer, first_b.at[0], rad_send.at[0], rad_recv.at[0], (m, s + 1))
    remote(s > 0, layer, first_b.at[2], rad_send.at[1], rad_recv.at[1], (m, s - 1))

    for k, buf in enumerate((sheet_f, sheet_i)):
        arrived(has_prev, buf.at[:, mid, :], buf.at[:, before, :], sheet_send.at[2 * k], sheet_recv.at[2 * k])
        arrived(has_next, buf.at[:, mid, :], buf.at[:, after, :], sheet_send.at[2 * k + 1], sheet_recv.at[2 * k + 1])

    def field_steps(n, first_row):
        row_id = lax.broadcasted_iota(jnp.int32, (n, width), 0) + first_row
        col_id = lax.broadcasted_iota(jnp.int32, (n, width), 1)
        valid = (row_id >= 0) & (row_id < M * S * rs)
        left_edge, right_edge = col_id == 0, col_id == width - 1

        def from_up(v):
            return pltpu.roll(v, 1, 0)

        def from_down(v):
            return pltpu.roll(v, n - 1, 0)

        def from_left(v):
            return jnp.where(left_edge, 0.0, pltpu.roll(v, 1, 1))

        def from_right(v):
            return jnp.where(right_edge, 0.0, pltpu.roll(v, width - 1, 1))

        return valid, (from_up, from_down, from_left, from_right)

    def krylov(warm, volt, pattern, first_row, count):
        valid, sides = field_steps(warm.shape[0], first_row)
        sigma = jnp.where(valid, jnp.where(pattern == 1, copper_factor, 1.0) / (1.0 + sheet_slope * warm), 0.0)
        coeffs = [0.5 * (sigma + side(sigma)) for side in sides]
        contact = jnp.where(pattern == 2, contact_gain, 0.0)
        diagonal = leak_diag + contact + coeffs[0] + coeffs[1] + coeffs[2] + coeffs[3]
        basis = [jnp.where(valid, contact * volt, 0.0)]
        for _ in range(count - 1):
            v = basis[-1]
            out = diagonal * v
            for c, side in zip(coeffs, sides):
                out = out - c * side(v)
            basis.append(jnp.where(valid, out, 0.0))
        return coeffs, sides, basis

    sub = lax.broadcasted_iota(jnp.int32, (8, 128), 0)
    lane = lax.broadcasted_iota(jnp.int32, (8, 128), 1)
    is_low = (lane & 32) != 0

    def folded(a, b, step):
        first = (sub & step) == 0
        near = jnp.where(first, a, b)
        far = jnp.where(first, pltpu.roll(a, 8 - step, 0), pltpu.roll(b, step, 0))
        return near, far

    def fold_lanes(p):
        for step in (64, 32):
            p = pair_add(p, (pltpu.roll(p[0], step, 1), pltpu.roll(p[1], step, 1)))
        return p

    def unpacked(tile):
        return tile, pltpu.roll(tile, 96, 1)

    def packed(p):
        return jnp.where(is_low, pltpu.roll(p[1], 32, 1), p[0])

    def gram_tile(basis, lo, hi):
        cells = [(r, c) for r in range(lo, hi, 8) for c in range(0, width, 128)]
        chunks = [[v[r : r + 8, c : c + 128] for r, c in cells] for v in basis]
        split = [[halves(v) for v in field] for field in chunks]
        pairs = []
        for i, j in GRAM:
            terms = [two_prod(a, b, sa, sb) for a, b, sa, sb in zip(chunks[i], chunks[j], split[i], split[j])]
            pairs.append(tree(terms, pair_add))
        eight, ninth = pairs[:8], pairs[8]
        for step in (4, 2, 1):
            merged = []
            for a, b in zip(eight[:step], eight[step:]):
                parts = [folded(x, y, step) for x, y in zip(a, b)]
                merged.append(pair_add((parts[0][0], parts[1][0]), (parts[0][1], parts[1][1])))
            eight = merged
        eight, ninth = fold_lanes(eight[0]), fold_lanes(ninth)
        both = [jnp.where(lane < 64, a, b) for a, b in zip(eight, ninth)]
        return jnp.where(is_low, both[1], both[0])

    _, _, basis = krylov(sheet_f[0], sheet_f[1], sheet_i[0], (g - 1) * rs, 4)
    cross_up, cross_down = (s == 0) & (m > 0), (s == S - 1) & (m < M - 1)
    is_cross = cross_up | cross_down
    red1[s] = jnp.where(is_cross, 0.0, gram_tile(basis, rs, 2 * rs))

    @pl.when(is_middle)
    def _():
        for k, (buf, border) in enumerate(((sheet_f, border_f), (sheet_i, border_i))):
            for slot in range(4):
                arrived(None, buf.at[:, mid, :], border.at[:, slot * rs : (slot + 1) * rs, :], border_send.at[k], border_recv.at[k, slot])

    for k, (border, cross) in enumerate(((border_f, cross_f), (border_i, cross_i))):
        remote(is_middle, border.at[:, 2 * rs : 3 * rs, :], cross, pass_send.at[k, 0], pass_recv.at[k], (m, S - 1))
        remote(is_middle, border.at[:, rs : 2 * rs, :], cross, pass_send.at[k, 1], pass_recv.at[k], (m + 1, 0))

    @pl.when(is_middle)
    def _():
        _, _, fields = krylov(border_f[0], border_f[1], border_i[0], (m * S + S - 2) * rs, 4)
        tile = gram_tile(fields, rs, 3 * rs)
        red1[s] = packed(pair_add(unpacked(red1[s]), unpacked(tile)))

    for d in range(1, S):
        remote(None, red1.at[s], red1.at[s], r1_send.at[d], r1_recv.at[d], (m, lax.rem(s + d, S)))

    arrived(s > 0, layer, first_b.at[0], rad_send.at[0], rad_recv.at[0])
    arrived(s < S - 1, layer, first_b.at[2], rad_send.at[1], rad_recv.at[1])

    def conduct(temps, kinds):
        return [lookup(k, conduct_table) * (1.0 + diffusivity_derivative * t) for t, k in zip(temps, kinds)]

    def rate(kind):
        return lookup(kind, tuple(time_step / c for c in capacity_table))

    temps = [first_b[i, 0] for i in range(3)]
    kinds = [first_b[i, 1] for i in range(3)]
    (flux,) = fluxes(temps, conduct(temps, kinds), 1, 2)
    later_b[REACH, 0] = temps[1] + rate(kinds[1]) * flux
    later_b[REACH, 1] = kinds[1]
    early, pending = pending, []
    def part(slot, d):
        if d == 1:
            return later_b.at[slot, 0]
        return later_b.at[slot, :, bmid, :] if d == REACH else later_b.at[slot]

    later_b[REACH - 1, 1] = kinds[0]
    later_b[REACH + 1, 1] = kinds[2]
    for d in range(1, REACH + 1):
        remote(s < S - d, part(REACH, d), part(REACH - d, d), late_send.at[2 * d - 2], late_recv.at[2 * d - 2], (m, s + d))
        remote(s >= d, part(REACH, d), part(REACH + d, d), late_send.at[2 * d - 1], late_recv.at[2 * d - 1], (m, s - d))
    late, pending = pending, []

    def pair_of(ref, i):
        return unpacked(ref[i])

    for d in range(1, S):
        src = lax.rem(s + S - d, S)
        arrived(None, red1.at[s], red1.at[src], r1_send.at[d], r1_recv.at[d])
    total = tree([pair_of(red1, i) for i in range(S)], pair_add)
    red2[m] = packed(total)
    for d in range(1, M):
        remote(None, red2.at[m], red2.at[m], r2_send.at[d], r2_recv.at[d], (lax.rem(m + d, M), s))
    for k, (border, cross) in enumerate(((border_f, cross_f), (border_i, cross_i))):
        arrived(is_cross, border.at[:, before, :], cross, pass_send.at[k, 0], pass_recv.at[k])

    @pl.when(cross_up)
    def _():
        sheet_f[:, before, :] = cross_f[...]
        sheet_i[:, before, :] = cross_i[...]

    @pl.when(cross_down)
    def _():
        sheet_f[:, after, :] = cross_f[...]
        sheet_i[:, after, :] = cross_i[...]

    coeffs, sides, basis = krylov(sheet_f[0], sheet_f[1], sheet_i[0], (g - 1) * rs, 3)

    before_string = s == 0

    def outer(a):
        return jnp.where(before_string, pltpu.roll(a[0:rs], 3, 0), a[2 * rs :])

    cell_ext = outer(sheet_i[1]) - base_cell
    cell_ext = jnp.clip(cell_ext, 0, 2 * spokes - 1)
    upper_ext = cell_ext >= spokes
    col_ext = jnp.where(upper_ext, cell_ext - spokes, cell_ext)
    for i in range(3):
        put_onehot(rs + i, col_ext[i : i + 1, :])

    for d in range(1, M):
        src = lax.rem(m + M - d, M)
        arrived(None, red2.at[m], red2.at[src], r2_send.at[d], r2_recv.at[d])
    high, low = tree([pair_of(red2, i) for i in range(M)], pair_add)
    def added(high, low, axes):
        grid = 1024.0 * jnp.max(jnp.abs(high), axis=axes, keepdims=True)
        coarse = (high + grid) - grid
        rest = jnp.sum((high - coarse) + low, axis=axes, keepdims=True)
        return two_sum(jnp.sum(coarse, axis=axes, keepdims=True), rest)

    in_eight, in_ninth = lane < 32, (lane >= 64) & (lane < 96)
    sums = added(jnp.where(in_eight, high, 0.0), jnp.where(in_eight, low, 0.0), 1)
    gram = {ij: (sums[0][n : n + 1], sums[1][n : n + 1]) for n, ij in enumerate(GRAM[:8])}
    gram[GRAM[8]] = added(jnp.where(in_ninth, high, 0.0), jnp.where(in_ninth, low, 0.0), (0, 1))

    def twice(x):
        return 2.0 * x[0], 2.0 * x[1]

    plain = {(i, j): gram[i, j] if i == j else twice(gram[i, j]) for i, j in GRAM if j < 3}
    with_a = {
        (0, 0): gram[0, 1],
        (0, 1): pair_add(gram[0, 2], gram[1, 1]),
        (1, 1): gram[1, 2],
        (0, 2): pair_add(gram[0, 3], gram[1, 2]),
        (1, 2): pair_add(gram[1, 3], gram[2, 2]),
        (2, 2): gram[2, 3],
    }

    def upto(table, n):
        return {ij: v for ij, v in table.items() if ij[1] < n}

    one = jnp.ones_like(gram[0, 0][0])
    norm0 = gram[0, 0][0]
    a0 = norm0 / gram[0, 1][0]
    norm1 = quadratic([one, -a0], upto(plain, 2))
    b1 = norm1 / norm0
    p1 = [1.0 + b1, -a0]
    a1 = norm1 / quadratic(p1, upto(with_a, 2))
    r2 = [one, -a0 - a1 * p1[0], -a1 * p1[1]]
    norm2 = quadratic(r2, plain)
    b2 = norm2 / norm1
    p2 = [r2[0] + b2 * p1[0], r2[1] + b2 * p1[1], r2[2]]
    a2 = norm2 / quadratic(p2, with_a)
    weights = [a0 + a1 * p1[0] + a2 * p2[0], a1 * p1[1] + a2 * p2[1], a2 * p2[2]]
    potential = weights[0] * basis[0] + weights[1] * basis[1] + weights[2] * basis[2]
    pot_out[...] = potential[rs : 2 * rs]

    joule = jnp.zeros_like(potential)
    for c, side in zip(coeffs, sides):
        drop = potential - side(potential)
        joule = joule + c * (drop * drop)
    joule = heat_factor * joule
    sub_id = lax.broadcasted_iota(jnp.int32, (rs, spokes), 0)

    def binned(power, upper, first, count):
        parts = []
        for value in (jnp.where(upper, 0.0, power), jnp.where(upper, power, 0.0)):
            for _ in range(2):
                part = value.astype(jnp.bfloat16).astype(F32)
                parts.append(part)
                value = value - part
        lhs = jnp.concatenate(parts, axis=0).astype(jnp.bfloat16)
        cols = onehot[first * spokes : (first + count) * spokes, :]
        out = lax.dot_general(lhs, cols, (((1,), (1,)), ((), ())), preferred_element_type=F32)
        heats = []
        for k in range(2):
            part = out[2 * k * rs : (2 * k + 1) * rs] + out[(2 * k + 1) * rs : (2 * k + 2) * rs]
            heat = jnp.zeros((rs, spokes), F32)
            for i in range(count):
                heat = jnp.where(sub_id == i, part[:, i * spokes : (i + 1) * spokes], heat)
            heats.append(heat)
        return heats

    lower, higher = binned(joule[rs : 2 * rs], upper_own, 0, rs)
    heat_own[0] = lower
    heat_own[1] = higher
    at = pl.ds(pl.multiple_of(8 + rs * s, 8), rs)

    def slots(t):
        return pl.ds(REACH + S - 2 - t, 2)

    mine, pending = pending, []
    for n, t in enumerate(reversed(range(target0, S))):
        remote(s != t, heat_own, heat_b.at[slots(t), at, :], h_send.at[n], h_recv.at[s], (m, t))
    ext_lower, ext_higher = binned(outer(joule), upper_ext, rs, 3)
    heat_ext[0] = jnp.where(before_string, pltpu.roll(ext_lower, rs - 3, 0), ext_lower)
    heat_ext[1] = jnp.where(before_string, pltpu.roll(ext_higher, rs - 3, 0), ext_higher)
    at_rim = (s == 0) | (s == S - 1)
    side_of = jnp.where(before_string, 0, 1)
    ext_at = pl.ds(pl.multiple_of(jnp.where(before_string, 0, rows + 8), 8), 8)
    for n, t in enumerate(reversed(range(target0, S))):
        remote(at_rim & (s != t), heat_ext, heat_b.at[slots(t), ext_at, :], e_send.at[n], e_recv.at[side_of], (m, t))

    @pl.when(heated)
    def _():
        slot = REACH + S - 2 - s
        heat_b[slot, at, :] = lower
        heat_b[slot + 1, at, :] = higher

        @pl.when(at_rim)
        def _():
            heat_b[slot, ext_at, :] = heat_ext[0]
            heat_b[slot + 1, ext_at, :] = heat_ext[1]

    for d in range(1, REACH + 1):
        arrived(s >= d, part(REACH, d), part(REACH - d, d), late_send.at[2 * d - 2], late_recv.at[2 * d - 2])
        arrived(s < S - d, part(REACH, d), part(REACH + d, d), late_send.at[2 * d - 1], late_recv.at[2 * d - 1])
    count = 2 * REACH + 1
    for i in range(count):
        kind = later_b[i, 1]
        base_b[i] = lookup(kind, conduct_table)
        rate_b[i] = rate(kind)
    sent(early + late + mine)
    pair = pl.ds(0, 2)
    for j in range(S):
        at_j = pl.ds(8 + rs * j, rs)
        arrived(heated & (s != j), heat_own, heat_b.at[pair, at_j, :], h_send.at[0], h_recv.at[j])
    arrived(heated & (s != 0), heat_ext, heat_b.at[pair, top_halo, :], e_send.at[0], e_recv.at[0])
    arrived(heated & (s != S - 1), heat_ext, heat_b.at[pair, end_halo, :], e_send.at[0], e_recv.at[1])

    count = 2 * REACH + 1
    temps = [later_b[i, 0] + rate_b[i] * heat_b[i] for i in range(count)]
    for step in range(1, REACH + 1):
        first, last = step, count - step
        near = range(first - 1, last + 1)
        conds = {i: base_b[i] * (1.0 + diffusivity_derivative * temps[i]) for i in near}
        for i, f in zip(range(first, last), fluxes(temps, conds, first, last)):
            temps[i] = temps[i] + rate_b[i] * (f + heat_b[i])
    brick_out[0] = temps[REACH][8 : 8 + rows]
    sent(pending)


def hand_over(pot, brick, pot_out, brick_out):
    pot_out[...] = pot[...]
    brick_out[...] = brick[...]


def solution(mesh):
    M, S = mesh.shape["magnet"], mesh.shape["slab"]

    def local(warm, volt, pattern, cells, temp, kind):
        rs, width = warm.shape
        depth, rows, spokes = temp.shape
        brick = rows + 16
        dma = pltpu.SemaphoreType.DMA
        targets = REACH + 2
        shapes = (
            jax.ShapeDtypeStruct((rs, width), F32),
            jax.ShapeDtypeStruct((depth, rows, spokes), F32),
        )
        outs = pl.pallas_call(
            functools.partial(kernel, M, S, depth * S),
            out_shape=shapes,
            in_specs=[pl.BlockSpec(memory_space=pltpu.HBM)] * 6,
            out_specs=[pl.BlockSpec(memory_space=pltpu.VMEM)] * 2,
            scratch_shapes=[
                pltpu.VMEM((2, 3 * rs, width), F32),
                pltpu.VMEM((2, 3 * rs, width), jnp.int32),
                pltpu.VMEM((rows, spokes), jnp.int32),
                pltpu.VMEM((3, 2, brick, spokes), F32),
                pltpu.VMEM((2 * REACH + 1, 2, brick, spokes), F32),
                pltpu.VMEM(((rs + 3) * spokes, width), jnp.bfloat16),
                pltpu.VMEM((S, 8, 128), F32),
                pltpu.VMEM((M, 8, 128), F32),
                pltpu.VMEM((2, rs, spokes), F32),
                pltpu.VMEM((2, rs, spokes), F32),
                pltpu.VMEM((2 * REACH + 2, brick, spokes), F32),
                pltpu.VMEM((2 * REACH + 1, brick, spokes), F32),
                pltpu.VMEM((2 * REACH + 1, brick, spokes), F32),
                pltpu.VMEM((2, 4 * rs, width), F32),
                pltpu.VMEM((2, 4 * rs, width), jnp.int32),
                pltpu.VMEM((2, rs, width), F32),
                pltpu.VMEM((2, rs, width), jnp.int32),
                dma((2,)), dma((2, 4)),
                dma((2, 2)), dma((2,)),
                dma((6,)),
                dma((4,)), dma((4,)),
                dma((2,)), dma((2,)),
                dma((2,)), dma((2,)),
                dma((2 * REACH,)), dma((2 * REACH,)),
                dma((S,)), dma((S,)),
                dma((M,)), dma((M,)),
                dma((targets,)), dma((S,)),
                dma((targets,)), dma((2,)),
            ],
            compiler_params=pltpu.CompilerParams(
                collective_id=0, has_side_effects=True, vmem_limit_bytes=63 * 1024 * 1024
            ),
            name="window",
        )(warm, volt, pattern, cells, temp, kind)
        return pl.pallas_call(
            hand_over,
            out_shape=shapes,
            in_specs=[pl.BlockSpec(memory_space=pltpu.VMEM)] * 2,
            out_specs=[pl.BlockSpec(memory_space=pltpu.VMEM)] * 2,
            compiler_params=pltpu.CompilerParams(vmem_limit_bytes=63 * 1024 * 1024),
            name="hand_over",
        )(*outs)

    return jax.shard_map(
        local,
        mesh=mesh,
        in_specs=(
            P(("magnet", "slab"), None),
            P(("magnet", "slab"), None),
            P(("magnet", "slab"), None),
            P("magnet", None),
            P("slab", "magnet", None),
            P("slab", "magnet", None),
        ),
        out_specs=(P(("magnet", "slab"), None), P("slab", "magnet", None)),
        check_vma=False,
    )
```
